256 devices in a mesh: view: 4 (over x_hi, core), patch: 64 (over y, x_lo, z).
Axes of the slice: x: 4 (x_hi: 2, x_lo: 2; x = x_hi * 2 + x_lo), y: 4, z: 8, core: 2. Of those that a mesh axis runs over, the one named last changes fastest.
Arguments:
- queries: bfloat16 [32768, 768], P(('view', 'patch')), may hold values from -6 to 6
- key_rows: bfloat16 [32768, 768], P(('view', 'patch')), may hold values from -6 to 6
- value_rows: bfloat16 [32768, 768], P(('view', 'patch')), may hold values from -6 to 6
- step_rates: float32 [32768, 4], P(('view', 'patch')), may hold values from 0.5 to 18, as said below
- fast_init: float32 [192, 4608], replicated, may hold values from -2.598076 to 2.598076
- out_grad: bfloat16 [32768, 768], P(('view', 'patch')), may hold values from -6 to 6
Outputs:
- query_grad: bfloat16 [32768, 768], P(('view', 'patch'))
- key_grad: bfloat16 [32768, 768], P(('view', 'patch'))
- value_grad: bfloat16 [32768, 768], P(('view', 'patch'))
- rate_grad: float32 [32768, 4], P(('view', 'patch'))
- fast_grad: float32 [192, 4608], P(None, ('view', 'patch'))
The draws below stay inside these ranges and needn't reach their ends.
Inputs may be any that keep to these rules, and one draw needn't show every extreme that they name: `step_rates`: positive learning rates.
All inputs are finite; a program needn't handle non-finite values.
Results may differ from the reference program's by a relative error of at most 0.0023.
Values sent between devices are 32-bit elements; how exact they have to be, the bound alone decides.
A program may use at most 128 MiB of HBM per device.

```python
import math
import jax
import jax.numpy as jnp
from jax import lax

HEADS = 4
HEAD_DIM = 192
FF = 384
D = 768
PATCHES = 32768
N_VIEW = 4
N_PATCH = 64


def draw_step_rates(key, part):
    position_ramp = jnp.arange(PATCHES, dtype=jnp.float32)[:, None] / max(PATCHES - 1, 1)
    growth = 1.0 + 2.0 * position_ramp
    spread = jnp.exp(jax.random.uniform(key, (PATCHES, HEADS), jnp.float32, math.log(0.5), math.log(2.0)))
    return spread * growth


def draw_fast_init(key, part):
    key_one, key_two, key_three = jax.random.split(key, 3)
    columns = 3 * HEADS * FF
    row_scale = jnp.exp(jax.random.uniform(key_one, (HEAD_DIM, 1), jnp.float32, math.log(0.3), math.log(3.0)))
    col_scale = jnp.exp(jax.random.uniform(key_two, (1, columns), jnp.float32, math.log(0.3), math.log(3.0)))
    entries = jnp.clip(jax.random.normal(key_three, (HEAD_DIM, columns), jnp.float32), -4.0, 4.0)
    return entries * row_scale * col_scale / math.sqrt(HEAD_DIM)


def steps_of(key, shape, cuts, low, largest):
    def one(position, parts):
        steps = jax.random.uniform(jax.random.fold_in(jax.random.fold_in(key, 6), position), (parts,), jnp.float32, low / len(cuts), largest / len(cuts))
        return jnp.repeat(jnp.exp(steps), shape[position] // parts).reshape((-1,) + (1,) * (len(shape) - position - 1))

    level = one(*cuts[0])
    for cut in cuts[1:]:
        level = level * one(*cut)
    return level


def normal_values(own_key, shape, deviation, limit, cuts=(), kind=jnp.bfloat16):
    factor_of = steps_of(own_key, shape, cuts, -0.22, 0.18) if cuts else 1.0
    result = jax.random.normal(own_key, shape, jnp.float32) * deviation * factor_of
    return jnp.minimum(jnp.maximum(result, -limit), limit).astype(kind)


def setup_inputs(seed: int = 0) -> dict:
    splits = jax.random.split(jax.random.key(seed), 7)
    return {
        "queries": normal_values(splits[0], (PATCHES, D), 1.0, 6.0, ((0, 256),)),
        "key_rows": normal_values(splits[1], (PATCHES, D), 1.0, 6.0, ((0, 256),)),
        "value_rows": normal_values(splits[2], (PATCHES, D), 1.0, 6.0, ((0, 256),)),
        "step_rates": draw_step_rates(jax.random.fold_in(splits[6], 71), 0),
        "fast_init": draw_fast_init(jax.random.fold_in(splits[6], 71), 0),
        "out_grad": normal_values(splits[5], (PATCHES, D), 1.0, 6.0, ((0, 256),)),
    }


highest = lax.Precision.HIGHEST
product_precision = lax.Precision.HIGH
step_size = 0.2
epsilon = 1e-06

def fast_apply(inputs, weights):
    gate_act = jnp.einsum('rhd,dhc->rhc', inputs, weights[:, 0], precision=product_precision)
    up_act = jnp.einsum('rhd,dhc->rhc', inputs, weights[:, 1], precision=product_precision)
    hidden = jax.nn.silu(gate_act) * up_act
    return jnp.einsum('rhc,dhc->rhd', hidden, weights[:, 2], precision=product_precision)

def update_term(key_part, value_part, rate_part, weights):

    def objective(fast):
        return -jnp.sum(rate_part[:, :, None] * value_part * fast_apply(key_part, fast))
    return jax.grad(objective)(weights)

def forward(query_heads, key_heads, value_heads, step_rates, weights):
    blocks = N_VIEW * N_PATCH // 8
    block_rows = PATCHES // blocks
    totals = lax.optimization_barrier(jnp.sum(step_rates, 0))
    eta = step_rates * (step_size * math.sqrt(PATCHES) / totals)

    def shaped(tensor):
        return tensor.reshape((blocks, block_rows) + tensor.shape[1:])

    def accumulate(running, block_data):
        return (running + update_term(block_data[0], block_data[1], block_data[2], weights), None)
    grad_sum, _ = lax.scan(jax.checkpoint(accumulate), jnp.zeros_like(weights), (shaped(key_heads), shaped(value_heads), shaped(eta)))
    moved = weights - grad_sum
    init_norm = jnp.sqrt(lax.optimization_barrier(jnp.sum(weights * weights, 0)) + epsilon)
    renormed = moved * init_norm * lax.rsqrt(lax.optimization_barrier(jnp.sum(moved * moved, 0)) + epsilon)

    def apply_block(block_data):
        return fast_apply(block_data, renormed)
    applied = lax.map(jax.checkpoint(apply_block), shaped(query_heads))
    return applied.reshape(query_heads.shape)

def reference(queries, key_rows, value_rows, step_rates, fast_init, out_grad):

    def to_heads(tensor):
        return tensor.astype(jnp.float32).reshape(PATCHES, HEADS, HEAD_DIM)

    def from_heads(tensor):
        return tensor.reshape(PATCHES, HEADS * HEAD_DIM).astype(jnp.bfloat16)
    weights = fast_init.reshape(HEAD_DIM, 3, HEADS, FF)
    _, pull_back = jax.vjp(forward, to_heads(queries), to_heads(key_rows), to_heads(value_rows), step_rates, weights)
    query_part, key_part, value_part, rate_part, fast_part = pull_back(to_heads(out_grad))
    fast_grad = fast_part.reshape(HEAD_DIM, 3 * HEADS * FF) / math.sqrt(PATCHES)
    return (from_heads(query_part), from_heads(key_part), from_heads(value_part), rate_part, fast_grad)
```

```python
import itertools
import math

import jax
import jax.numpy as jnp
from jax import lax
from jax.experimental import pallas as pl
from jax.experimental.pallas import tpu as pltpu
from jax.sharding import PartitionSpec as P

MESH = pl.DeviceIdType.MESH
f32, bf16 = jnp.float32, jnp.bfloat16

step_size = 0.2
epsilon = 1e-06

NX, NY, NZ = 4, 4, 8
HEADS, HD, FF = 4, 192, 384
HALF = FF // 2
ROWS = 128
SLOTS = 8
ALL_ROWS = SLOTS * ROWS
CHUNK = 256
TOTAL_ROWS = ROWS * NX * NY * NZ * 2
COEFFICIENT = step_size * math.sqrt(TOTAL_ROWS)
N_SEMS = 160
GROUP = 6


def device(x, y, z, core):
    return ((x // 2) * 2 + core, (y * 2 + x % 2) * 8 + z)


PARTS = (("x", (0, 1, 2)), ("z", (3, 4)))


def part_sizes(part):
    axis, lane_tiles = part
    first, second = (NX, NZ) if axis == "x" else (NZ, NX)
    row_tiles = HALF // 8 // first
    shard = row_tiles * len(lane_tiles)
    window = -(-shard // second)
    if (shard - window) // (second - 1) >= window:
        window += 1
    return first, second, row_tiles, shard, window


def nt(a, b):
    return lax.dot_general(a, b, (((1,), (1,)), ((), ())), preferred_element_type=f32)


def nn(a, b):
    return lax.dot_general(a, b, (((1,), (0,)), ((), ())), preferred_element_type=f32)


def tn(a, b):
    return lax.dot_general(a, b, (((0,), (0,)), ((), ())), preferred_element_type=f32)


def split(value):
    high = value.astype(bf16)
    return high, (value - high.astype(f32)).astype(bf16)


def tn2(a, b):
    high, low = split(a)
    return tn(high, b) + tn(low, b)


def kernel(
    q_ref, k_ref, v_ref, r_ref, g_ref, w_hbm,
    qg_out, kg_out, vg_out, rg_out, fg_out,
    w_load, w_own, wh, wl, nh, nl, moved, gm, norms,
    kv_send, qg_send, kv, qg, rates,
    kb, vb, qb, gb, ga_s, up_s, t_s,
    s1h, s1l, s2h, s2l, s3h, s3l, s4h, s4l, s5h, s5l, s6h, s6l,
    acc, rate_rows, dq, xq, oq, rq, dkv, xkv, okv, rkv,
    p0_t, p0_r1, p0_s1, p0_r2, p0_s2, p0_a1, p0_f1, p0_g,
    p1_t, p1_r1, p1_s1, p1_r2, p1_s2, p1_a1, p1_f1, p1_g,
    f_t, f_r1, f_s1, f_r2, d_grp, f_msg,
    send_sems, recv_sems, far_sems, load_sems,
):
    view, patch = lax.axis_index("view"), lax.axis_index("patch")
    x, core = (view // 2) * 2 + (patch // 8) % 2, view % 2
    y, z = patch // 16, patch % 8
    mine = view * 64 + patch
    half_block = 2 * y + core

    def peer(axis, offset):
        if axis == "x":
            return device((x + offset) % NX, y, z, core)
        if axis == "y":
            return device(x, (y + offset) % NY, z, core)
        if axis == "z":
            return device(x, y, (z + offset) % NZ, core)
        return device(x, y, z, 1 - core)

    place = {"x": x, "z": z}
    size = {"x": NX, "z": NZ}

    far_group = [32 * (8 * m + half_block) + 8 * x + z for m in range(3)]
    far_owner = [group // 3 for group in far_group]
    near_source = []
    for t in range(3):
        group = 3 * mine + t
        block, rest = group // 32, group % 32
        near_source.append((rest // 8, (block % 8) // 2, rest % 8, block % 2))
    near_index = []
    for sx, sy, sz, sc in near_source:
        sv, sp = device(sx, sy, sz, sc)
        near_index.append(sv * 64 + sp)

    barrier = pltpu.get_barrier_semaphore()
    peers = [("x", d) for d in range(1, NX)] + [("z", d) for d in range(1, NZ)]
    peers += [("y", d) for d in range(1, NY)] + [("core", 1)]
    for axis, offset in peers:
        pl.semaphore_signal(barrier, inc=1, device_id=peer(axis, offset), device_id_type=MESH)
    for t in range(3):
        @pl.when(near_index[t] != mine)
        def _():
            pl.semaphore_signal(barrier, inc=1, device_id=device(*near_source[t]), device_id_type=MESH)

    ids = itertools.count()
    started = []

    def send(src, dst, target):
        which = next(ids)
        copy = pltpu.make_async_remote_copy(
            src_ref=src, dst_ref=dst, send_sem=send_sems.at[which], recv_sem=recv_sems.at[which],
            device_id=target, device_id_type=MESH,
        )
        copy.start()
        started.append(copy)
        return copy

    loads = []
    for m in range(3):
        first = pl.multiple_of(m * HEADS * FF + y * FF, 128)
        load = pltpu.make_async_copy(w_hbm.at[:, pl.ds(first, FF)], w_load.at[m], load_sems.at[m])
        load.start()
        loads.append(load)

    def pack(buffer, left, right):
        for h in range(HEADS):
            cols = slice(HD * h, HD * (h + 1))
            buffer[h, 0:ROWS, 0:HD] = left[:, cols].astype(f32)
            buffer[h, 0:ROWS, HD:2 * HD] = right[:, cols].astype(f32)

    pack(kv_send, k_ref, v_ref)
    for h in range(HEADS):
        kv_send[h, ROWS:ROWS + 8, :] = jnp.zeros((8, 2 * HD), f32)
        kv_send[h, ROWS:ROWS + 8, 0:ROWS] = jnp.broadcast_to(r_ref[h:h + 1, :], (8, ROWS))

    far_count = sum((owner != mine).astype(jnp.int32) for owner in far_owner)
    pl.semaphore_wait(barrier, len(peers) + far_count)

    def scatter_heads(buffer, landing):
        out = {}
        for d in (1, 3, 2):
            out[d] = send(buffer.at[(y + d) % NY], landing.at[d], peer("y", d))
        out["own"] = send(buffer.at[y], landing.at[4], peer("core", 1))
        return out

    def forward(copies, landing):
        passed = []
        for d in (1, 3, 2):
            copies[d].wait_recv()
            passed.append(send(landing.at[d], landing.at[4 + d], peer("core", 1)))
        return passed

    kv_copies = scatter_heads(kv_send, kv)
    pack(qg_send, q_ref, g_ref)
    qg_copies = scatter_heads(qg_send, qg)

    for m in range(3):
        loads[m].wait()
        both = w_load[m]
        own = jnp.where(core == 0, both[:, 0:HALF], both[:, HALF:FF]).T
        w_own[m] = own
        wh[m], wl[m] = split(own)

    def unpack_kv(s):
        kb[s * ROWS:(s + 1) * ROWS, :] = kv[s, 0:ROWS, 0:HD].astype(bf16)
        vb[s * ROWS:(s + 1) * ROWS, :] = kv[s, 0:ROWS, HD:2 * HD].astype(bf16)
        column = kv[s, ROWS:ROWS + 8, 0:ROWS].T
        rates[s * ROWS:(s + 1) * ROWS, :] = column[:, 0:1]

    def unpack_qg(s):
        qb[s * ROWS:(s + 1) * ROWS, :] = qg[s, 0:ROWS, 0:HD].astype(bf16)
        gb[s * ROWS:(s + 1) * ROWS, :] = qg[s, 0:ROWS, HD:2 * HD].astype(bf16)

    kv[0] = kv_send[y]
    qg[0] = qg_send[y]
    passed = forward(kv_copies, kv)
    for s in range(4):
        unpack_kv(s)
    kv_copies["own"].wait_recv()
    for copy in passed:
        copy.wait_recv()
    for s in range(4, 8):
        unpack_kv(s)

    rate_sum = sum(kv[s, ROWS:ROWS + 8, 0:ROWS] for s in range(SLOTS))
    total_part = jnp.sum(rate_sum[0:1, :], axis=1, keepdims=True)

    def silu_parts(gate):
        sig = 1.0 / (1.0 + jnp.exp(-gate))
        act = gate * sig
        slope = sig + act * (1.0 - sig)
        return sig, act, slope

    for m in range(3):
        acc[m] = jnp.zeros((HALF, HD), f32)

    def update_chunk(i, _):
        rows = pl.ds(pl.multiple_of(i * CHUNK, CHUNK), CHUNK)
        keys, values, eta = kb[rows, :], vb[rows, :], rates[rows, :]
        gate = nt(keys, wh[0]) + nt(keys, wl[0])
        up = nt(keys, wh[1]) + nt(keys, wl[1])
        pulled = nt(values, wh[2]) + nt(values, wl[2])
        ga_s[rows, :], up_s[rows, :], t_s[rows, :] = gate, up, pulled
        _, act, slope = silu_parts(gate)
        scaled = eta * pulled
        acc[0] -= tn2(scaled * up * slope, keys)
        acc[1] -= tn2(scaled * act, keys)
        acc[2] -= tn2(eta * act * up, values)
        return 0

    lax.fori_loop(0, ALL_ROWS // CHUNK, update_chunk, 0)

    parts = (
        (p0_t, p0_r1, p0_s1, p0_r2, p0_s2, p0_a1, p0_f1, p0_g),
        (p1_t, p1_r1, p1_s1, p1_r2, p1_s2, p1_a1, p1_f1, p1_g),
    )

    def lanes_of(first, second, third, tail):
        return (
            first[:, 0:128],
            jnp.concatenate([first[:, 128:192], second[:, 0:64]], axis=1),
            second[:, 64:192],
            third[:, 0:128],
            jnp.concatenate([third[:, 128:192], tail], axis=1),
        )

    def start_stage(r, p, source):
        axis, lane_tiles = PARTS[p]
        first, second, row_tiles, shard, window = part_sizes(PARTS[p])
        t = parts[p][0]
        for s in range(first):
            for jj, j in enumerate(lane_tiles):
                block = source[j][s * row_tiles * 8:(s + 1) * row_tiles * 8, :]
                t[r, s * shard + jj * row_tiles:s * shard + (jj + 1) * row_tiles] = block.reshape(row_tiles, 8, 128)
        copies = []
        for d in range(1, first):
            there = (place[axis] + d) % first
            copies.append(send(t.at[r, pl.ds(there * shard, shard)], parts[p][1].at[r, d - 1], peer(axis, d)))
        return copies

    def start_of(p, k):
        _, second, _, shard, window = part_sizes(PARTS[p])
        return ((shard - window) * k) // (second - 1)

    def second_stage(r, p, copies):
        axis = PARTS[p][0]
        other = "z" if axis == "x" else "x"
        first, second, row_tiles, shard, window = part_sizes(PARTS[p])
        t, r1, s1, r2 = parts[p][:4]
        total = t[r, pl.ds(place[axis] * shard, shard)]
        for d in range(1, first):
            copies[d - 1].wait_recv()
            total = total + r1[r, d - 1]
        s1[r] = total
        out = []
        for d in range(1, second):
            there = (place[other] + d) % second
            out.append(send(s1.at[r, pl.ds(start_of(p, there), window)], r2.at[r, d - 1], peer(other, d)))
        return out

    def third_stage(r, p, copies):
        other = "z" if PARTS[p][0] == "x" else "x"
        _, second, _, shard, window = part_sizes(PARTS[p])
        _, _, s1, r2, s2, a1, f1, _ = parts[p]
        total = s1[r, pl.ds(start_of(p, place[other]), window)]
        for d in range(1, second):
            copies[d - 1].wait_recv()
            total = total + r2[r, d - 1]
        s2[r] = total
        return [send(s2.at[r], a1.at[r, d - 1], peer(other, d)) for d in range(1, second)]

    def fourth_stage(r, p, copies):
        axis = PARTS[p][0]
        other = "z" if axis == "x" else "x"
        first, second, _, shard, window = part_sizes(PARTS[p])
        _, _, _, _, s2, a1, f1, g = parts[p]
        f1[r, pl.ds(start_of(p, place[other]), window)] = s2[r]
        for d in range(1, second):
            copies[d - 1].wait_recv()
            there = (place[other] + second - d) % second
            f1[r, pl.ds(start_of(p, there), window)] = a1[r, d - 1]
        here = pl.ds(place[axis] * shard, shard)
        out = [send(f1.at[r], g.at[r, here], peer(axis, d)) for d in range(1, first)]
        g[r, here] = f1[r]
        return out

    def gathered(r, copies):
        for group in copies:
            for copy in group:
                copy.wait_recv()
        tiles = {}
        for p in range(2):
            first, _, row_tiles, shard, _ = part_sizes(PARTS[p])
            for jj, j in enumerate(PARTS[p][1]):
                rows = [
                    parts[p][7][r, s * shard + jj * row_tiles:s * shard + (jj + 1) * row_tiles].reshape(row_tiles * 8, 128)
                    for s in range(first)
                ]
                tiles[j] = jnp.concatenate(rows, axis=0)
        gate = jnp.concatenate([tiles[0], tiles[1][:, 0:64]], axis=1)
        up = jnp.concatenate([tiles[1][:, 64:128], tiles[2]], axis=1)
        down = jnp.concatenate([tiles[3], tiles[4][:, 0:64]], axis=1)
        return gate, up, down, tiles[4][:, 64:128]

    def reduce_all(r, tail, between):
        source = lanes_of(acc[0], acc[1], acc[2], tail)
        copies = [start_stage(r, p, source) for p in range(2)]
        between()
        copies = [second_stage(r, p, copies[p]) for p in range(2)]
        copies = [third_stage(r, p, copies[p]) for p in range(2)]
        copies = [fourth_stage(r, p, copies[p]) for p in range(2)]
        return gathered(r, copies)

    def take_queries():
        passed = forward(qg_copies, qg)
        for s in range(4):
            unpack_qg(s)
        qg_copies["own"].wait_recv()
        for copy in passed:
            copy.wait_recv()
        for s in range(4, 8):
            unpack_qg(s)

    *terms, tail = reduce_all(0, jnp.broadcast_to(total_part, (HALF, 64)), take_queries)
    totals = tail[0:1, 0:1]
    scale = COEFFICIENT / totals
    for m in range(3):
        weight = w_own[m]
        change = terms[m] * scale
        shifted = weight - change
        init_norm = jnp.sqrt(jnp.sum(weight * weight, axis=1, keepdims=True) + epsilon)
        inverse = lax.rsqrt(jnp.sum(shifted * shifted, axis=1, keepdims=True) + epsilon)
        gm[m], moved[m] = change, shifted
        norms[m, 0], norms[m, 1] = init_norm, inverse
        nh[m], nl[m] = split(shifted * (init_norm * inverse))
        acc[m] = jnp.zeros((HALF, HD), f32)

    def apply_chunk(i, _):
        rows = pl.ds(pl.multiple_of(i * CHUNK, CHUNK), CHUNK)
        queries, grads = qb[rows, :], gb[rows, :]
        gate = nt(queries, nh[0]) + nt(queries, nl[0])
        up = nt(queries, nh[1]) + nt(queries, nl[1])
        pulled = nt(grads, nh[2]) + nt(grads, nl[2])
        _, act, slope = silu_parts(gate)
        d_gate_h, d_gate_l = split(pulled * up * slope)
        d_up_h, d_up_l = split(pulled * act)
        acc[0] += tn(d_gate_h, queries) + tn(d_gate_l, queries)
        acc[1] += tn(d_up_h, queries) + tn(d_up_l, queries)
        acc[2] += tn2(act * up, grads)
        s1h[rows, :], s1l[rows, :] = d_gate_h, d_gate_l
        s2h[rows, :], s2l[rows, :] = d_up_h, d_up_l
        return 0

    lax.fori_loop(0, ALL_ROWS // CHUNK, apply_chunk, 0)

    def product(ah, al, bh, bl, rows):
        high = ah[rows, :]
        return nn(high, bh) + nn(high, bl) + nn(al[rows, :], bh)

    def query_chunk(i, _):
        rows = pl.ds(pl.multiple_of(i * ROWS, ROWS), ROWS)
        dq[i] = product(s1h, s1l, nh[0], nl[0], rows) + product(s2h, s2l, nh[1], nl[1], rows)
        return 0

    query_copies = {}

    def send_queries():
        lax.fori_loop(0, SLOTS, query_chunk, 0)
        query_copies["pair"] = send(dq.at[pl.ds(4, 4)], xq, peer("core", 1))

    def return_rows(pair, partial, arrived, sums, landing):
        pair.wait_recv()
        out = []
        for d in (1, 3, 2, 0):
            if d == 0:
                landing[0] = partial[0] + arrived[0]
            else:
                sums[d] = partial[d] + arrived[d]
                out.append(send(sums.at[d], landing.at[d], peer("y", NY - d)))
        return out

    d_new = reduce_all(1, jnp.zeros((HALF, 64), f32), send_queries)
    query_back = return_rows(query_copies["pair"], dq, xq, oq, rq)

    head_part = jnp.zeros((1, 1), f32)
    direct = []
    for m in range(3):
        init_norm, inverse = norms[m, 0], norms[m, 1]
        weight, shifted = w_own[m], moved[m]
        dots = jnp.sum(d_new[m] * shifted, axis=1, keepdims=True)
        d_moved = d_new[m] * (init_norm * inverse) - shifted * (dots * init_norm * inverse * inverse * inverse)
        direct.append(d_moved + weight * (dots * inverse / init_norm))
        by_row = jnp.sum(d_moved * gm[m], axis=1, keepdims=True)
        head_part = head_part - jnp.sum(by_row, axis=0, keepdims=True)
        nh[m], nl[m] = split(d_moved * scale)
        acc[m] = jnp.zeros((HALF, HD), f32)
    d_totals = -head_part / totals
    direct_tiles = lanes_of(*direct, jnp.zeros((HALF, 64), f32))
    for j in range(5):
        for n in range(HALF // GROUP):
            d_grp[n, 0:GROUP, 128 * j:128 * (j + 1)] = direct_tiles[j][GROUP * n:GROUP * (n + 1), :]

    def pull_chunk(i, _):
        rows = pl.ds(pl.multiple_of(i * CHUNK, CHUNK), CHUNK)
        keys, values, eta = kb[rows, :], vb[rows, :], rates[rows, :]
        gate, up, pulled = ga_s[rows, :], up_s[rows, :], t_s[rows, :]
        one = nt(keys, nh[0]) + nt(keys, nl[0])
        two = nt(keys, nh[1]) + nt(keys, nl[1])
        three = nt(values, nh[2]) + nt(values, nl[2])
        sig, act, slope = silu_parts(gate)
        curve = sig * (1.0 - sig) * (2.0 + gate * (1.0 - 2.0 * sig))
        up_slope = up * slope
        mix = one * up_slope + two * act
        hidden = act * up
        by_rate_h, by_rate_l = split(mix * pulled + three * hidden)
        ones = jnp.ones((8, HALF), bf16)
        rate_rows[i] = nt(ones, by_rate_h) + nt(ones, by_rate_l)
        scaled = eta * pulled
        eta_three = eta * three
        c_gate_h, c_gate_l = split(scaled * (one * up * curve + two * slope) + eta_three * up_slope)
        c_up_h, c_up_l = split(scaled * one * slope + eta_three * act)
        c_pull_h, c_pull_l = split(eta * mix)
        acc[0] += tn(c_gate_h, keys) + tn(c_gate_l, keys)
        acc[1] += tn(c_up_h, keys) + tn(c_up_l, keys)
        acc[2] += tn(c_pull_h, values) + tn(c_pull_l, values)
        s1h[rows, :], s1l[rows, :] = c_gate_h, c_gate_l
        s2h[rows, :], s2l[rows, :] = c_up_h, c_up_l
        s3h[rows, :], s3l[rows, :] = c_pull_h, c_pull_l
        s4h[rows, :], s4l[rows, :] = split(scaled * up_slope)
        s5h[rows, :], s5l[rows, :] = split(scaled * act)
        s6h[rows, :], s6l[rows, :] = split(eta * hidden)
        return 0

    lax.fori_loop(0, ALL_ROWS // CHUNK, pull_chunk, 0)

    tiles = lanes_of(acc[0], acc[1], acc[2], jnp.zeros((HALF, 64), f32))
    for j in range(5):
        f_t[:, 128 * j:128 * (j + 1)] = tiles[j]
    x_rows = HALF // NX
    weight_copies = []
    for d in range(1, NX):
        first = pl.multiple_of(((x + d) % NX) * x_rows, x_rows)
        weight_copies.append(send(f_t.at[pl.ds(first, x_rows)], f_r1.at[d - 1], peer("x", d)))

    def key_chunk(i, _):
        rows = pl.ds(pl.multiple_of(i * ROWS, ROWS), ROWS)
        key_part = product(s1h, s1l, wh[0], wl[0], rows) + product(s2h, s2l, wh[1], wl[1], rows)
        key_part += product(s4h, s4l, nh[0], nl[0], rows) + product(s5h, s5l, nh[1], nl[1], rows)
        value_part = product(s3h, s3l, wh[2], wl[2], rows) + product(s6h, s6l, nh[2], nl[2], rows)
        dkv[i, 0:ROWS, 0:HD] = key_part
        dkv[i, 0:ROWS, HD:2 * HD] = value_part
        return 0

    lax.fori_loop(0, SLOTS, key_chunk, 0)
    for s in range(SLOTS):
        dkv[s, ROWS:ROWS + 8, :] = jnp.zeros((8, 2 * HD), f32)
        lane = (s % 2) * ROWS
        dkv[s, ROWS:ROWS + 8, 0:ROWS] = rate_rows[s // 2, :, lane:lane + ROWS] + d_totals
    pair = send(dkv.at[pl.ds(4, 4)], xkv, peer("core", 1))

    total = f_t[pl.ds(pl.multiple_of(x * x_rows, x_rows), x_rows), :]
    for d in range(1, NX):
        weight_copies[d - 1].wait_recv()
        total = total + f_r1[d - 1]
    for n in range(NZ):
        f_s1[n, 0:GROUP, :] = total[GROUP * n:GROUP * (n + 1), :]
        f_s1[n, GROUP:8, :] = jnp.zeros((8 - GROUP, 640), f32)
    weight_copies = [send(f_s1.at[(z + d) % NZ], f_r2.at[d - 1], peer("z", d)) for d in range(1, NZ)]
    row_back = return_rows(pair, dkv, xkv, okv, rkv)

    total = f_s1[z]
    for d in range(1, NZ):
        weight_copies[d - 1].wait_recv()
        total = total + f_r2[d - 1]
    total = (total + d_grp[8 * x + z]) * (1.0 / math.sqrt(TOTAL_ROWS))
    f_msg[0, :, 0:HD] = total[:, 0:HD]
    f_msg[1, :, 0:HD] = total[:, HD:2 * HD]
    f_msg[2, :, 0:HD] = total[:, 2 * HD:3 * HD]
    far_copies = []
    for m in range(3):
        slot = far_group[m] % 3
        owner = far_owner[m]
        copy = pltpu.make_async_remote_copy(
            src_ref=f_msg.at[m], dst_ref=fg_out.at[slot], send_sem=far_sems.at[0, m], recv_sem=far_sems.at[1, slot],
            device_id=(owner // 64, owner % 64), device_id_type=MESH,
        )

        @pl.when(owner != mine)
        def _():
            copy.start()

        @pl.when(owner == mine)
        def _():
            fg_out[slot] = f_msg[m]

        far_copies.append(copy)

    def rows_out(out_ref, landing, lanes):
        for h in range(HEADS):
            d = (h + NY - y) % NY
            out_ref[:, HD * h:HD * (h + 1)] = landing[d, 0:ROWS, lanes:lanes + HD].astype(bf16)

    for copy in query_back:
        copy.wait_recv()
    rows_out(qg_out, rq, 0)
    for copy in row_back:
        copy.wait_recv()
    rows_out(kg_out, rkv, 0)
    rows_out(vg_out, rkv, HD)
    for h in range(HEADS):
        rg_out[h] = rkv[(h + NY - y) % NY, ROWS:ROWS + 8, 0:ROWS]

    for m in range(3):
        @pl.when(near_index[m] != mine)
        def _():
            pltpu.make_async_remote_copy(
                src_ref=f_msg.at[m], dst_ref=fg_out.at[m], send_sem=far_sems.at[0, m], recv_sem=far_sems.at[1, m],
                device_id=(view, patch), device_id_type=MESH,
            ).wait_recv()

        @pl.when(far_owner[m] != mine)
        def _():
            far_copies[m].wait_send()
    for copy in started:
        copy.wait_send()


def scratch():
    tile = (8, 128)
    shapes = [
        pltpu.VMEM((3, HD, FF), f32),
        pltpu.VMEM((3, HALF, HD), f32),
        *[pltpu.VMEM((3, HALF, HD), bf16)] * 4,
        *[pltpu.VMEM((3, HALF, HD), f32)] * 2,
        pltpu.VMEM((3, 2, HALF, 1), f32),
        *[pltpu.VMEM((HEADS, ROWS + 8, 2 * HD), f32)] * 2,
        *[pltpu.VMEM((SLOTS, ROWS + 8, 2 * HD), f32)] * 2,
        pltpu.VMEM((ALL_ROWS, 1), f32),
        *[pltpu.VMEM((ALL_ROWS, HD), bf16)] * 4,
        *[pltpu.VMEM((ALL_ROWS, HALF), f32)] * 3,
        *[pltpu.VMEM((ALL_ROWS, HALF), bf16)] * 12,
        pltpu.VMEM((3, HALF, HD), f32),
        pltpu.VMEM((ALL_ROWS // CHUNK, 8, CHUNK), f32),
        pltpu.VMEM((SLOTS, ROWS, HD), f32),
        *[pltpu.VMEM((4, ROWS, HD), f32)] * 3,
        pltpu.VMEM((SLOTS, ROWS + 8, 2 * HD), f32),
        *[pltpu.VMEM((4, ROWS + 8, 2 * HD), f32)] * 3,
    ]
    for part in PARTS:
        first, second, _, shard, window = part_sizes(part)
        shapes += [
            pltpu.VMEM((2, first * shard) + tile, f32),
            pltpu.VMEM((2, first - 1, shard) + tile, f32),
            pltpu.VMEM((2, shard) + tile, f32),
            pltpu.VMEM((2, second - 1, window) + tile, f32),
            pltpu.VMEM((2, window) + tile, f32),
            pltpu.VMEM((2, second - 1, window) + tile, f32),
            pltpu.VMEM((2, shard) + tile, f32),
            pltpu.VMEM((2, first * shard) + tile, f32),
        ]
    shapes += [
        pltpu.VMEM((HALF, 640), f32),
        pltpu.VMEM((NX - 1, HALF // NX, 640), f32),
        pltpu.VMEM((NZ, 8, 640), f32),
        pltpu.VMEM((NZ - 1, 8, 640), f32),
        pltpu.VMEM((HALF // GROUP, 8, 640), f32),
        pltpu.VMEM((3, 8, 256), f32),
        pltpu.SemaphoreType.DMA((N_SEMS,)),
        pltpu.SemaphoreType.DMA((N_SEMS,)),
        pltpu.SemaphoreType.DMA((2, 3)),
        pltpu.SemaphoreType.DMA((3,)),
    ]
    return shapes


def on_device(queries, key_rows, value_rows, step_rates, fast_init, out_grad):
    vmem = pl.BlockSpec(memory_space=pltpu.VMEM)
    rows = jax.ShapeDtypeStruct((ROWS, HEADS * HD), bf16)
    query_grad, key_grad, value_grad, rate_tiles, groups = pl.pallas_call(
        kernel,
        out_shape=(
            rows, rows, rows,
            jax.ShapeDtypeStruct((HEADS, 8, ROWS), f32),
            jax.ShapeDtypeStruct((3, 8, 256), f32),
        ),
        in_specs=[vmem] * 5 + [pl.BlockSpec(memory_space=pl.ANY)],
        out_specs=(vmem,) * 5,
        scratch_shapes=scratch(),
        compiler_params=pltpu.CompilerParams(
            collective_id=0, has_side_effects=True, vmem_limit_bytes=56 * 2**20
        ),
        name="layer_grad",
    )(queries, key_rows, value_rows, step_rates.T, out_grad, fast_init)
    rate_grad = rate_tiles[:, 0, :].T
    fast_grad = groups[:, :GROUP, :HD].reshape(3 * GROUP, HD).T
    return query_grad, key_grad, value_grad, rate_grad, fast_grad


def solution(mesh):
    both = ("view", "patch")
    return jax.shard_map(
        on_device,
        mesh=mesh,
        in_specs=(P(both, None), P(both, None), P(both, None), P(both, None), P(), P(both, None)),
        out_specs=(P(both, None), P(both, None), P(both, None), P(both, None), P(None, both)),
        check_vma=False,
    )
```

```python
import itertools
import math

import jax
import jax.numpy as jnp
from jax import lax
from jax.experimental import pallas as pl
from jax.experimental.pallas import tpu as pltpu
from jax.sharding import PartitionSpec as P

MESH = pl.DeviceIdType.MESH
f32, bf16 = jnp.float32, jnp.bfloat16

step_size = 0.2
epsilon = 1e-06

NX, NY, NZ = 4, 4, 8
HEADS, HD, FF = 4, 192, 384
HALF = FF // 2
ROWS = 128
SLOTS = 8
ALL_ROWS = SLOTS * ROWS
CHUNK = 256
TOTAL_ROWS = ROWS * NX * NY * NZ * 2
COEFFICIENT = step_size * math.sqrt(TOTAL_ROWS)
N_SEMS = 160
GROUP = 6


def device(x, y, z, core):
    return ((x // 2) * 2 + core, (y * 2 + x % 2) * 8 + z)


PARTS = (("x", (0, 1, 2)), ("z", (3, 4)))


def part_sizes(part):
    axis, lane_tiles = part
    first, second = (NX, NZ) if axis == "x" else (NZ, NX)
    row_tiles = HALF // 8 // first
    shard = row_tiles * len(lane_tiles)
    window = -(-shard // second)
    if (shard - window) // (second - 1) >= window:
        window += 1
    return first, second, row_tiles, shard, window


def nt(a, b):
    return lax.dot_general(a, b, (((1,), (1,)), ((), ())), preferred_element_type=f32)


def nn(a, b):
    return lax.dot_general(a, b, (((1,), (0,)), ((), ())), preferred_element_type=f32)


def tn(a, b):
    return lax.dot_general(a, b, (((0,), (0,)), ((), ())), preferred_element_type=f32)


def split(value):
    high = value.astype(bf16)
    return high, (value - high.astype(f32)).astype(bf16)


def tn2(a, b):
    high, low = split(a)
    return tn(high, b) + tn(low, b)


def kernel(
    q_ref, k_ref, v_ref, r_ref, g_ref, w_hbm,
    rows_ref, rg_out, fg_out,
    w_load, w_own, wh, wl, nh, nl, moved, gm, norms,
    kv_send, qg_send, kv, qg, rates,
    inv_rates, kb, vb, qb, gb, ga_s, up_s, t_s, m1, m2, m3, m4,
    s1h, s1l, s2h, s2l, s3h, s3l, s4h, s4l, s5h, s5l, s6h, s6l,
    acc, rate_rows, dq, xq, oq, rq, dkv, xkv, okv, rkv,
    p0_t, p0_r1, p0_s1, p0_r2, p0_s2, p0_a1, p0_f1, p0_g,
    p1_t, p1_r1, p1_s1, p1_r2, p1_s2, p1_a1, p1_f1, p1_g,
    f_t, f_r1, f_s1, f_r2, d_grp, f_msg,
    send_sems, recv_sems, far_sems, load_sems,
):
    view, patch = lax.axis_index("view"), lax.axis_index("patch")
    x, core = (view // 2) * 2 + (patch // 8) % 2, view % 2
    y, z = patch // 16, patch % 8
    mine = view * 64 + patch
    half_block = 2 * y + core

    def peer(axis, offset):
        if axis == "x":
            return device((x + offset) % NX, y, z, core)
        if axis == "y":
            return device(x, (y + offset) % NY, z, core)
        if axis == "z":
            return device(x, y, (z + offset) % NZ, core)
        return device(x, y, z, 1 - core)

    place = {"x": x, "z": z}
    size = {"x": NX, "z": NZ}

    far_group = [32 * (8 * m + half_block) + 8 * x + z for m in range(3)]
    far_owner = [group // 3 for group in far_group]
    near_source = []
    for t in range(3):
        group = 3 * mine + t
        block, rest = group // 32, group % 32
        near_source.append((rest // 8, (block % 8) // 2, rest % 8, block % 2))
    near_index = []
    for sx, sy, sz, sc in near_source:
        sv, sp = device(sx, sy, sz, sc)
        near_index.append(sv * 64 + sp)

    barrier = pltpu.get_barrier_semaphore()
    peers = [("x", d) for d in range(1, NX)] + [("z", d) for d in range(1, NZ)]
    peers += [("y", d) for d in range(1, NY)] + [("core", 1)]
    for axis, offset in peers:
        pl.semaphore_signal(barrier, inc=1, device_id=peer(axis, offset), device_id_type=MESH)
    for t in range(3):
        @pl.when(near_index[t] != mine)
        def _():
            pl.semaphore_signal(barrier, inc=1, device_id=device(*near_source[t]), device_id_type=MESH)

    ids = itertools.count()
    started = []

    def send(src, dst, target):
        which = next(ids)
        copy = pltpu.make_async_remote_copy(
            src_ref=src, dst_ref=dst, send_sem=send_sems.at[which], recv_sem=recv_sems.at[which],
            device_id=target, device_id_type=MESH,
        )
        copy.start()
        started.append(copy)
        return copy

    loads = []
    for m in range(3):
        first = pl.multiple_of(m * HEADS * FF + y * FF, 128)
        load = pltpu.make_async_copy(w_hbm.at[:, pl.ds(first, FF)], w_load.at[m], load_sems.at[m])
        load.start()
        loads.append(load)

    def pack(buffer, left, right):
        for h in range(HEADS):
            cols = slice(HD * h, HD * (h + 1))
            buffer[h, 0:ROWS, 0:HD] = left[:, cols].astype(f32)
            buffer[h, 0:ROWS, HD:2 * HD] = right[:, cols].astype(f32)

    pack(kv_send, k_ref, v_ref)
    for h in range(HEADS):
        kv_send[h, ROWS:ROWS + 8, :] = jnp.zeros((8, 2 * HD), f32)
        kv_send[h, ROWS:ROWS + 8, 0:ROWS] = jnp.broadcast_to(r_ref[h:h + 1, :], (8, ROWS))

    far_count = sum((owner != mine).astype(jnp.int32) for owner in far_owner)
    pl.semaphore_wait(barrier, len(peers) + far_count)

    def scatter_heads(buffer, landing):
        out = {}
        for d in (1, 3, 2):
            out[d] = send(buffer.at[(y + d) % NY], landing.at[d], peer("y", d))
        out["own"] = send(buffer.at[y], landing.at[4], peer("core", 1))
        return out

    kv_copies = scatter_heads(kv_send, kv)
    pack(qg_send, q_ref, g_ref)

    for m in range(3):
        loads[m].wait()
        both = w_load[m]
        own = jnp.where(core == 0, both[:, 0:HALF], both[:, HALF:FF]).T
        w_own[m] = own
        wh[m], wl[m] = split(own)

    def row_block(s):
        first = (s % 4) * CHUNK + (s // 4) * ROWS
        return slice(first, first + ROWS)

    def unpack_kv(s):
        kb[row_block(s), :] = kv[s, 0:ROWS, 0:HD].astype(bf16)
        vb[row_block(s), :] = kv[s, 0:ROWS, HD:2 * HD].astype(bf16)
        column = kv[s, ROWS:ROWS + 8, 0:ROWS].T[:, 0:1]
        rates[row_block(s), :] = column
        inv_rates[row_block(s), :] = 1.0 / column

    def unpack_qg(s):
        qb[row_block(s), :] = qg[s, 0:ROWS, 0:HD].astype(bf16)
        gb[row_block(s), :] = qg[s, 0:ROWS, HD:2 * HD].astype(bf16)

    def silu_parts(gate):
        sig = 1.0 / (1.0 + jnp.exp(-gate))
        act = gate * sig
        slope = sig + act * (1.0 - sig)
        return sig, act, slope

    for m in range(3):
        acc[m] = jnp.zeros((HALF, HD), f32)

    def update_chunk(i):
        rows = slice(i * CHUNK, (i + 1) * CHUNK)
        keys, values, eta = kb[rows, :], vb[rows, :], rates[rows, :]
        gate = nt(keys, wh[0]) + nt(keys, wl[0])
        up = nt(keys, wh[1]) + nt(keys, wl[1])
        pulled = nt(values, wh[2]) + nt(values, wl[2])
        ga_s[rows, :], up_s[rows, :], t_s[rows, :] = gate, up, pulled
        _, act, slope = silu_parts(gate)
        scaled = eta * pulled
        acc[0] -= tn2(scaled * up * slope, keys)
        acc[1] -= tn2(scaled * act, keys)
        acc[2] -= tn2(eta * act * up, values)

    def take_pair(d):
        unpack_kv(d)
        unpack_kv(4 + d)
        update_chunk(d)

    def pass_on(copies, landing, d):
        copies[d].wait_recv()
        return send(landing.at[d], landing.at[4 + d], peer("core", 1))

    with jax.named_scope("keys_own"):
        kv[0] = kv_send[y]
        kv_copies["own"].wait_recv()
        take_pair(0)
    passed = {}
    with jax.named_scope("keys_first"):
        passed[1] = pass_on(kv_copies, kv, 1)
        passed[3] = pass_on(kv_copies, kv, 3)
        passed[1].wait_recv()
        take_pair(1)
    with jax.named_scope("keys_second"):
        passed[2] = pass_on(kv_copies, kv, 2)
        qg_copies = scatter_heads(qg_send, qg)
        passed[3].wait_recv()
        take_pair(3)
    with jax.named_scope("keys_third"):
        passed[2].wait_recv()
        take_pair(2)

    rate_sum = sum(kv[s, ROWS:ROWS + 8, 0:ROWS] for s in range(SLOTS))
    total_part = jnp.sum(rate_sum[0:1, :], axis=1, keepdims=True)

    parts = (
        (p0_t, p0_r1, p0_s1, p0_r2, p0_s2, p0_a1, p0_f1, p0_g),
        (p1_t, p1_r1, p1_s1, p1_r2, p1_s2, p1_a1, p1_f1, p1_g),
    )

    def lanes_of(first, second, third, tail):
        return (
            first[:, 0:128],
            jnp.concatenate([first[:, 128:192], second[:, 0:64]], axis=1),
            second[:, 64:192],
            third[:, 0:128],
            jnp.concatenate([third[:, 128:192], tail], axis=1),
        )

    def start_stage(r, p, source):
        axis, lane_tiles = PARTS[p]
        first, second, row_tiles, shard, window = part_sizes(PARTS[p])
        t = parts[p][0]
        for s in range(first):
            for jj, j in enumerate(lane_tiles):
                block = source[j][s * row_tiles * 8:(s + 1) * row_tiles * 8, :]
                t[r, s * shard + jj * row_tiles:s * shard + (jj + 1) * row_tiles] = block.reshape(row_tiles, 8, 128)
        copies = []
        for d in range(1, first):
            there = (place[axis] + d) % first
            copies.append(send(t.at[r, pl.ds(there * shard, shard)], parts[p][1].at[r, d - 1], peer(axis, d)))
        return copies

    def start_of(p, k):
        _, second, _, shard, window = part_sizes(PARTS[p])
        return ((shard - window) * k) // (second - 1)

    def second_stage(r, p, copies):
        axis = PARTS[p][0]
        other = "z" if axis == "x" else "x"
        first, second, row_tiles, shard, window = part_sizes(PARTS[p])
        t, r1, s1, r2 = parts[p][:4]
        total = t[r, pl.ds(place[axis] * shard, shard)]
        for d in range(1, first):
            copies[d - 1].wait_recv()
            total = total + r1[r, d - 1]
        s1[r] = total
        out = []
        for d in range(1, second):
            there = (place[other] + d) % second
            out.append(send(s1.at[r, pl.ds(start_of(p, there), window)], r2.at[r, d - 1], peer(other, d)))
        return out

    def third_stage(r, p, copies):
        other = "z" if PARTS[p][0] == "x" else "x"
        _, second, _, shard, window = part_sizes(PARTS[p])
        _, _, s1, r2, s2, a1, f1, _ = parts[p]
        total = s1[r, pl.ds(start_of(p, place[other]), window)]
        for d in range(1, second):
            copies[d - 1].wait_recv()
            total = total + r2[r, d - 1]
        s2[r] = total
        return [send(s2.at[r], a1.at[r, d - 1], peer(other, d)) for d in range(1, second)]

    def fourth_stage(r, p, copies):
        axis = PARTS[p][0]
        other = "z" if axis == "x" else "x"
        first, second, _, shard, window = part_sizes(PARTS[p])
        _, _, _, _, s2, a1, f1, g = parts[p]
        f1[r, pl.ds(start_of(p, place[other]), window)] = s2[r]
        for d in range(1, second):
            copies[d - 1].wait_recv()
            there = (place[other] + second - d) % second
            f1[r, pl.ds(start_of(p, there), window)] = a1[r, d - 1]
        here = pl.ds(place[axis] * shard, shard)
        out = [send(f1.at[r], g.at[r, here], peer(axis, d)) for d in range(1, first)]
        g[r, here] = f1[r]
        return out

    def gathered(r, copies):
        for group in copies:
            for copy in group:
                copy.wait_recv()
        tiles = {}
        for p in range(2):
            first, _, row_tiles, shard, _ = part_sizes(PARTS[p])
            for jj, j in enumerate(PARTS[p][1]):
                rows = [
                    parts[p][7][r, s * shard + jj * row_tiles:s * shard + (jj + 1) * row_tiles].reshape(row_tiles * 8, 128)
                    for s in range(first)
                ]
                tiles[j] = jnp.concatenate(rows, axis=0)
        gate = jnp.concatenate([tiles[0], tiles[1][:, 0:64]], axis=1)
        up = jnp.concatenate([tiles[1][:, 64:128], tiles[2]], axis=1)
        down = jnp.concatenate([tiles[3], tiles[4][:, 0:64]], axis=1)
        return gate, up, down, tiles[4][:, 64:128]

    def reduce_all(r, tail, hooks):
        with jax.named_scope("first_sends"):
            source = lanes_of(acc[0], acc[1], acc[2], tail)
            copies = [start_stage(r, p, source) for p in (1, 0)][::-1]
        with jax.named_scope("first_hook"):
            hooks[0]()
        with jax.named_scope("second_sends"):
            copies = [second_stage(r, p, copies[p]) for p in range(2)]
        with jax.named_scope("second_hook"):
            hooks[1]()
        with jax.named_scope("third_sends"):
            copies = [third_stage(r, p, copies[p]) for p in range(2)]
        with jax.named_scope("third_hook"):
            hooks[2]()
        with jax.named_scope("fourth_sends"):
            copies = [fourth_stage(r, p, copies[p]) for p in range(2)]
        with jax.named_scope("gathered"):
            return gathered(r, copies)

    def prepare_chunk(i, _):
        rows = pl.ds(pl.multiple_of(i * CHUNK, CHUNK), CHUNK)
        eta, gate, up, pulled = rates[rows, :], ga_s[rows, :], up_s[rows, :], t_s[rows, :]
        sig, act, slope = silu_parts(gate)
        curve = sig * (1.0 - sig) * (2.0 + gate * (1.0 - 2.0 * sig))
        scaled = eta * pulled
        by_slope, by_act = eta * (up * slope), eta * act
        m1[rows, :], m2[rows, :] = scaled * up * curve, scaled * slope
        m3[rows, :], m4[rows, :] = by_slope, by_act
        s4h[rows, :], s4l[rows, :] = split(by_slope * pulled)
        s5h[rows, :], s5l[rows, :] = split(by_act * pulled)
        s6h[rows, :], s6l[rows, :] = split(by_act * up)
        return 0

    query_passed = {}

    def prepare():
        lax.fori_loop(0, ALL_ROWS // CHUNK, prepare_chunk, 0)

    def pass_queries():
        qg[0] = qg_send[y]
        for d in (1, 3, 2):
            query_passed[d] = pass_on(qg_copies, qg, d)

    def take_queries():
        qg_copies["own"].wait_recv()
        for d in (1, 3, 2):
            query_passed[d].wait_recv()
        for s in range(SLOTS):
            unpack_qg(s)

    *terms, tail = reduce_all(0, jnp.broadcast_to(total_part, (HALF, 64)), (prepare, pass_queries, take_queries))
    totals = tail[0:1, 0:1]
    scale = COEFFICIENT / totals
    new_scope = jax.named_scope("new_weights")
    new_scope.__enter__()
    for m in range(3):
        weight = w_own[m]
        change = terms[m] * scale
        shifted = weight - change
        init_norm = jnp.sqrt(jnp.sum(weight * weight, axis=1, keepdims=True) + epsilon)
        inverse = lax.rsqrt(jnp.sum(shifted * shifted, axis=1, keepdims=True) + epsilon)
        gm[m], moved[m] = change, shifted
        norms[m, 0], norms[m, 1] = init_norm, inverse
        nh[m], nl[m] = split(shifted * (init_norm * inverse))
        acc[m] = jnp.zeros((HALF, HD), f32)

    new_scope.__exit__(None, None, None)

    def apply_chunk(i, _):
        rows = pl.ds(pl.multiple_of(i * CHUNK, CHUNK), CHUNK)
        queries, grads = qb[rows, :], gb[rows, :]
        gate = nt(queries, nh[0]) + nt(queries, nl[0])
        up = nt(queries, nh[1]) + nt(queries, nl[1])
        pulled = nt(grads, nh[2]) + nt(grads, nl[2])
        _, act, slope = silu_parts(gate)
        d_gate_h, d_gate_l = split(pulled * up * slope)
        d_up_h, d_up_l = split(pulled * act)
        acc[0] += tn(d_gate_h, queries) + tn(d_gate_l, queries)
        acc[1] += tn(d_up_h, queries) + tn(d_up_l, queries)
        acc[2] += tn2(act * up, grads)
        s1h[rows, :], s1l[rows, :] = d_gate_h, d_gate_l
        s2h[rows, :], s2l[rows, :] = d_up_h, d_up_l
        return 0

    with jax.named_scope("apply"):
        lax.fori_loop(0, ALL_ROWS // CHUNK, apply_chunk, 0)

    def product(ah, al, bh, bl, rows):
        high = ah[rows, :]
        return nn(high, bh) + nn(high, bl) + nn(al[rows, :], bh)

    def query_chunk(i, _):
        rows = pl.ds(pl.multiple_of(i * ROWS, ROWS), ROWS)
        slot = (i % 2) * 4 + i // 2
        dq[slot] = product(s1h, s1l, nh[0], nl[0], rows) + product(s2h, s2l, nh[1], nl[1], rows)
        return 0

    query_copies = {}

    def send_queries():
        lax.fori_loop(0, SLOTS, query_chunk, 0)
        query_copies["pair"] = send(dq.at[pl.ds(4, 4)], xq, peer("core", 1))

    def return_rows(pair, partial, arrived, sums, landing):
        pair.wait_recv()
        out = []
        for d in (1, 3, 2, 0):
            if d == 0:
                landing[0] = partial[0] + arrived[0]
            else:
                sums[d] = partial[d] + arrived[d]
                out.append(send(sums.at[d], landing.at[d], peer("y", NY - d)))
        return out

    def return_queries():
        query_copies["back"] = return_rows(query_copies["pair"], dq, xq, oq, rq)

    d_new = reduce_all(1, jnp.zeros((HALF, 64), f32), (send_queries, return_queries, lambda: None))
    query_back = query_copies["back"]

    pre_scope = jax.named_scope("pull_weights")
    pre_scope.__enter__()
    head_part = jnp.zeros((1, 1), f32)
    direct = []
    for m in range(3):
        init_norm, inverse = norms[m, 0], norms[m, 1]
        weight, shifted = w_own[m], moved[m]
        dots = jnp.sum(d_new[m] * shifted, axis=1, keepdims=True)
        d_moved = d_new[m] * (init_norm * inverse) - shifted * (dots * init_norm * inverse * inverse * inverse)
        direct.append(d_moved + weight * (dots * inverse / init_norm))
        by_row = jnp.sum(d_moved * gm[m], axis=1, keepdims=True)
        head_part = head_part - jnp.sum(by_row, axis=0, keepdims=True)
        nh[m], nl[m] = split(d_moved * scale)
        acc[m] = jnp.zeros((HALF, HD), f32)
    d_totals = -head_part / totals
    pre_scope.__exit__(None, None, None)

    def pull_chunk(i, _):
        rows = pl.ds(pl.multiple_of(i * CHUNK, CHUNK), CHUNK)
        keys, values = kb[rows, :], vb[rows, :]
        one = nt(keys, nh[0]) + nt(keys, nl[0])
        two = nt(keys, nh[1]) + nt(keys, nl[1])
        three = nt(values, nh[2]) + nt(values, nl[2])
        by_slope, by_act, by_two = m3[rows, :], m4[rows, :], m2[rows, :]
        c_pull = one * by_slope + two * by_act
        c_gate_h, c_gate_l = split(one * m1[rows, :] + two * by_two + three * by_slope)
        c_up_h, c_up_l = split(one * by_two + three * by_act)
        c_pull_h, c_pull_l = split(c_pull)
        acc[0] += tn(c_gate_h, keys) + tn(c_gate_l, keys)
        acc[1] += tn(c_up_h, keys) + tn(c_up_l, keys)
        acc[2] += tn(c_pull_h, values) + tn(c_pull_l, values)
        by_rate = c_pull * t_s[rows, :] + three * (by_act * up_s[rows, :])
        by_rate_h, by_rate_l = split(by_rate * inv_rates[rows, :])
        ones = jnp.ones((8, HALF), bf16)
        rate_rows[i] = nt(ones, by_rate_h) + nt(ones, by_rate_l)
        s1h[rows, :], s1l[rows, :] = c_gate_h, c_gate_l
        s2h[rows, :], s2l[rows, :] = c_up_h, c_up_l
        s3h[rows, :], s3l[rows, :] = c_pull_h, c_pull_l
        return 0

    with jax.named_scope("pull"):
        lax.fori_loop(0, ALL_ROWS // CHUNK, pull_chunk, 0)

    tiles = lanes_of(acc[0], acc[1], acc[2], jnp.zeros((HALF, 64), f32))
    for j in range(5):
        f_t[:, 128 * j:128 * (j + 1)] = tiles[j]
    x_rows = HALF // NX
    weight_copies = []
    for d in range(1, NX):
        first = pl.multiple_of(((x + d) % NX) * x_rows, x_rows)
        weight_copies.append(send(f_t.at[pl.ds(first, x_rows)], f_r1.at[d - 1], peer("x", d)))

    def key_chunk(i, _):
        rows = pl.ds(pl.multiple_of(i * ROWS, ROWS), ROWS)
        slot = (i % 2) * 4 + i // 2
        key_part = product(s1h, s1l, wh[0], wl[0], rows) + product(s2h, s2l, wh[1], wl[1], rows)
        key_part += product(s4h, s4l, nh[0], nl[0], rows) + product(s5h, s5l, nh[1], nl[1], rows)
        value_part = product(s3h, s3l, wh[2], wl[2], rows) + product(s6h, s6l, nh[2], nl[2], rows)
        dkv[slot, 0:ROWS, 0:HD] = key_part
        dkv[slot, 0:ROWS, HD:2 * HD] = value_part
        return 0

    with jax.named_scope("row_grads"):
        lax.fori_loop(0, SLOTS, key_chunk, 0)
        for s in range(SLOTS):
            dkv[s, ROWS:ROWS + 8, :] = jnp.zeros((8, 2 * HD), f32)
            lane = (s // 4) * ROWS
            dkv[s, ROWS:ROWS + 8, 0:ROWS] = rate_rows[s % 4, :, lane:lane + ROWS] + d_totals
        pair = send(dkv.at[pl.ds(4, 4)], xkv, peer("core", 1))

    with jax.named_scope("x_sums"):
        total = f_t[pl.ds(pl.multiple_of(x * x_rows, x_rows), x_rows), :]
        for d in range(1, NX):
            weight_copies[d - 1].wait_recv()
            total = total + f_r1[d - 1]
        for n in range(NZ):
            f_s1[n, 0:GROUP, :] = total[GROUP * n:GROUP * (n + 1), :]
            f_s1[n, GROUP:8, :] = jnp.zeros((8 - GROUP, 640), f32)
        weight_copies = [send(f_s1.at[(z + d) % NZ], f_r2.at[d - 1], peer("z", d)) for d in range(1, NZ)]
    with jax.named_scope("row_returns"):
        row_back = return_rows(pair, dkv, xkv, okv, rkv)
    with jax.named_scope("direct"):
        direct_tiles = lanes_of(*direct, jnp.zeros((HALF, 64), f32))
        for j in range(5):
            for n in range(HALF // GROUP):
                d_grp[n, 0:GROUP, 128 * j:128 * (j + 1)] = direct_tiles[j][GROUP * n:GROUP * (n + 1), :]

    z_scope = jax.named_scope("z_sums")
    z_scope.__enter__()
    total = f_s1[z]
    for d in range(1, NZ):
        weight_copies[d - 1].wait_recv()
        total = total + f_r2[d - 1]
    total = (total + d_grp[8 * x + z]) * (1.0 / math.sqrt(TOTAL_ROWS))
    f_msg[0, :, 0:HD] = total[:, 0:HD]
    f_msg[1, :, 0:HD] = total[:, HD:2 * HD]
    f_msg[2, :, 0:HD] = total[:, 2 * HD:3 * HD]
    far_copies = []
    for m in range(3):
        slot = far_group[m] % 3
        owner = far_owner[m]
        copy = pltpu.make_async_remote_copy(
            src_ref=f_msg.at[m], dst_ref=fg_out.at[slot], send_sem=far_sems.at[0, m], recv_sem=far_sems.at[1, slot],
            device_id=(owner // 64, owner % 64), device_id_type=MESH,
        )

        @pl.when(owner != mine)
        def _():
            copy.start()

        @pl.when(owner == mine)
        def _():
            fg_out[slot] = f_msg[m]

        far_copies.append(copy)

    z_scope.__exit__(None, None, None)

    def rows_out(which, landing, lanes):
        for h in range(HEADS):
            d = (h + NY - y) % NY
            rows_ref[which, :, HD * h:HD * (h + 1)] = landing[d, 0:ROWS, lanes:lanes + HD].astype(bf16)

    with jax.named_scope("query_rows"):
        for copy in query_back:
            copy.wait_recv()
        rows_out(0, rq, 0)
    with jax.named_scope("key_rows"):
        for copy in row_back:
            copy.wait_recv()
        rows_out(1, rkv, 0)
        rows_out(2, rkv, HD)
        for h in range(HEADS):
            rg_out[h:h + 1, :] = rkv[(h + NY - y) % NY, ROWS:ROWS + 1, 0:ROWS]

    with jax.named_scope("columns"):
        for m in range(3):
            @pl.when(near_index[m] != mine)
            def _():
                pltpu.make_async_remote_copy(
                    src_ref=f_msg.at[m], dst_ref=fg_out.at[m], send_sem=far_sems.at[0, m],
                    recv_sem=far_sems.at[1, m], device_id=(view, patch), device_id_type=MESH,
                ).wait_recv()

            @pl.when(far_owner[m] != mine)
            def _():
                far_copies[m].wait_send()
        for copy in started:
            copy.wait_send()


def finish(rows, rate_rows, groups, query_out, key_out, value_out, rate_out, fast_out, sems):
    copies = [
        pltpu.make_async_copy(rows.at[n], out, sems.at[n]) for n, out in enumerate((query_out, key_out, value_out))
    ]
    for copy in copies:
        copy.start()
    rate_out[...] = rate_rows[...]
    for m in range(3):
        fast_out[GROUP * m:GROUP * (m + 1), :] = groups[m, 0:GROUP, 0:HD]
    for copy in copies:
        copy.wait()


def scratch():
    tile = (8, 128)
    shapes = [
        pltpu.VMEM((3, HD, FF), f32),
        pltpu.VMEM((3, HALF, HD), f32),
        *[pltpu.VMEM((3, HALF, HD), bf16)] * 4,
        *[pltpu.VMEM((3, HALF, HD), f32)] * 2,
        pltpu.VMEM((3, 2, HALF, 1), f32),
        *[pltpu.VMEM((HEADS, ROWS + 8, 2 * HD), f32)] * 2,
        *[pltpu.VMEM((SLOTS, ROWS + 8, 2 * HD), f32)] * 2,
        *[pltpu.VMEM((ALL_ROWS, 1), f32)] * 2,
        *[pltpu.VMEM((ALL_ROWS, HD), bf16)] * 4,
        *[pltpu.VMEM((ALL_ROWS, HALF), f32)] * 7,
        *[pltpu.VMEM((ALL_ROWS, HALF), bf16)] * 12,
        pltpu.VMEM((3, HALF, HD), f32),
        pltpu.VMEM((ALL_ROWS // CHUNK, 8, CHUNK), f32),
        pltpu.VMEM((SLOTS, ROWS, HD), f32),
        *[pltpu.VMEM((4, ROWS, HD), f32)] * 3,
        pltpu.VMEM((SLOTS, ROWS + 8, 2 * HD), f32),
        *[pltpu.VMEM((4, ROWS + 8, 2 * HD), f32)] * 3,
    ]
    for part in PARTS:
        first, second, _, shard, window = part_sizes(part)
        shapes += [
            pltpu.VMEM((2, first * shard) + tile, f32),
            pltpu.VMEM((2, first - 1, shard) + tile, f32),
            pltpu.VMEM((2, shard) + tile, f32),
            pltpu.VMEM((2, second - 1, window) + tile, f32),
            pltpu.VMEM((2, window) + tile, f32),
            pltpu.VMEM((2, second - 1, window) + tile, f32),
            pltpu.VMEM((2, shard) + tile, f32),
            pltpu.VMEM((2, first * shard) + tile, f32),
        ]
    shapes += [
        pltpu.VMEM((HALF, 640), f32),
        pltpu.VMEM((NX - 1, HALF // NX, 640), f32),
        pltpu.VMEM((NZ, 8, 640), f32),
        pltpu.VMEM((NZ - 1, 8, 640), f32),
        pltpu.VMEM((HALF // GROUP, 8, 640), f32),
        pltpu.VMEM((3, 8, 256), f32),
        pltpu.SemaphoreType.DMA((N_SEMS,)),
        pltpu.SemaphoreType.DMA((N_SEMS,)),
        pltpu.SemaphoreType.DMA((2, 3)),
        pltpu.SemaphoreType.DMA((3,)),
    ]
    return shapes


def on_device(queries, key_rows, value_rows, step_rates, fast_init, out_grad):
    vmem = pl.BlockSpec(memory_space=pltpu.VMEM)
    anywhere = pl.BlockSpec(memory_space=pl.ANY)
    rates_shape = jax.ShapeDtypeStruct((HEADS, ROWS), f32)
    results = pl.pallas_call(
        kernel,
        out_shape=(
            jax.ShapeDtypeStruct((3, ROWS, HEADS * HD), bf16),
            rates_shape,
            jax.ShapeDtypeStruct((3, 8, 256), f32),
        ),
        in_specs=[vmem] * 5 + [anywhere],
        out_specs=(vmem,) * 3,
        scratch_shapes=scratch(),
        compiler_params=pltpu.CompilerParams(
            collective_id=0, has_side_effects=True, vmem_limit_bytes=56 * 2**20
        ),
        name="layer_grad",
    )(queries, key_rows, value_rows, step_rates.T, out_grad, fast_init)
    rows = jax.ShapeDtypeStruct((ROWS, HEADS * HD), bf16)
    query_grad, key_grad, value_grad, rate_grad, fast_grad = pl.pallas_call(
        finish,
        out_shape=(rows, rows, rows, rates_shape, jax.ShapeDtypeStruct((3 * GROUP, HD), f32)),
        in_specs=[vmem] * 3,
        out_specs=(anywhere,) * 3 + (vmem,) * 2,
        scratch_shapes=[pltpu.SemaphoreType.DMA((3,))],
        name="outputs",
    )(*results)
    return query_grad, key_grad, value_grad, rate_grad.T, fast_grad.T


def solution(mesh):
    both = ("view", "patch")
    return jax.shard_map(
        on_device,
        mesh=mesh,
        in_specs=(P(both, None), P(both, None), P(both, None), P(both, None), P(), P(both, None)),
        out_specs=(P(both, None), P(both, None), P(both, None), P(both, None), P(None, both)),
        check_vma=False,
    )
```

```python
import itertools
import math

import jax
import jax.numpy as jnp
from jax import lax
from jax.experimental import pallas as pl
from jax.experimental.pallas import tpu as pltpu
from jax.sharding import PartitionSpec as P

MESH = pl.DeviceIdType.MESH
f32, bf16 = jnp.float32, jnp.bfloat16

step_size = 0.2
epsilon = 1e-06

NX, NY, NZ = 4, 4, 8
HEADS, HD, FF = 4, 192, 384
HALF = FF // 2
ROWS = 128
SLOTS = 8
ALL_ROWS = SLOTS * ROWS
CHUNK = 256
TOTAL_ROWS = ROWS * NX * NY * NZ * 2
COEFFICIENT = step_size * math.sqrt(TOTAL_ROWS)
N_SEMS = 240
GROUP = 6


def device(x, y, z, core):
    return ((x // 2) * 2 + core, (y * 2 + x % 2) * 8 + z)


BLOCKS = 2
UNITS = HALF // BLOCKS
PAD = 128
ROW_TILES = UNITS // 8
PIECE = UNITS // NX

PARTS = (("x", (0, 1, 2)), ("z", (3, 4)))


def part_sizes(part):
    axis, lane_tiles = part
    first, second = (NX, NZ) if axis == "x" else (NZ, NX)
    shard = ROW_TILES * len(lane_tiles) // first
    window = -(-shard // second)
    if (shard - window) // (second - 1) >= window and shard > second:
        window += 1
    return first, second, shard, window


def nt(a, b):
    return lax.dot_general(a, b, (((1,), (1,)), ((), ())), preferred_element_type=f32)


def nn(a, b):
    return lax.dot_general(a, b, (((1,), (0,)), ((), ())), preferred_element_type=f32)


def tn(a, b):
    return lax.dot_general(a, b, (((0,), (0,)), ((), ())), preferred_element_type=f32)


def split(value):
    high = value.astype(bf16)
    return high, (value - high.astype(f32)).astype(bf16)


def kernel(
    q_hbm, k_hbm, v_hbm, r_ref, g_hbm, w_hbm,
    rows_ref, rg_out, fg_out,
    q_ref, k_ref, v_ref, g_ref,
    w_load, w_own, wh_ab, wl_ab, nh_ab, nl_ab, wh_c, wl_c, nh_c, nl_c, moved, gm, norms,
    kv_send, qg_send, kv, qg, rates, inv_rates, kb, vb, qb, gb,
    gate_s, up_s, pull_s, m1, m2, m3, m4,
    s_ab_h, s_ab_l, e_ab_h, e_ab_l, s_c_h, s_c_l, e_c_h, e_c_l,
    acc_ab, acc_c, rate_rows, dq, xq, oq, rq, dkv, xkv, okv, rkv,
    p0_t, p0_r1, p0_s1, p0_r2, p0_s2, p0_a1, p0_f1, p0_g,
    p1_t, p1_r1, p1_s1, p1_r2, p1_s2, p1_a1, p1_f1, p1_g,
    f_t, f_r1, f_s1, f_r2, d_grp, f_msg,
    send_sems, recv_sems, far_sems, load_sems,
):
    view, patch = lax.axis_index("view"), lax.axis_index("patch")
    x, core = (view // 2) * 2 + (patch // 8) % 2, view % 2
    y, z = patch // 16, patch % 8
    mine = view * 64 + patch
    half_block = 2 * y + core

    def peer(axis, offset):
        if axis == "x":
            return device((x + offset) % NX, y, z, core)
        if axis == "y":
            return device(x, (y + offset) % NY, z, core)
        if axis == "z":
            return device(x, y, (z + offset) % NZ, core)
        return device(x, y, z, 1 - core)

    place = {"x": x, "z": z}

    far_group = [32 * (8 * m + half_block) + 8 * x + z for m in range(3)]
    far_owner = [group // 3 for group in far_group]
    near_source = []
    for t in range(3):
        group = 3 * mine + t
        block, rest = group // 32, group % 32
        near_source.append((rest // 8, (block % 8) // 2, rest % 8, block % 2))
    near_index = []
    for sx, sy, sz, sc in near_source:
        sv, sp = device(sx, sy, sz, sc)
        near_index.append(sv * 64 + sp)

    barrier = pltpu.get_barrier_semaphore()
    peers = [("x", d) for d in range(1, NX)] + [("z", d) for d in range(1, NZ)]
    peers += [("y", d) for d in range(1, NY)] + [("core", 1)]
    for axis, offset in peers:
        pl.semaphore_signal(barrier, inc=1, device_id=peer(axis, offset), device_id_type=MESH)
    for t in range(3):
        @pl.when(near_index[t] != mine)
        def _():
            pl.semaphore_signal(barrier, inc=1, device_id=device(*near_source[t]), device_id_type=MESH)

    ids = itertools.count()
    started = []

    def send(src, dst, target):
        which = next(ids)
        copy = pltpu.make_async_remote_copy(
            src_ref=src, dst_ref=dst, send_sem=send_sems.at[which], recv_sem=recv_sems.at[which],
            device_id=target, device_id_type=MESH,
        )
        copy.start()
        started.append(copy)
        return copy

    row_loads = []
    for n, (src, dst) in enumerate(((k_hbm, k_ref), (v_hbm, v_ref), (q_hbm, q_ref), (g_hbm, g_ref))):
        load = pltpu.make_async_copy(src, dst, load_sems.at[3 + n])
        load.start()
        row_loads.append(load)
    loads = []
    for m in range(3):
        first = pl.multiple_of(m * HEADS * FF + y * FF, 128)
        load = pltpu.make_async_copy(w_hbm.at[:, pl.ds(first, FF)], w_load.at[m], load_sems.at[m])
        load.start()
        loads.append(load)

    def pack(buffer, left, right):
        for h in range(HEADS):
            cols = slice(HD * h, HD * (h + 1))
            buffer[h, 0:ROWS, 0:HD] = left[:, cols].astype(f32)
            buffer[h, 0:ROWS, HD:2 * HD] = right[:, cols].astype(f32)

    row_loads[0].wait()
    row_loads[1].wait()
    pack(kv_send, k_ref, v_ref)
    for h in range(HEADS):
        kv_send[h, ROWS:ROWS + 8, :] = jnp.zeros((8, 2 * HD), f32)
        kv_send[h, ROWS:ROWS + 8, 0:ROWS] = jnp.broadcast_to(r_ref[h:h + 1, :], (8, ROWS))

    far_count = sum((owner != mine).astype(jnp.int32) for owner in far_owner)
    pl.semaphore_wait(barrier, len(peers) + far_count)

    def scatter_heads(buffer, landing):
        out = {}
        for d in (1, 3, 2):
            out[d] = send(buffer.at[(y + d) % NY], landing.at[d], peer("y", d))
        out["own"] = send(buffer.at[y], landing.at[4], peer("core", 1))
        return out

    kv_copies = scatter_heads(kv_send, kv)
    row_loads[2].wait()
    row_loads[3].wait()
    pack(qg_send, q_ref, g_ref)

    def store_weights(ab_h, ab_l, c_h, c_l, b, m, value):
        if m < 2:
            rows = (b, slice(PAD * m, PAD * m + UNITS))
            ab_h[rows], ab_l[rows] = split(value)
        else:
            rows = (b, slice(0, UNITS))
            c_h[rows], c_l[rows] = split(value)

    for b in range(BLOCKS):
        none = jnp.zeros((PAD - UNITS, HD), bf16)
        for ref in (wh_ab, wl_ab, nh_ab, nl_ab):
            ref[b, UNITS:PAD] = none
            ref[b, PAD + UNITS:2 * PAD] = none
        for ref in (wh_c, wl_c, nh_c, nl_c):
            ref[b, UNITS:PAD] = none
    for m in range(3):
        loads[m].wait()
        both = w_load[m]
        own = jnp.where(core == 0, both[:, 0:HALF], both[:, HALF:FF]).T
        for b in range(BLOCKS):
            pieces = [own[2 * PIECE * n + PIECE * b:2 * PIECE * n + PIECE * (b + 1), :] for n in range(NX)]
            block = jnp.concatenate(pieces, axis=0)
            w_own[b, m] = block
            norms[b, m, 0] = jnp.sqrt(jnp.sum(block * block, axis=1, keepdims=True) + epsilon)
            store_weights(wh_ab, wl_ab, wh_c, wl_c, b, m, block)

    def row_block(s):
        first = (s % 4) * CHUNK + (s // 4) * ROWS
        return slice(first, first + ROWS)

    def unpack_kv(s):
        kb[row_block(s), :] = kv[s, 0:ROWS, 0:HD].astype(bf16)
        vb[row_block(s), :] = kv[s, 0:ROWS, HD:2 * HD].astype(bf16)
        column = kv[s, ROWS:ROWS + 8, 0:ROWS].T[:, 0:1]
        rates[row_block(s), :] = column
        inv_rates[row_block(s), :] = 1.0 / column

    def unpack_qg(s):
        qb[row_block(s), :] = qg[s, 0:ROWS, 0:HD].astype(bf16)
        gb[row_block(s), :] = qg[s, 0:ROWS, HD:2 * HD].astype(bf16)

    def silu_parts(gate):
        sig = 1.0 / (1.0 + jnp.exp(-gate))
        act = gate * sig
        slope = sig + act * (1.0 - sig)
        return sig, act, slope

    def clear(b):
        acc_ab[b] = jnp.zeros((2 * PAD, HD), f32)
        acc_c[b] = jnp.zeros((PAD, HD), f32)

    for b in range(BLOCKS):
        clear(b)

    GATE, UP = slice(0, PAD), slice(PAD, 2 * PAD)

    def add_terms(b, rows, gate_term, up_term, pull_term, left, right):
        s_ab_h[b, rows, GATE], s_ab_l[b, rows, GATE] = split(gate_term)
        s_ab_h[b, rows, UP], s_ab_l[b, rows, UP] = split(up_term)
        s_c_h[b, rows, :], s_c_l[b, rows, :] = split(pull_term)
        acc_ab[b] += tn(s_ab_h[b, rows, :], left) + tn(s_ab_l[b, rows, :], left)
        acc_c[b] += tn(s_c_h[b, rows, :], right) + tn(s_c_l[b, rows, :], right)

    def update_chunk(b, i):
        rows = slice(i * CHUNK, (i + 1) * CHUNK)
        keys, values, eta = kb[rows, :], vb[rows, :], rates[rows, :]
        both = nt(keys, wh_ab[b]) + nt(keys, wl_ab[b])
        gate, up = both[:, GATE], both[:, UP]
        pulled = nt(values, wh_c[b]) + nt(values, wl_c[b])
        gate_s[b, rows, :], up_s[b, rows, :], pull_s[b, rows, :] = gate, up, pulled
        _, act, slope = silu_parts(gate)
        scaled = -eta * pulled
        add_terms(b, rows, scaled * up * slope, scaled * act, -eta * act * up, keys, values)

    def take_pair(d):
        unpack_kv(d)
        unpack_kv(4 + d)

    def pass_on(copies, landing, d):
        copies[d].wait_recv()
        return send(landing.at[d], landing.at[4 + d], peer("core", 1))

    with jax.named_scope("keys_own"):
        kv[0] = kv_send[y]
        kv_copies["own"].wait_recv()
        take_pair(0)
        for b in range(BLOCKS):
            update_chunk(b, 0)
    passed = {}
    with jax.named_scope("keys_first"):
        passed[1] = pass_on(kv_copies, kv, 1)
        passed[3] = pass_on(kv_copies, kv, 3)
        passed[1].wait_recv()
        take_pair(1)
        for b in range(BLOCKS):
            update_chunk(b, 1)
    with jax.named_scope("keys_second"):
        passed[2] = pass_on(kv_copies, kv, 2)
        qg_copies = scatter_heads(qg_send, qg)
        passed[3].wait_recv()
        take_pair(3)
        for b in range(BLOCKS):
            update_chunk(b, 3)
    with jax.named_scope("keys_third"):
        passed[2].wait_recv()
        take_pair(2)

    rate_sum = sum(kv[s, ROWS:ROWS + 8, 0:ROWS] for s in range(SLOTS))
    total_part = jnp.sum(rate_sum[0:1, :], axis=1, keepdims=True)

    parts = (
        (p0_t, p0_r1, p0_s1, p0_r2, p0_s2, p0_a1, p0_f1, p0_g),
        (p1_t, p1_r1, p1_s1, p1_r2, p1_s2, p1_a1, p1_f1, p1_g),
    )

    def lanes_of(first, second, third, tail):
        return (
            first[:, 0:128],
            second[:, 0:128],
            jnp.concatenate([first[:, 128:192], second[:, 128:192]], axis=1),
            third[:, 0:128],
            jnp.concatenate([third[:, 128:192], tail], axis=1),
        )

    def sums_of(b, tail):
        return lanes_of(
            acc_ab[b, 0:UNITS, :], acc_ab[b, PAD:PAD + UNITS, :], acc_c[b, 0:UNITS, :], tail
        )

    def start_stage(r, p, source):
        axis, lane_tiles = PARTS[p]
        first, second, shard, window = part_sizes(PARTS[p])
        t = parts[p][0]
        for jj, j in enumerate(lane_tiles):
            t[r, jj * ROW_TILES:(jj + 1) * ROW_TILES] = source[j].reshape(ROW_TILES, 8, 128)
        copies = []
        for d in range(1, first):
            there = (place[axis] + d) % first
            copies.append(send(t.at[r, pl.ds(there * shard, shard)], parts[p][1].at[r, d - 1], peer(axis, d)))
        return copies

    def start_of(p, k):
        _, second, shard, window = part_sizes(PARTS[p])
        return ((shard - window) * k) // (second - 1)

    def second_stage(r, p, copies):
        axis = PARTS[p][0]
        other = "z" if axis == "x" else "x"
        first, second, shard, window = part_sizes(PARTS[p])
        t, r1, s1, r2 = parts[p][:4]
        total = t[r, pl.ds(place[axis] * shard, shard)]
        for d in range(1, first):
            copies[d - 1].wait_recv()
            total = total + r1[r, d - 1]
        s1[r] = total
        out = []
        for d in range(1, second):
            there = (place[other] + d) % second
            out.append(send(s1.at[r, pl.ds(start_of(p, there), window)], r2.at[r, d - 1], peer(other, d)))
        return out

    def third_stage(r, p, copies):
        other = "z" if PARTS[p][0] == "x" else "x"
        _, second, shard, window = part_sizes(PARTS[p])
        _, _, s1, r2, s2, a1, f1, _ = parts[p]
        total = s1[r, pl.ds(start_of(p, place[other]), window)]
        for d in range(1, second):
            copies[d - 1].wait_recv()
            total = total + r2[r, d - 1]
        s2[r] = total
        return [send(s2.at[r], a1.at[r, d - 1], peer(other, d)) for d in range(1, second)]

    def fourth_stage(r, p, copies):
        axis = PARTS[p][0]
        other = "z" if axis == "x" else "x"
        first, second, shard, window = part_sizes(PARTS[p])
        _, _, _, _, s2, a1, f1, g = parts[p]
        f1[r, pl.ds(start_of(p, place[other]), window)] = s2[r]
        for d in range(1, second):
            copies[d - 1].wait_recv()
            there = (place[other] + second - d) % second
            f1[r, pl.ds(start_of(p, there), window)] = a1[r, d - 1]
        here = pl.ds(place[axis] * shard, shard)
        out = [send(f1.at[r], g.at[r, here], peer(axis, d)) for d in range(1, first)]
        g[r, here] = f1[r]
        return out

    class Sum:
        def __init__(self, r, b):
            self.r = 2 * r + b
            self.b = b

        def start(self, tail):
            source = sums_of(self.b, tail)
            self.copies = [start_stage(self.r, p, source) for p in (1, 0)][::-1]

        def step(self, stage):
            self.copies = [stage(self.r, p, self.copies[p]) for p in range(2)]

        def result(self):
            for group in self.copies:
                for copy in group:
                    copy.wait_recv()
            tiles = {}
            for p in range(2):
                for jj, j in enumerate(PARTS[p][1]):
                    tiles[j] = parts[p][7][self.r, jj * ROW_TILES:(jj + 1) * ROW_TILES].reshape(UNITS, 128)
            gate = jnp.concatenate([tiles[0], tiles[2][:, 0:64]], axis=1)
            up = jnp.concatenate([tiles[1], tiles[2][:, 64:128]], axis=1)
            down = jnp.concatenate([tiles[3], tiles[4][:, 0:64]], axis=1)
            return (gate, up, down), tiles[4][0:1, 64:65]

    def prepare_chunk(i, _):
        rows = pl.ds(pl.multiple_of(i * CHUNK, CHUNK), CHUNK)
        eta = rates[rows, :]
        for b in range(BLOCKS):
            gate, up, pulled = gate_s[b, rows, :], up_s[b, rows, :], pull_s[b, rows, :]
            sig, act, slope = silu_parts(gate)
            curve = sig * (1.0 - sig) * (2.0 + gate * (1.0 - 2.0 * sig))
            scaled = eta * pulled
            by_slope, by_act = eta * (up * slope), eta * act
            m1[b, rows, :], m2[b, rows, :] = scaled * up * curve, scaled * slope
            m3[b, rows, :], m4[b, rows, :] = by_slope, by_act
            e_ab_h[b, rows, GATE], e_ab_l[b, rows, GATE] = split(by_slope * pulled)
            e_ab_h[b, rows, UP], e_ab_l[b, rows, UP] = split(by_act * pulled)
            e_c_h[b, rows, :], e_c_l[b, rows, :] = split(by_act * up)
        return 0

    query_passed = {}

    def prepare():
        lax.fori_loop(0, ALL_ROWS // CHUNK, prepare_chunk, 0)

    def pass_queries():
        qg[0] = qg_send[y]
        for d in (1, 3, 2):
            query_passed[d] = pass_on(qg_copies, qg, d)

    def take_queries():
        qg_copies["own"].wait_recv()
        for d in (1, 3, 2):
            query_passed[d].wait_recv()
        for s in range(SLOTS):
            unpack_qg(s)

    tail = jnp.broadcast_to(total_part, (UNITS, 64))
    sums = [Sum(0, b) for b in range(BLOCKS)]
    for b in range(BLOCKS):
        with jax.named_scope("keys_last"):
            update_chunk(b, 2)
            sums[b].start(tail)
    prepare()
    for stage, work in ((second_stage, pass_queries), (third_stage, take_queries), (fourth_stage, None)):
        for b in range(BLOCKS):
            sums[b].step(stage)
        if work is not None:
            work()

    def new_weights(b):
        terms, total = sums[b].result()
        scale = COEFFICIENT / total
        for m in range(3):
            change = terms[m] * scale
            shifted = w_own[b, m] - change
            inverse = lax.rsqrt(jnp.sum(shifted * shifted, axis=1, keepdims=True) + epsilon)
            gm[b, m], moved[b, m], norms[b, m, 1] = change, shifted, inverse
            store_weights(nh_ab, nl_ab, nh_c, nl_c, b, m, shifted * (norms[b, m, 0] * inverse))
        clear(b)
        return total, scale

    def apply_block(b):
        def apply_chunk(i, _):
            rows = pl.ds(pl.multiple_of(i * CHUNK, CHUNK), CHUNK)
            queries, grads = qb[rows, :], gb[rows, :]
            both = nt(queries, nh_ab[b]) + nt(queries, nl_ab[b])
            gate, up = both[:, GATE], both[:, UP]
            pulled = nt(grads, nh_c[b]) + nt(grads, nl_c[b])
            _, act, slope = silu_parts(gate)
            add_terms(b, rows, pulled * up * slope, pulled * act, act * up, queries, grads)
            return 0

        lax.fori_loop(0, ALL_ROWS // CHUNK, apply_chunk, 0)

    new_sums = [Sum(1, b) for b in range(BLOCKS)]
    for b in range(BLOCKS):
        with jax.named_scope("apply"):
            totals, scale = new_weights(b)
            apply_block(b)
            new_sums[b].start(jnp.zeros((UNITS, 64), f32))

    def product(ah, al, bh, bl, rows):
        high = ah[rows, :]
        return nn(high, bh) + nn(high, bl) + nn(al[rows, :], bh)

    def query_grads(b):
        def query_chunk(i, _):
            rows = pl.ds(pl.multiple_of(i * ROWS, ROWS), ROWS)
            slot = (i % 2) * 4 + i // 2
            part = product(s_ab_h.at[b], s_ab_l.at[b], nh_ab[b], nl_ab[b], rows)
            dq[slot] = part if b == 0 else dq[slot] + part
            return 0

        lax.fori_loop(0, SLOTS, query_chunk, 0)

    def return_rows(pair, partial, arrived, sums, landing):
        pair.wait_recv()
        out = []
        for d in (1, 3, 2, 0):
            if d == 0:
                landing[0] = partial[0] + arrived[0]
            else:
                sums[d] = partial[d] + arrived[d]
                out.append(send(sums.at[d], landing.at[d], peer("y", NY - d)))
        return out

    for b in range(BLOCKS):
        with jax.named_scope("query_grads"):
            query_grads(b)
        new_sums[b].step(second_stage)
    query_pair = send(dq.at[pl.ds(4, 4)], xq, peer("core", 1))
    new_sums[0].step(third_stage)
    query_back = return_rows(query_pair, dq, xq, oq, rq)
    new_sums[1].step(third_stage)
    for b in range(BLOCKS):
        new_sums[b].step(fourth_stage)

    direct = {}

    def pull_weights(b):
        d_new, _ = new_sums[b].result()
        head_part = jnp.zeros((1, 1), f32)
        for m in range(3):
            init_norm, inverse = norms[b, m, 0], norms[b, m, 1]
            shifted = moved[b, m]
            dots = jnp.sum(d_new[m] * shifted, axis=1, keepdims=True)
            d_moved = d_new[m] * (init_norm * inverse) - shifted * (dots * init_norm * inverse * inverse * inverse)
            direct[b, m] = d_moved + w_own[b, m] * (dots * inverse / init_norm)
            by_row = jnp.sum(d_moved * gm[b, m], axis=1, keepdims=True)
            head_part = head_part - jnp.sum(by_row, axis=0, keepdims=True)
            store_weights(nh_ab, nl_ab, nh_c, nl_c, b, m, d_moved * scale)
        clear(b)
        return -head_part / totals

    def pull_block(b):
        def pull_chunk(i, _):
            rows = pl.ds(pl.multiple_of(i * CHUNK, CHUNK), CHUNK)
            keys, values = kb[rows, :], vb[rows, :]
            both = nt(keys, nh_ab[b]) + nt(keys, nl_ab[b])
            one, two = both[:, GATE], both[:, UP]
            three = nt(values, nh_c[b]) + nt(values, nl_c[b])
            by_slope, by_act, by_two = m3[b, rows, :], m4[b, rows, :], m2[b, rows, :]
            c_gate = one * m1[b, rows, :] + two * by_two + three * by_slope
            c_up = one * by_two + three * by_act
            c_pull = one * by_slope + two * by_act
            add_terms(b, rows, c_gate, c_up, c_pull, keys, values)
            by_rate = c_pull * pull_s[b, rows, :] + three * (by_act * up_s[b, rows, :])
            by_rate_h, by_rate_l = split(by_rate * inv_rates[rows, :])
            ones = jnp.ones((8, PAD), bf16)
            part = nt(ones, by_rate_h) + nt(ones, by_rate_l)
            rate_rows[i] = part if b == 0 else rate_rows[i] + part
            return 0

        lax.fori_loop(0, ALL_ROWS // CHUNK, pull_chunk, 0)

    weight_copies = []
    d_totals = jnp.zeros((1, 1), f32)
    for b in range(BLOCKS):
        with jax.named_scope("pull"):
            d_totals = d_totals + pull_weights(b)
            pull_block(b)
            tiles = sums_of(b, jnp.zeros((UNITS, 64), f32))
            for j in range(5):
                f_t[b, :, 128 * j:128 * (j + 1)] = tiles[j]
            for d in range(1, NX):
                first = pl.multiple_of(((x + d) % NX) * PIECE, PIECE)
                weight_copies.append(send(f_t.at[b, pl.ds(first, PIECE)], f_r1.at[b, d - 1], peer("x", d)))

    def key_chunk(i, _):
        rows = pl.ds(pl.multiple_of(i * ROWS, ROWS), ROWS)
        slot = (i % 2) * 4 + i // 2
        key_part, value_part = 0.0, 0.0
        for b in range(BLOCKS):
            key_part += product(s_ab_h.at[b], s_ab_l.at[b], wh_ab[b], wl_ab[b], rows)
            key_part += product(e_ab_h.at[b], e_ab_l.at[b], nh_ab[b], nl_ab[b], rows)
            value_part += product(s_c_h.at[b], s_c_l.at[b], wh_c[b], wl_c[b], rows)
            value_part += product(e_c_h.at[b], e_c_l.at[b], nh_c[b], nl_c[b], rows)
        dkv[slot, 0:ROWS, 0:HD] = key_part
        dkv[slot, 0:ROWS, HD:2 * HD] = value_part
        return 0

    with jax.named_scope("row_grads"):
        lax.fori_loop(0, SLOTS, key_chunk, 0)
        for s in range(SLOTS):
            dkv[s, ROWS:ROWS + 8, :] = jnp.zeros((8, 2 * HD), f32)
            lane = (s // 4) * ROWS
            dkv[s, ROWS:ROWS + 8, 0:ROWS] = rate_rows[s % 4, :, lane:lane + ROWS] + d_totals
        pair = send(dkv.at[pl.ds(4, 4)], xkv, peer("core", 1))

    with jax.named_scope("x_sums"):
        for b in range(BLOCKS):
            total = f_t[b, pl.ds(pl.multiple_of(x * PIECE, PIECE), PIECE), :]
            for d in range(1, NX):
                weight_copies[(NX - 1) * b + d - 1].wait_recv()
                total = total + f_r1[b, d - 1]
            for n in range(4):
                f_s1[4 * b + n, 0:GROUP, :] = total[GROUP * n:GROUP * (n + 1), :]
                f_s1[4 * b + n, GROUP:8, :] = jnp.zeros((8 - GROUP, 640), f32)
        weight_copies = [send(f_s1.at[(z + d) % NZ], f_r2.at[d - 1], peer("z", d)) for d in range(1, NZ)]
    with jax.named_scope("row_returns"):
        row_back = return_rows(pair, dkv, xkv, okv, rkv)
    with jax.named_scope("direct"):
        for b in range(BLOCKS):
            tiles = lanes_of(direct[b, 0], direct[b, 1], direct[b, 2], jnp.zeros((UNITS, 64), f32))
            for j in range(5):
                for n in range(16):
                    group = 8 * (n // 4) + 4 * b + n % 4
                    d_grp[group, 0:GROUP, 128 * j:128 * (j + 1)] = tiles[j][GROUP * n:GROUP * (n + 1), :]

    z_scope = jax.named_scope("z_sums")
    z_scope.__enter__()
    total = f_s1[z]
    for d in range(1, NZ):
        weight_copies[d - 1].wait_recv()
        total = total + f_r2[d - 1]
    total = (total + d_grp[8 * x + z]) * (1.0 / math.sqrt(TOTAL_ROWS))
    for m, (low, high) in enumerate(((0, 256), (128, 320), (384, 512))):
        f_msg[m, :, 0:128] = total[:, low:low + 128]
        f_msg[m, :, 128:HD] = total[:, high:high + 64]
    far_copies = []
    for m in range(3):
        slot = far_group[m] % 3
        owner = far_owner[m]
        copy = pltpu.make_async_remote_copy(
            src_ref=f_msg.at[m], dst_ref=fg_out.at[slot], send_sem=far_sems.at[0, m], recv_sem=far_sems.at[1, slot],
            device_id=(owner // 64, owner % 64), device_id_type=MESH,
        )

        @pl.when(owner != mine)
        def _():
            copy.start()

        @pl.when(owner == mine)
        def _():
            fg_out[slot] = f_msg[m]

        far_copies.append(copy)

    z_scope.__exit__(None, None, None)

    def rows_out(which, landing, lanes):
        for h in range(HEADS):
            d = (h + NY - y) % NY
            rows_ref[which, :, HD * h:HD * (h + 1)] = landing[d, 0:ROWS, lanes:lanes + HD].astype(bf16)

    with jax.named_scope("query_rows"):
        for copy in query_back:
            copy.wait_recv()
        rows_out(0, rq, 0)
    with jax.named_scope("key_rows"):
        for copy in row_back:
            copy.wait_recv()
        rows_out(1, rkv, 0)
        rows_out(2, rkv, HD)
        for h in range(HEADS):
            rg_out[h:h + 1, :] = rkv[(h + NY - y) % NY, ROWS:ROWS + 1, 0:ROWS]

    with jax.named_scope("columns"):
        for m in range(3):
            @pl.when(near_index[m] != mine)
            def _():
                pltpu.make_async_remote_copy(
                    src_ref=f_msg.at[m], dst_ref=fg_out.at[m], send_sem=far_sems.at[0, m],
                    recv_sem=far_sems.at[1, m], device_id=(view, patch), device_id_type=MESH,
                ).wait_recv()

            @pl.when(far_owner[m] != mine)
            def _():
                far_copies[m].wait_send()
        for copy in started:
            copy.wait_send()


def finish(rows, rate_rows, groups, query_out, key_out, value_out, rate_out, fast_out, sems):
    copies = [
        pltpu.make_async_copy(rows.at[n], out, sems.at[n]) for n, out in enumerate((query_out, key_out, value_out))
    ]
    for copy in copies:
        copy.start()
    rate_out[...] = rate_rows[...]
    for m in range(3):
        fast_out[GROUP * m:GROUP * (m + 1), :] = groups[m, 0:GROUP, 0:HD]
    for copy in copies:
        copy.wait()


def scratch():
    tile = (8, 128)
    halves = (BLOCKS, ALL_ROWS)
    shapes = [
        *[pltpu.VMEM((ROWS, HEADS * HD), bf16)] * 4,
        pltpu.VMEM((3, HD, FF), f32),
        pltpu.VMEM((BLOCKS, 3, UNITS, HD), f32),
        *[pltpu.VMEM((BLOCKS, 2 * PAD, HD), bf16)] * 4,
        *[pltpu.VMEM((BLOCKS, PAD, HD), bf16)] * 4,
        *[pltpu.VMEM((BLOCKS, 3, UNITS, HD), f32)] * 2,
        pltpu.VMEM((BLOCKS, 3, 2, UNITS, 1), f32),
        *[pltpu.VMEM((HEADS, ROWS + 8, 2 * HD), f32)] * 2,
        *[pltpu.VMEM((SLOTS, ROWS + 8, 2 * HD), f32)] * 2,
        *[pltpu.VMEM((ALL_ROWS, 1), f32)] * 2,
        *[pltpu.VMEM((ALL_ROWS, HD), bf16)] * 4,
        *[pltpu.VMEM(halves + (PAD,), f32)] * 7,
        *[pltpu.VMEM(halves + (2 * PAD,), bf16)] * 4,
        *[pltpu.VMEM(halves + (PAD,), bf16)] * 4,
        pltpu.VMEM((BLOCKS, 2 * PAD, HD), f32),
        pltpu.VMEM((BLOCKS, PAD, HD), f32),
        pltpu.VMEM((ALL_ROWS // CHUNK, 8, CHUNK), f32),
        pltpu.VMEM((SLOTS, ROWS, HD), f32),
        *[pltpu.VMEM((4, ROWS, HD), f32)] * 3,
        pltpu.VMEM((SLOTS, ROWS + 8, 2 * HD), f32),
        *[pltpu.VMEM((4, ROWS + 8, 2 * HD), f32)] * 3,
    ]
    rounds = 2 * BLOCKS
    for part in PARTS:
        first, second, shard, window = part_sizes(part)
        shapes += [
            pltpu.VMEM((rounds, first * shard) + tile, f32),
            pltpu.VMEM((rounds, first - 1, shard) + tile, f32),
            pltpu.VMEM((rounds, shard) + tile, f32),
            pltpu.VMEM((rounds, second - 1, window) + tile, f32),
            pltpu.VMEM((rounds, window) + tile, f32),
            pltpu.VMEM((rounds, second - 1, window) + tile, f32),
            pltpu.VMEM((rounds, shard) + tile, f32),
            pltpu.VMEM((rounds, first * shard) + tile, f32),
        ]
    shapes += [
        pltpu.VMEM((BLOCKS, UNITS, 640), f32),
        pltpu.VMEM((BLOCKS, NX - 1, PIECE, 640), f32),
        pltpu.VMEM((NZ, 8, 640), f32),
        pltpu.VMEM((NZ - 1, 8, 640), f32),
        pltpu.VMEM((HALF // GROUP, 8, 640), f32),
        pltpu.VMEM((3, 8, 256), f32),
        pltpu.SemaphoreType.DMA((N_SEMS,)),
        pltpu.SemaphoreType.DMA((N_SEMS,)),
        pltpu.SemaphoreType.DMA((2, 3)),
        pltpu.SemaphoreType.DMA((7,)),
    ]
    return shapes


def on_device(queries, key_rows, value_rows, step_rates, fast_init, out_grad):
    vmem = pl.BlockSpec(memory_space=pltpu.VMEM)
    anywhere = pl.BlockSpec(memory_space=pl.ANY)
    rates_shape = jax.ShapeDtypeStruct((HEADS, ROWS), f32)
    results = pl.pallas_call(
        kernel,
        out_shape=(
            jax.ShapeDtypeStruct((3, ROWS, HEADS * HD), bf16),
            rates_shape,
            jax.ShapeDtypeStruct((3, 8, 256), f32),
        ),
        in_specs=[anywhere] * 3 + [vmem] + [anywhere] * 2,
        out_specs=(vmem,) * 3,
        scratch_shapes=scratch(),
        compiler_params=pltpu.CompilerParams(
            collective_id=0, has_side_effects=True, vmem_limit_bytes=56 * 2**20
        ),
        name="layer_grad",
    )(queries, key_rows, value_rows, step_rates.T, out_grad, fast_init)
    rows = jax.ShapeDtypeStruct((ROWS, HEADS * HD), bf16)
    query_grad, key_grad, value_grad, rate_grad, fast_grad = pl.pallas_call(
        finish,
        out_shape=(rows, rows, rows, rates_shape, jax.ShapeDtypeStruct((3 * GROUP, HD), f32)),
        in_specs=[vmem] * 3,
        out_specs=(anywhere,) * 3 + (vmem,) * 2,
        scratch_shapes=[pltpu.SemaphoreType.DMA((3,))],
        name="outputs",
    )(*results)
    return query_grad, key_grad, value_grad, rate_grad.T, fast_grad.T


def solution(mesh):
    both = ("view", "patch")
    return jax.shard_map(
        on_device,
        mesh=mesh,
        in_specs=(P(both, None), P(both, None), P(both, None), P(both, None), P(), P(both, None)),
        out_specs=(P(both, None), P(both, None), P(both, None), P(both, None), P(None, both)),
        check_vma=False,
    )
```

```python
import itertools
import math

import jax
import jax.numpy as jnp
from jax import lax
from jax.experimental import pallas as pl
from jax.experimental.pallas import tpu as pltpu
from jax.sharding import PartitionSpec as P

MESH = pl.DeviceIdType.MESH
f32, bf16 = jnp.float32, jnp.bfloat16

step_size = 0.2
epsilon = 1e-06

NX, NY, NZ = 4, 4, 8
HEADS, HD, FF = 4, 192, 384
HALF = FF // 2
ROWS = 128
SLOTS = 8
ALL_ROWS = SLOTS * ROWS
CHUNK = 256
TOTAL_ROWS = ROWS * NX * NY * NZ * 2
COEFFICIENT = step_size * math.sqrt(TOTAL_ROWS)
N_SEMS = 64
GROUP = 6


def device(x, y, z, core):
    return ((x // 2) * 2 + core, (y * 2 + x % 2) * 8 + z)


BLOCKS = 2
UNITS = HALF // BLOCKS
PAD = 128
ROW_TILES = UNITS // 8
PIECE = UNITS // NX

PARTS = (("x", (0, 1, 2, 3, 4)),)


def part_sizes(part):
    axis, lane_tiles = part
    first, second = (NX, NZ) if axis == "x" else (NZ, NX)
    shard = ROW_TILES * len(lane_tiles) // first
    window = -(-shard // second)
    if (shard - window) // (second - 1) >= window and shard > second:
        window += 1
    return first, second, shard, window


def nt(a, b):
    return lax.dot_general(a, b, (((1,), (1,)), ((), ())), preferred_element_type=f32)


def nn(a, b):
    return lax.dot_general(a, b, (((1,), (0,)), ((), ())), preferred_element_type=f32)


def tn(a, b):
    return lax.dot_general(a, b, (((0,), (0,)), ((), ())), preferred_element_type=f32)


def split(value):
    high = value.astype(bf16)
    return high, (value - high.astype(f32)).astype(bf16)


def kernel(
    q_hbm, k_hbm, v_hbm, r_ref, g_hbm, w_hbm,
    rows_ref, rg_out, fg_out,
    q_ref, k_ref, v_ref, g_ref,
    w_load, w_own, wh_ab, wl_ab, nh_ab, nl_ab, wh_c, wl_c, nh_c, nl_c, moved, gm, norms,
    kv_send, qg_send, kv, qg, rates, inv_rates, kb, vb, qb, gb,
    gate_s, up_s, pull_s, m1, m2, m3, m4,
    s_ab_h, s_ab_l, e_ab_h, e_ab_l, s_c_h, s_c_l, e_c_h, e_c_l,
    acc_ab, acc_c, rate_rows, dq, xq, oq, rq, dkv, xkv, okv, rkv,
    p0_t, p0_r1, p0_s1, p0_r2, p0_s2, p0_a1, p0_f1, p0_g,
    f_t, f_r1, f_s1, f_r2, d_grp, f_msg,
    send_sems, recv_sems, far_sems, load_sems,
):
    view, patch = lax.axis_index("view"), lax.axis_index("patch")
    x, core = (view // 2) * 2 + (patch // 8) % 2, view % 2
    y, z = patch // 16, patch % 8
    mine = view * 64 + patch
    half_block = 2 * y + core

    def peer(axis, offset):
        if axis == "x":
            return device((x + offset) % NX, y, z, core)
        if axis == "y":
            return device(x, (y + offset) % NY, z, core)
        if axis == "z":
            return device(x, y, (z + offset) % NZ, core)
        return device(x, y, z, 1 - core)

    place = {"x": x, "z": z}

    far_group = [32 * (8 * m + half_block) + 8 * x + z for m in range(3)]
    far_owner = [group // 3 for group in far_group]
    near_source = []
    for t in range(3):
        group = 3 * mine + t
        block, rest = group // 32, group % 32
        near_source.append((rest // 8, (block % 8) // 2, rest % 8, block % 2))
    near_index = []
    for sx, sy, sz, sc in near_source:
        sv, sp = device(sx, sy, sz, sc)
        near_index.append(sv * 64 + sp)

    barrier = pltpu.get_barrier_semaphore()
    peers = [("x", d) for d in range(1, NX)] + [("z", d) for d in range(1, NZ)]
    peers += [("y", d) for d in range(1, NY)] + [("core", 1)]
    for t in range(3):
        @pl.when(near_index[t] != mine)
        def _():
            pl.semaphore_signal(barrier, inc=1, device_id=device(*near_source[t]), device_id_type=MESH)
    peers = sorted(peers, key=lambda one: one[0], reverse=True)
    for axis, offset in peers:
        pl.semaphore_signal(barrier, inc=1, device_id=peer(axis, offset), device_id_type=MESH)

    ids = itertools.count()
    started = []

    def send(src, dst, target):
        which = next(ids)
        copy = pltpu.make_async_remote_copy(
            src_ref=src, dst_ref=dst, send_sem=send_sems.at[which], recv_sem=recv_sems.at[which],
            device_id=target, device_id_type=MESH,
        )
        copy.start()
        started.append(copy)
        return copy

    def send_all(triples, all_of_them):
        which = next(ids)
        for src, dst, target in triples:
            copy = pltpu.make_async_remote_copy(
                src_ref=src, dst_ref=dst, send_sem=send_sems.at[which], recv_sem=recv_sems.at[which],
                device_id=target, device_id_type=MESH,
            )
            copy.start()
        whole = pltpu.make_async_remote_copy(
            src_ref=all_of_them, dst_ref=all_of_them, send_sem=send_sems.at[which], recv_sem=recv_sems.at[which],
            device_id=target, device_id_type=MESH,
        )
        started.append(whole)
        return whole

    def take_started():
        taken = list(started)
        started.clear()
        return taken

    def drain(copies):
        for copy in copies:
            copy.wait_send()

    row_loads = []
    for n, (src, dst) in enumerate(((k_hbm, k_ref), (v_hbm, v_ref), (q_hbm, q_ref), (g_hbm, g_ref))):
        load = pltpu.make_async_copy(src, dst, load_sems.at[3 + n])
        load.start()
        row_loads.append(load)
    loads = []
    for m in range(3):
        first = pl.multiple_of(m * HEADS * FF + y * FF, 128)
        load = pltpu.make_async_copy(w_hbm.at[:, pl.ds(first, FF)], w_load.at[m], load_sems.at[m])
        load.start()
        loads.append(load)

    def pack(buffer, left, right):
        for h in range(HEADS):
            cols = slice(HD * h, HD * (h + 1))
            buffer[h, 0:ROWS, 0:HD] = left[:, cols].astype(f32)
            buffer[h, 0:ROWS, HD:2 * HD] = right[:, cols].astype(f32)

    row_loads[0].wait()
    row_loads[1].wait()
    pack(kv_send, k_ref, v_ref)
    for h in range(HEADS):
        kv_send[h, ROWS:ROWS + 8, :] = jnp.zeros((8, 2 * HD), f32)
        kv_send[h, ROWS:ROWS + 8, 0:ROWS] = jnp.broadcast_to(r_ref[h:h + 1, :], (8, ROWS))

    far_count = sum((owner != mine).astype(jnp.int32) for owner in far_owner)
    pl.semaphore_wait(barrier, len(peers) + far_count)

    def scatter_heads(buffer, landing):
        out = {}
        for d in (1, 3, 2):
            out[d] = send(buffer.at[(y + d) % NY], landing.at[d], peer("y", d))
        out["own"] = send(buffer.at[y], landing.at[4], peer("core", 1))
        return out

    kv_copies = scatter_heads(kv_send, kv)
    row_loads[2].wait()
    row_loads[3].wait()
    pack(qg_send, q_ref, g_ref)

    def store_weights(ab_h, ab_l, c_h, c_l, b, m, value):
        if m < 2:
            rows = (b, slice(PAD * m, PAD * m + UNITS))
            ab_h[rows], ab_l[rows] = split(value)
        else:
            rows = (b, slice(0, UNITS))
            c_h[rows], c_l[rows] = split(value)

    for b in range(BLOCKS):
        none = jnp.zeros((PAD - UNITS, HD), bf16)
        for ref in (wh_ab, wl_ab, nh_ab, nl_ab):
            ref[b, UNITS:PAD] = none
            ref[b, PAD + UNITS:2 * PAD] = none
        for ref in (wh_c, wl_c, nh_c, nl_c):
            ref[b, UNITS:PAD] = none
    for m in range(3):
        loads[m].wait()
        both = w_load[m]
        own = jnp.where(core == 0, both[:, 0:HALF], both[:, HALF:FF]).T
        for b in range(BLOCKS):
            pieces = [own[2 * PIECE * n + PIECE * b:2 * PIECE * n + PIECE * (b + 1), :] for n in range(NX)]
            block = jnp.concatenate(pieces, axis=0)
            w_own[b, m] = block
            norms[b, m, 0] = jnp.sqrt(jnp.sum(block * block, axis=1, keepdims=True) + epsilon)
            store_weights(wh_ab, wl_ab, wh_c, wl_c, b, m, block)

    def row_block(s):
        first = (s % 4) * CHUNK + (s // 4) * ROWS
        return slice(first, first + ROWS)

    def unpack_kv(s):
        kb[row_block(s), :] = kv[s, 0:ROWS, 0:HD].astype(bf16)
        vb[row_block(s), :] = kv[s, 0:ROWS, HD:2 * HD].astype(bf16)
        column = kv[s, ROWS:ROWS + 8, 0:ROWS].T[:, 0:1]
        rates[row_block(s), :] = column
        inv_rates[row_block(s), :] = 1.0 / column

    def unpack_qg(s):
        qb[row_block(s), :] = qg[s, 0:ROWS, 0:HD].astype(bf16)
        gb[row_block(s), :] = qg[s, 0:ROWS, HD:2 * HD].astype(bf16)

    def silu_parts(gate):
        sig = 1.0 / (1.0 + jnp.exp(-gate))
        act = gate * sig
        slope = sig + act * (1.0 - sig)
        return sig, act, slope

    def clear(b):
        acc_ab[b] = jnp.zeros((2 * PAD, HD), f32)
        acc_c[b] = jnp.zeros((PAD, HD), f32)

    for b in range(BLOCKS):
        clear(b)

    GATE, UP = slice(0, PAD), slice(PAD, 2 * PAD)

    def add_terms(b, rows, gate_term, up_term, pull_term, left, right, passes=2):
        both = jnp.concatenate([gate_term, up_term], axis=1)
        both_h, both_l = split(both)
        pull_h, pull_l = split(pull_term)
        s_ab_h[b, rows, :], s_c_h[b, rows, :] = both_h, pull_h
        s_ab_l[b, rows, :], s_c_l[b, rows, :] = both_l, pull_l
        both_sum, pull_sum = tn(both_h, left), tn(pull_h, right)
        if passes == 2:
            both_sum, pull_sum = both_sum + tn(both_l, left), pull_sum + tn(pull_l, right)
        acc_ab[b] += both_sum
        acc_c[b] += pull_sum

    def update_chunk(b, i):
        rows = slice(i * CHUNK, (i + 1) * CHUNK)
        keys, values, eta = kb[rows, :], vb[rows, :], rates[rows, :]
        both = nt(keys, wh_ab[b]) + nt(keys, wl_ab[b])
        gate, up = both[:, GATE], both[:, UP]
        pulled = nt(values, wh_c[b]) + nt(values, wl_c[b])
        gate_s[b, rows, :], up_s[b, rows, :], pull_s[b, rows, :] = gate, up, pulled
        _, act, slope = silu_parts(gate)
        scaled = -eta * pulled
        add_terms(b, rows, scaled * up * slope, scaled * act, -eta * act * up, keys, values)

    def take_pair(d):
        unpack_kv(d)
        unpack_kv(4 + d)

    def pass_on(copies, landing, d):
        copies[d].wait_recv()
        return send(landing.at[d], landing.at[4 + d], peer("core", 1))

    with jax.named_scope("keys_own"):
        kv[0] = kv_send[y]
        kv_copies["own"].wait_recv()
        take_pair(0)
        for b in range(BLOCKS):
            update_chunk(b, 0)
    passed = {}
    with jax.named_scope("keys_first"):
        passed[1] = pass_on(kv_copies, kv, 1)
        passed[3] = pass_on(kv_copies, kv, 3)
        passed[1].wait_recv()
        take_pair(1)
        for b in range(BLOCKS):
            update_chunk(b, 1)
    with jax.named_scope("keys_second"):
        passed[2] = pass_on(kv_copies, kv, 2)
        qg_copies = scatter_heads(qg_send, qg)
        passed[3].wait_recv()
        take_pair(3)
        for b in range(BLOCKS):
            update_chunk(b, 3)
    with jax.named_scope("keys_third"):
        passed[2].wait_recv()
        take_pair(2)

    rate_sum = sum(kv[s, ROWS:ROWS + 8, 0:ROWS] for s in range(SLOTS))
    total_part = jnp.sum(rate_sum[0:1, :], axis=1, keepdims=True)

    parts = ((p0_t, p0_r1, p0_s1, p0_r2, p0_s2, p0_a1, p0_f1, p0_g),)

    def lanes_of(first, second, third, tail):
        return (
            first[:, 0:128],
            second[:, 0:128],
            jnp.concatenate([first[:, 128:192], second[:, 128:192]], axis=1),
            third[:, 0:128],
            jnp.concatenate([third[:, 128:192], tail], axis=1),
        )

    def sums_of(b, tail):
        return lanes_of(
            acc_ab[b, 0:UNITS, :], acc_ab[b, PAD:PAD + UNITS, :], acc_c[b, 0:UNITS, :], tail
        )

    def start_stage(r, p, source):
        axis, lane_tiles = PARTS[p]
        first, second, shard, window = part_sizes(PARTS[p])
        t = parts[p][0]
        for jj, j in enumerate(lane_tiles):
            t[r, jj * ROW_TILES:(jj + 1) * ROW_TILES] = source[j].reshape(ROW_TILES, 8, 128)
        r1 = parts[p][1]
        triples = []
        for d in range(1, first):
            there = (place[axis] + d) % first
            triples.append((t.at[r, pl.ds(there * shard, shard)], r1.at[r, d - 1], peer(axis, d)))
        return send_all(triples, r1.at[r])

    def start_of(p, k):
        _, second, shard, window = part_sizes(PARTS[p])
        return ((shard - window) * k) // (second - 1)

    def second_stage(r, p, copies):
        axis = PARTS[p][0]
        other = "z" if axis == "x" else "x"
        first, second, shard, window = part_sizes(PARTS[p])
        t, r1, s1, r2 = parts[p][:4]
        total = t[r, pl.ds(place[axis] * shard, shard)]
        copies.wait_recv()
        for d in range(1, first):
            total = total + r1[r, d - 1]
        s1[r] = total
        triples = []
        for d in range(1, second):
            there = (place[other] + d) % second
            triples.append((s1.at[r, pl.ds(start_of(p, there), window)], r2.at[r, d - 1], peer(other, d)))
        return send_all(triples, r2.at[r])

    def third_stage(r, p, copies):
        other = "z" if PARTS[p][0] == "x" else "x"
        _, second, shard, window = part_sizes(PARTS[p])
        _, _, s1, r2, s2, a1, f1, _ = parts[p]
        total = s1[r, pl.ds(start_of(p, place[other]), window)]
        copies.wait_recv()
        for d in range(1, second):
            total = total + r2[r, d - 1]
        s2[r] = total
        return send_all([(s2.at[r], a1.at[r, d - 1], peer(other, d)) for d in range(1, second)], a1.at[r])

    def fourth_stage(r, p, copies):
        axis = PARTS[p][0]
        other = "z" if axis == "x" else "x"
        first, second, shard, window = part_sizes(PARTS[p])
        _, _, _, _, s2, a1, f1, g = parts[p]
        f1[r, pl.ds(start_of(p, place[other]), window)] = s2[r]
        copies.wait_recv()
        for d in range(1, second):
            there = (place[other] + second - d) % second
            f1[r, pl.ds(start_of(p, there), window)] = a1[r, d - 1]
        here = pl.ds(place[axis] * shard, shard)
        out = send_all([(f1.at[r], g.at[r, here], peer(axis, d)) for d in range(1, first)], parts[p][1].at[r])
        g[r, here] = f1[r]
        return out

    class Sum:
        def __init__(self, r, b):
            self.r = 2 * r + b
            self.b = b

        def start(self, tail):
            source = sums_of(self.b, tail)
            self.copies = [start_stage(self.r, p, source) for p in range(len(PARTS))]

        def step(self, stage):
            self.copies = [stage(self.r, p, self.copies[p]) for p in range(len(PARTS))]

        def result(self):
            for group in self.copies:
                group.wait_recv()
            tiles = {}
            for p in range(len(PARTS)):
                for jj, j in enumerate(PARTS[p][1]):
                    tiles[j] = parts[p][7][self.r, jj * ROW_TILES:(jj + 1) * ROW_TILES].reshape(UNITS, 128)
            gate = jnp.concatenate([tiles[0], tiles[2][:, 0:64]], axis=1)
            up = jnp.concatenate([tiles[1], tiles[2][:, 64:128]], axis=1)
            down = jnp.concatenate([tiles[3], tiles[4][:, 0:64]], axis=1)
            return (gate, up, down), tiles[4][0:1, 64:65]

    def prepare_chunk(i, _):
        rows = pl.ds(pl.multiple_of(i * CHUNK, CHUNK), CHUNK)
        eta = rates[rows, :]
        for b in range(BLOCKS):
            gate, up, pulled = gate_s[b, rows, :], up_s[b, rows, :], pull_s[b, rows, :]
            sig, act, slope = silu_parts(gate)
            curve = sig * (1.0 - sig) * (2.0 + gate * (1.0 - 2.0 * sig))
            scaled = eta * pulled
            by_slope, by_act = eta * (up * slope), eta * act
            m1[b, rows, :], m2[b, rows, :] = scaled * up * curve, scaled * slope
            m3[b, rows, :], m4[b, rows, :] = by_slope, by_act
            e_ab_h[b, rows, GATE], e_ab_l[b, rows, GATE] = split(by_slope * pulled)
            e_ab_h[b, rows, UP], e_ab_l[b, rows, UP] = split(by_act * pulled)
            e_c_h[b, rows, :], e_c_l[b, rows, :] = split(by_act * up)
        return 0

    query_passed = {}

    def prepare():
        lax.fori_loop(0, ALL_ROWS // CHUNK, prepare_chunk, 0)

    def pass_queries():
        qg[0] = qg_send[y]
        for d in (1, 3, 2):
            query_passed[d] = pass_on(qg_copies, qg, d)

    def take_queries():
        qg_copies["own"].wait_recv()
        for d in (1, 3, 2):
            query_passed[d].wait_recv()
        for s in range(SLOTS):
            unpack_qg(s)

    tail = jnp.broadcast_to(total_part, (UNITS, 64))
    sums = [Sum(0, b) for b in range(BLOCKS)]
    for b in range(BLOCKS):
        with jax.named_scope("keys_last"):
            update_chunk(b, 2)
            sums[b].start(tail)
    prepare()
    for stage, work in ((second_stage, pass_queries), (third_stage, take_queries), (fourth_stage, None)):
        for b in range(BLOCKS):
            sums[b].step(stage)
        if work is not None:
            work()

    def new_weights(b):
        terms, total = sums[b].result()
        scale = COEFFICIENT / total
        for m in range(3):
            change = terms[m] * scale
            shifted = w_own[b, m] - change
            inverse = lax.rsqrt(jnp.sum(shifted * shifted, axis=1, keepdims=True) + epsilon)
            gm[b, m], moved[b, m], norms[b, m, 1] = change, shifted, inverse
            store_weights(nh_ab, nl_ab, nh_c, nl_c, b, m, shifted * (norms[b, m, 0] * inverse))
        clear(b)
        return total, scale

    def apply_block(b):
        def apply_chunk(i, _):
            rows = pl.ds(pl.multiple_of(i * CHUNK, CHUNK), CHUNK)
            queries, grads = qb[rows, :], gb[rows, :]
            both = nt(queries, nh_ab[b]) + nt(queries, nl_ab[b])
            gate, up = both[:, GATE], both[:, UP]
            pulled = nt(grads, nh_c[b]) + nt(grads, nl_c[b])
            _, act, slope = silu_parts(gate)
            add_terms(b, rows, pulled * up * slope, pulled * act, act * up, queries, grads)
            return 0

        lax.fori_loop(0, ALL_ROWS // CHUNK, apply_chunk, 0)

    new_sums = [Sum(1, b) for b in range(BLOCKS)]
    early = take_started()
    for b in range(BLOCKS):
        with jax.named_scope("apply"):
            totals, scale = new_weights(b)
            apply_block(b)
            new_sums[b].start(jnp.zeros((UNITS, 64), f32))

    def product(ah, al, bh, bl, rows):
        high = ah[rows, :]
        return nn(high, bh) + nn(high, bl) + nn(al[rows, :], bh)

    def query_grads(b):
        def query_chunk(i, _):
            rows = pl.ds(pl.multiple_of(i * ROWS, ROWS), ROWS)
            slot = (i % 2) * 4 + i // 2
            part = product(s_ab_h.at[b], s_ab_l.at[b], nh_ab[b], nl_ab[b], rows)
            dq[slot] = part if b == 0 else dq[slot] + part
            return 0

        lax.fori_loop(0, SLOTS, query_chunk, 0)

    def return_rows(pair, partial, arrived, sums, landing):
        pair.wait_recv()
        out = []
        for d in (1, 3, 2, 0):
            if d == 0:
                landing[0] = partial[0] + arrived[0]
            else:
                sums[d] = partial[d] + arrived[d]
                out.append(send(sums.at[d], landing.at[d], peer("y", NY - d)))
        return out

    for b in range(BLOCKS):
        with jax.named_scope("query_grads"):
            query_grads(b)
        new_sums[b].step(second_stage)
    query_pair = send(dq.at[pl.ds(4, 4)], xq, peer("core", 1))
    new_sums[0].step(third_stage)
    query_back = return_rows(query_pair, dq, xq, oq, rq)
    drain(early)
    new_sums[1].step(third_stage)
    for b in range(BLOCKS):
        new_sums[b].step(fourth_stage)

    direct = {}

    def pull_weights(b):
        d_new, _ = new_sums[b].result()
        head_part = jnp.zeros((1, 1), f32)
        for m in range(3):
            init_norm, inverse = norms[b, m, 0], norms[b, m, 1]
            shifted = moved[b, m]
            dots = jnp.sum(d_new[m] * shifted, axis=1, keepdims=True)
            d_moved = d_new[m] * (init_norm * inverse) - shifted * (dots * init_norm * inverse * inverse * inverse)
            direct[b, m] = d_moved + w_own[b, m] * (dots * inverse / init_norm)
            by_row = jnp.sum(d_moved * gm[b, m], axis=1, keepdims=True)
            head_part = head_part - jnp.sum(by_row, axis=0, keepdims=True)
            store_weights(nh_ab, nl_ab, nh_c, nl_c, b, m, d_moved * scale)
        clear(b)
        return -head_part / totals

    def pull_block(b):
        def pull_chunk(i, _):
            rows = pl.ds(pl.multiple_of(i * CHUNK, CHUNK), CHUNK)
            keys, values = kb[rows, :], vb[rows, :]
            both = nt(keys, nh_ab[b]) + nt(keys, nl_ab[b])
            one, two = both[:, GATE], both[:, UP]
            three = nt(values, nh_c[b]) + nt(values, nl_c[b])
            by_slope, by_act, by_two = m3[b, rows, :], m4[b, rows, :], m2[b, rows, :]
            c_gate = one * m1[b, rows, :] + two * by_two + three * by_slope
            c_up = one * by_two + three * by_act
            c_pull = one * by_slope + two * by_act
            add_terms(b, rows, c_gate, c_up, c_pull, keys, values, passes=1)
            by_rate = c_pull * pull_s[b, rows, :] + three * (by_act * up_s[b, rows, :])
            by_rate_h, by_rate_l = split(by_rate * inv_rates[rows, :])
            ones = jnp.ones((8, PAD), bf16)
            part = nt(ones, by_rate_h) + nt(ones, by_rate_l)
            rate_rows[i] = part if b == 0 else rate_rows[i] + part
            return 0

        lax.fori_loop(0, ALL_ROWS // CHUNK, pull_chunk, 0)

    early = take_started()
    weight_copies = []
    d_totals = jnp.zeros((1, 1), f32)
    for b in range(BLOCKS):
        with jax.named_scope("pull"):
            d_totals = d_totals + pull_weights(b)
            pull_block(b)
            tiles = sums_of(b, jnp.zeros((UNITS, 64), f32))
            for j in range(5):
                f_t[b, :, 128 * j:128 * (j + 1)] = tiles[j]
            triples = []
            for d in range(1, NX):
                first = pl.multiple_of(((x + d) % NX) * PIECE, PIECE)
                triples.append((f_t.at[b, pl.ds(first, PIECE)], f_r1.at[b, d - 1], peer("x", d)))
            weight_copies.append(send_all(triples, f_r1.at[b]))

    def key_chunk(i, _):
        rows = pl.ds(pl.multiple_of(i * ROWS, ROWS), ROWS)
        slot = (i % 2) * 4 + i // 2
        key_part, value_part = 0.0, 0.0
        for b in range(BLOCKS):
            key_part += product(s_ab_h.at[b], s_ab_l.at[b], wh_ab[b], wl_ab[b], rows)
            key_part += product(e_ab_h.at[b], e_ab_l.at[b], nh_ab[b], nl_ab[b], rows)
            value_part += product(s_c_h.at[b], s_c_l.at[b], wh_c[b], wl_c[b], rows)
            value_part += product(e_c_h.at[b], e_c_l.at[b], nh_c[b], nl_c[b], rows)
        dkv[slot, 0:ROWS, 0:HD] = key_part
        dkv[slot, 0:ROWS, HD:2 * HD] = value_part
        return 0

    with jax.named_scope("row_grads"):
        lax.fori_loop(0, SLOTS, key_chunk, 0)
        for s in range(SLOTS):
            dkv[s, ROWS:ROWS + 8, :] = jnp.zeros((8, 2 * HD), f32)
            lane = (s // 4) * ROWS
            dkv[s, ROWS:ROWS + 8, 0:ROWS] = rate_rows[s % 4, :, lane:lane + ROWS] + d_totals
        pair = send(dkv.at[pl.ds(4, 4)], xkv, peer("core", 1))

    with jax.named_scope("x_sums"):
        for b in range(BLOCKS):
            total = f_t[b, pl.ds(pl.multiple_of(x * PIECE, PIECE), PIECE), :]
            weight_copies[b].wait_recv()
            for d in range(1, NX):
                total = total + f_r1[b, d - 1]
            for n in range(4):
                f_s1[4 * b + n, 0:GROUP, :] = total[GROUP * n:GROUP * (n + 1), :]
                f_s1[4 * b + n, GROUP:8, :] = jnp.zeros((8 - GROUP, 640), f32)
        triples = [(f_s1.at[(z + d) % NZ], f_r2.at[d - 1], peer("z", d)) for d in range(1, NZ)]
        weight_copies = send_all(triples, f_r2)
    with jax.named_scope("row_returns"):
        row_back = return_rows(pair, dkv, xkv, okv, rkv)
    with jax.named_scope("direct"):
        for b in range(BLOCKS):
            tiles = lanes_of(direct[b, 0], direct[b, 1], direct[b, 2], jnp.zeros((UNITS, 64), f32))
            for j in range(5):
                for n in range(16):
                    group = 8 * (n // 4) + 4 * b + n % 4
                    d_grp[group, 0:GROUP, 128 * j:128 * (j + 1)] = tiles[j][GROUP * n:GROUP * (n + 1), :]

    drain(early)
    z_scope = jax.named_scope("z_sums")
    z_scope.__enter__()
    total = f_s1[z]
    weight_copies.wait_recv()
    for d in range(1, NZ):
        total = total + f_r2[d - 1]
    total = (total + d_grp[8 * x + z]) * (1.0 / math.sqrt(TOTAL_ROWS))
    for m, (low, high) in enumerate(((0, 256), (128, 320), (384, 512))):
        f_msg[m, :, 0:128] = total[:, low:low + 128]
        f_msg[m, :, 128:HD] = total[:, high:high + 64]
    far_copies = []
    for m in range(3):
        slot = far_group[m] % 3
        owner = far_owner[m]
        copy = pltpu.make_async_remote_copy(
            src_ref=f_msg.at[m], dst_ref=fg_out.at[slot], send_sem=far_sems.at[0, m], recv_sem=far_sems.at[1, slot],
            device_id=(owner // 64, owner % 64), device_id_type=MESH,
        )

        @pl.when(owner != mine)
        def _():
            copy.start()

        @pl.when(owner == mine)
        def _():
            fg_out[slot] = f_msg[m]

        far_copies.append(copy)

    z_scope.__exit__(None, None, None)

    def rows_out(which, landing, lanes):
        for h in range(HEADS):
            d = (h + NY - y) % NY
            rows_ref[which, :, HD * h:HD * (h + 1)] = landing[d, 0:ROWS, lanes:lanes + HD].astype(bf16)

    with jax.named_scope("query_rows"):
        for copy in query_back:
            copy.wait_recv()
        rows_out(0, rq, 0)
    with jax.named_scope("key_rows"):
        for copy in row_back:
            copy.wait_recv()
        rows_out(1, rkv, 0)
        rows_out(2, rkv, HD)
        for h in range(HEADS):
            rg_out[h:h + 1, :] = rkv[(h + NY - y) % NY, ROWS:ROWS + 1, 0:ROWS]

    with jax.named_scope("columns"):
        for m in range(3):
            @pl.when(near_index[m] != mine)
            def _():
                pltpu.make_async_remote_copy(
                    src_ref=f_msg.at[m], dst_ref=fg_out.at[m], send_sem=far_sems.at[0, m],
                    recv_sem=far_sems.at[1, m], device_id=(view, patch), device_id_type=MESH,
                ).wait_recv()

            @pl.when(far_owner[m] != mine)
            def _():
                far_copies[m].wait_send()
        drain(started)


def finish(rows, rate_rows, groups, query_out, key_out, value_out, rate_out, fast_out, sems):
    copies = [
        pltpu.make_async_copy(rows.at[n], out, sems.at[n]) for n, out in enumerate((query_out, key_out, value_out))
    ]
    for copy in copies:
        copy.start()
    rate_out[...] = rate_rows[...]
    for m in range(3):
        fast_out[GROUP * m:GROUP * (m + 1), :] = groups[m, 0:GROUP, 0:HD]
    for copy in copies:
        copy.wait()


def scratch():
    tile = (8, 128)
    halves = (BLOCKS, ALL_ROWS)
    shapes = [
        *[pltpu.VMEM((ROWS, HEADS * HD), bf16)] * 4,
        pltpu.VMEM((3, HD, FF), f32),
        pltpu.VMEM((BLOCKS, 3, UNITS, HD), f32),
        *[pltpu.VMEM((BLOCKS, 2 * PAD, HD), bf16)] * 4,
        *[pltpu.VMEM((BLOCKS, PAD, HD), bf16)] * 4,
        *[pltpu.VMEM((BLOCKS, 3, UNITS, HD), f32)] * 2,
        pltpu.VMEM((BLOCKS, 3, 2, UNITS, 1), f32),
        *[pltpu.VMEM((HEADS, ROWS + 8, 2 * HD), f32)] * 2,
        *[pltpu.VMEM((SLOTS, ROWS + 8, 2 * HD), f32)] * 2,
        *[pltpu.VMEM((ALL_ROWS, 1), f32)] * 2,
        *[pltpu.VMEM((ALL_ROWS, HD), bf16)] * 4,
        *[pltpu.VMEM(halves + (PAD,), f32)] * 7,
        *[pltpu.VMEM(halves + (2 * PAD,), bf16)] * 4,
        *[pltpu.VMEM(halves + (PAD,), bf16)] * 4,
        pltpu.VMEM((BLOCKS, 2 * PAD, HD), f32),
        pltpu.VMEM((BLOCKS, PAD, HD), f32),
        pltpu.VMEM((ALL_ROWS // CHUNK, 8, CHUNK), f32),
        pltpu.VMEM((SLOTS, ROWS, HD), f32),
        *[pltpu.VMEM((4, ROWS, HD), f32)] * 3,
        pltpu.VMEM((SLOTS, ROWS + 8, 2 * HD), f32),
        *[pltpu.VMEM((4, ROWS + 8, 2 * HD), f32)] * 3,
    ]
    rounds = 2 * BLOCKS
    for part in PARTS:
        first, second, shard, window = part_sizes(part)
        shapes += [
            pltpu.VMEM((rounds, first * shard) + tile, f32),
            pltpu.VMEM((rounds, first - 1, shard) + tile, f32),
            pltpu.VMEM((rounds, shard) + tile, f32),
            pltpu.VMEM((rounds, second - 1, window) + tile, f32),
            pltpu.VMEM((rounds, window) + tile, f32),
            pltpu.VMEM((rounds, second - 1, window) + tile, f32),
            pltpu.VMEM((rounds, shard) + tile, f32),
            pltpu.VMEM((rounds, first * shard) + tile, f32),
        ]
    shapes += [
        pltpu.VMEM((BLOCKS, UNITS, 640), f32),
        pltpu.VMEM((BLOCKS, NX - 1, PIECE, 640), f32),
        pltpu.VMEM((NZ, 8, 640), f32),
        pltpu.VMEM((NZ - 1, 8, 640), f32),
        pltpu.VMEM((HALF // GROUP, 8, 640), f32),
        pltpu.VMEM((3, 8, 256), f32),
        pltpu.SemaphoreType.DMA((N_SEMS,)),
        pltpu.SemaphoreType.DMA((N_SEMS,)),
        pltpu.SemaphoreType.DMA((2, 3)),
        pltpu.SemaphoreType.DMA((7,)),
    ]
    return shapes


def on_device(queries, key_rows, value_rows, step_rates, fast_init, out_grad):
    vmem = pl.BlockSpec(memory_space=pltpu.VMEM)
    anywhere = pl.BlockSpec(memory_space=pl.ANY)
    rates_shape = jax.ShapeDtypeStruct((HEADS, ROWS), f32)
    results = pl.pallas_call(
        kernel,
        out_shape=(
            jax.ShapeDtypeStruct((3, ROWS, HEADS * HD), bf16),
            rates_shape,
            jax.ShapeDtypeStruct((3, 8, 256), f32),
        ),
        in_specs=[anywhere] * 3 + [vmem] + [anywhere] * 2,
        out_specs=(vmem,) * 3,
        scratch_shapes=scratch(),
        compiler_params=pltpu.CompilerParams(
            collective_id=0, has_side_effects=True, vmem_limit_bytes=56 * 2**20
        ),
        name="layer_grad",
    )(queries, key_rows, value_rows, step_rates.T, out_grad, fast_init)
    rows = jax.ShapeDtypeStruct((ROWS, HEADS * HD), bf16)
    query_grad, key_grad, value_grad, rate_grad, fast_grad = pl.pallas_call(
        finish,
        out_shape=(rows, rows, rows, rates_shape, jax.ShapeDtypeStruct((3 * GROUP, HD), f32)),
        in_specs=[vmem] * 3,
        out_specs=(anywhere,) * 3 + (vmem,) * 2,
        scratch_shapes=[pltpu.SemaphoreType.DMA((3,))],
        name="outputs",
    )(*results)
    return query_grad, key_grad, value_grad, rate_grad.T, fast_grad.T


def solution(mesh):
    both = ("view", "patch")
    return jax.shard_map(
        on_device,
        mesh=mesh,
        in_specs=(P(both, None), P(both, None), P(both, None), P(both, None), P(), P(both, None)),
        out_specs=(P(both, None), P(both, None), P(both, None), P(both, None), P(None, both)),
        check_vma=False,
    )
```

```python
import itertools
import math

import jax
import jax.numpy as jnp
from jax import lax
from jax.experimental import pallas as pl
from jax.experimental.pallas import tpu as pltpu
from jax.sharding import PartitionSpec as P

MESH = pl.DeviceIdType.MESH
f32, bf16 = jnp.float32, jnp.bfloat16

step_size = 0.2
epsilon = 1e-06

NX, NY, NZ = 4, 4, 8
HEADS, HD, FF = 4, 192, 384
HALF = FF // 2
ROWS = 128
SLOTS = 8
ALL_ROWS = SLOTS * ROWS
CHUNK = 256
WIDE = 512
TOTAL_ROWS = ROWS * NX * NY * NZ * 2
COEFFICIENT = step_size * math.sqrt(TOTAL_ROWS)
N_SEMS = 64
GROUP = 6


def device(x, y, z, core):
    return (lax.div(x, 2) * 2 + core, (y * 2 + lax.rem(x, 2)) * 8 + z)


BLOCKS = 2
UNITS = HALF // BLOCKS
PAD = 128
ROW_TILES = UNITS // 8
PIECE = UNITS // NX

PARTS = (("x", (0, 1, 2, 3, 4)),)


def part_sizes(part):
    axis, lane_tiles = part
    first, second = (NX, NZ) if axis == "x" else (NZ, NX)
    shard = ROW_TILES * len(lane_tiles) // first
    window = -(-shard // second)
    if (shard - window) // (second - 1) >= window and shard > second:
        window += 1
    return first, second, shard, window


def nt(a, b):
    return lax.dot_general(a, b, (((1,), (1,)), ((), ())), preferred_element_type=f32)


def nn(a, b):
    return lax.dot_general(a, b, (((1,), (0,)), ((), ())), preferred_element_type=f32)


def tn(a, b):
    return lax.dot_general(a, b, (((0,), (0,)), ((), ())), preferred_element_type=f32)


def split(value):
    high = value.astype(bf16)
    return high, (value - high.astype(f32)).astype(bf16)


def kernel(
    q_hbm, k_hbm, v_hbm, r_hbm, g_hbm, w_hbm,
    rows_ref, rg_out, fg_out,
    q_ref, k_ref, v_ref, g_ref, r_ref,
    w_load, w_own, wh_ab, wl_ab, nh_ab, nl_ab, wh_c, wl_c, nh_c, nl_c, moved, gm, norms,
    kv_send, qg_send, kv, qg, rates, inv_rates, kb, vb, qb, gb,
    gate_s, up_s, pull_s, m1, m2, m3, m4,
    s_ab_h, s_ab_l, e_ab_h, e_ab_l, s_c_h, s_c_l, e_c_h, e_c_l,
    acc_ab, acc_c, rate_rows, dq, xq, oq, rq, dkv, xkv, okv, rkv,
    p0_t, p0_r1, p0_s1, p0_r2, p0_s2, p0_a1, p0_f1, p0_g,
    f_t, f_r1, f_s1, f_r2, d_grp, f_msg,
    send_sems, recv_sems, far_sems, load_sems,
):
    view, patch = lax.axis_index("view"), lax.axis_index("patch")
    x, core = (view // 2) * 2 + (patch // 8) % 2, view % 2
    y, z = patch // 16, patch % 8
    mine = view * 64 + patch
    half_block = 2 * y + core

    known = {}

    def peer(axis, offset):
        if (axis, offset) not in known:
            if axis == "x":
                target = device(lax.rem(x + offset, NX), y, z, core)
            elif axis == "y":
                target = device(x, lax.rem(y + offset, NY), z, core)
            elif axis == "z":
                target = device(x, y, lax.rem(z + offset, NZ), core)
            else:
                target = device(x, y, z, 1 - core)
            known[axis, offset] = target
        return known[axis, offset]

    place = {"x": x, "z": z}

    far_group = [32 * (8 * m + half_block) + 8 * x + z for m in range(3)]
    far_owner = [group // 3 for group in far_group]
    near_source = []
    for t in range(3):
        group = 3 * mine + t
        block, rest = group // 32, group % 32
        near_source.append((rest // 8, (block % 8) // 2, rest % 8, block % 2))
    near_index = []
    for sx, sy, sz, sc in near_source:
        sv, sp = device(sx, sy, sz, sc)
        near_index.append(sv * 64 + sp)

    barrier = pltpu.get_barrier_semaphore()
    peers = [("x", d) for d in range(1, NX)] + [("z", d) for d in range(1, NZ)]
    peers += [("y", d) for d in range(1, NY)] + [("core", 1)]
    for t in range(3):
        @pl.when(near_index[t] != mine)
        def _():
            pl.semaphore_signal(barrier, inc=1, device_id=device(*near_source[t]), device_id_type=MESH)
    peers = sorted(peers, key=lambda one: one[0], reverse=True)
    for axis, offset in peers:
        pl.semaphore_signal(barrier, inc=1, device_id=peer(axis, offset), device_id_type=MESH)

    ids = itertools.count()
    started = []

    def send(src, dst, target):
        which = next(ids)
        copy = pltpu.make_async_remote_copy(
            src_ref=src, dst_ref=dst, send_sem=send_sems.at[which], recv_sem=recv_sems.at[which],
            device_id=target, device_id_type=MESH,
        )
        copy.start()
        started.append(copy)
        return copy

    def send_all(triples, all_of_them):
        which = next(ids)
        for src, dst, target in triples:
            copy = pltpu.make_async_remote_copy(
                src_ref=src, dst_ref=dst, send_sem=send_sems.at[which], recv_sem=recv_sems.at[which],
                device_id=target, device_id_type=MESH,
            )
            copy.start()
        whole = pltpu.make_async_remote_copy(
            src_ref=all_of_them, dst_ref=all_of_them, send_sem=send_sems.at[which], recv_sem=recv_sems.at[which],
            device_id=target, device_id_type=MESH,
        )
        started.append(whole)
        return whole

    def take_started():
        taken = list(started)
        started.clear()
        return taken

    def drain(copies):
        for copy in copies:
            copy.wait_send()

    row_loads = []
    for n, (src, dst) in enumerate(((k_hbm, k_ref), (v_hbm, v_ref), (r_hbm, r_ref), (q_hbm, q_ref), (g_hbm, g_ref))):
        load = pltpu.make_async_copy(src, dst, load_sems.at[3 + n])
        load.start()
        row_loads.append(load)
    loads = []
    for m in range(3):
        first = pl.multiple_of(m * HEADS * FF + y * FF, 128)
        load = pltpu.make_async_copy(w_hbm.at[:, pl.ds(first, FF)], w_load.at[m], load_sems.at[m])
        load.start()
        loads.append(load)

    def pack(buffer, left, right):
        for h in range(HEADS):
            cols = slice(HD * h, HD * (h + 1))
            buffer[h, 0:ROWS, 0:HD] = left[:, cols].astype(f32)
            buffer[h, 0:ROWS, HD:2 * HD] = right[:, cols].astype(f32)

    for load in row_loads[:3]:
        load.wait()
    pack(kv_send, k_ref, v_ref)
    for h in range(HEADS):
        kv_send[h, ROWS:ROWS + 8, :] = jnp.zeros((8, 2 * HD), f32)
        kv_send[h, ROWS:ROWS + 8, 0:ROWS] = jnp.broadcast_to(r_ref[h:h + 1, :], (8, ROWS))

    far_count = sum((owner != mine).astype(jnp.int32) for owner in far_owner)
    pl.semaphore_wait(barrier, len(peers) + far_count)

    def scatter_heads(buffer, landing):
        out = {}
        for d in (1, 3, 2):
            out[d] = send(buffer.at[(y + d) % NY], landing.at[d], peer("y", d))
        out["own"] = send(buffer.at[y], landing.at[4], peer("core", 1))
        return out

    kv_copies = scatter_heads(kv_send, kv)
    for load in row_loads[3:]:
        load.wait()
    pack(qg_send, q_ref, g_ref)

    def store_weights(ab_h, ab_l, c_h, c_l, b, m, value):
        if m < 2:
            rows = (b, slice(PAD * m, PAD * m + UNITS))
            ab_h[rows], ab_l[rows] = split(value)
        else:
            rows = (b, slice(0, UNITS))
            c_h[rows], c_l[rows] = split(value)

    for b in range(BLOCKS):
        none = jnp.zeros((PAD - UNITS, HD), bf16)
        for ref in (wh_ab, wl_ab, nh_ab, nl_ab):
            ref[b, UNITS:PAD] = none
            ref[b, PAD + UNITS:2 * PAD] = none
        for ref in (wh_c, wl_c, nh_c, nl_c):
            ref[b, UNITS:PAD] = none
    for m in range(3):
        loads[m].wait()
        both = w_load[m]
        own = jnp.where(core == 0, both[:, 0:HALF], both[:, HALF:FF]).T
        for b in range(BLOCKS):
            pieces = [own[2 * PIECE * n + PIECE * b:2 * PIECE * n + PIECE * (b + 1), :] for n in range(NX)]
            block = jnp.concatenate(pieces, axis=0)
            w_own[b, m] = block
            norms[b, m, 0] = jnp.sqrt(jnp.sum(block * block, axis=1, keepdims=True) + epsilon)
            store_weights(wh_ab, wl_ab, wh_c, wl_c, b, m, block)

    def row_block(s):
        first = (s % 4) * CHUNK + (s // 4) * ROWS
        return slice(first, first + ROWS)

    def unpack_kv(s):
        kb[row_block(s), :] = kv[s, 0:ROWS, 0:HD].astype(bf16)
        vb[row_block(s), :] = kv[s, 0:ROWS, HD:2 * HD].astype(bf16)
        column = kv[s, ROWS:ROWS + 8, 0:ROWS].T[:, 0:1]
        rates[row_block(s), :] = column
        inv_rates[row_block(s), :] = 1.0 / column

    def unpack_qg(s):
        qb[row_block(s), :] = qg[s, 0:ROWS, 0:HD].astype(bf16)
        gb[row_block(s), :] = qg[s, 0:ROWS, HD:2 * HD].astype(bf16)

    def silu_parts(gate):
        sig = 1.0 / (1.0 + jnp.exp(-gate))
        act = gate * sig
        slope = sig + act * (1.0 - sig)
        return sig, act, slope

    def clear(b):
        acc_ab[b] = jnp.zeros((2 * PAD, HD), f32)
        acc_c[b] = jnp.zeros((PAD, HD), f32)

    for b in range(BLOCKS):
        clear(b)

    GATE, UP = slice(0, PAD), slice(PAD, 2 * PAD)

    def add_terms(b, rows, gate_term, up_term, pull_term, left, right):
        both = jnp.concatenate([gate_term, up_term], axis=1)
        both_h, both_l = split(both)
        pull_h, pull_l = split(pull_term)
        s_ab_h[b, rows, :], s_c_h[b, rows, :] = both_h, pull_h
        s_ab_l[b, rows, :], s_c_l[b, rows, :] = both_l, pull_l
        acc_ab[b] += tn(both_h, left) + tn(both_l, left)
        acc_c[b] += tn(pull_h, right) + tn(pull_l, right)

    def update_chunk(b, i):
        rows = slice(i * CHUNK, (i + 1) * CHUNK)
        keys, values, eta = kb[rows, :], vb[rows, :], rates[rows, :]
        both = nt(keys, wh_ab[b]) + nt(keys, wl_ab[b])
        gate, up = both[:, GATE], both[:, UP]
        pulled = nt(values, wh_c[b]) + nt(values, wl_c[b])
        gate_s[b, rows, :], up_s[b, rows, :], pull_s[b, rows, :] = gate, up, pulled
        _, act, slope = silu_parts(gate)
        scaled = -eta * pulled
        add_terms(b, rows, scaled * up * slope, scaled * act, -eta * act * up, keys, values)

    def take_pair(d):
        unpack_kv(d)
        unpack_kv(4 + d)

    def pass_on(copies, landing, d):
        copies[d].wait_recv()
        return send(landing.at[d], landing.at[4 + d], peer("core", 1))

    with jax.named_scope("keys_own"):
        kv[0] = kv_send[y]
        kv_copies["own"].wait_recv()
        take_pair(0)
        for b in range(BLOCKS):
            update_chunk(b, 0)
    passed = {}
    with jax.named_scope("keys_first"):
        passed[1] = pass_on(kv_copies, kv, 1)
        passed[3] = pass_on(kv_copies, kv, 3)
        passed[1].wait_recv()
        take_pair(1)
        for b in range(BLOCKS):
            update_chunk(b, 1)
    with jax.named_scope("keys_second"):
        passed[2] = pass_on(kv_copies, kv, 2)
        qg_copies = scatter_heads(qg_send, qg)
        passed[3].wait_recv()
        take_pair(3)
        for b in range(BLOCKS):
            update_chunk(b, 3)
    with jax.named_scope("keys_third"):
        passed[2].wait_recv()
        take_pair(2)

    rate_sum = sum(kv[s, ROWS:ROWS + 8, 0:ROWS] for s in range(SLOTS))
    total_part = jnp.sum(rate_sum[0:1, :], axis=1, keepdims=True)

    parts = ((p0_t, p0_r1, p0_s1, p0_r2, p0_s2, p0_a1, p0_f1, p0_g),)

    def lanes_of(first, second, third, tail):
        return (
            first[:, 0:128],
            second[:, 0:128],
            jnp.concatenate([first[:, 128:192], second[:, 128:192]], axis=1),
            third[:, 0:128],
            jnp.concatenate([third[:, 128:192], tail], axis=1),
        )

    def sums_of(b, tail):
        return lanes_of(
            acc_ab[b, 0:UNITS, :], acc_ab[b, PAD:PAD + UNITS, :], acc_c[b, 0:UNITS, :], tail
        )

    def start_stage(r, p, source):
        axis, lane_tiles = PARTS[p]
        first, second, shard, window = part_sizes(PARTS[p])
        t = parts[p][0]
        for jj, j in enumerate(lane_tiles):
            t[r, jj * ROW_TILES:(jj + 1) * ROW_TILES] = source[j].reshape(ROW_TILES, 8, 128)
        r1 = parts[p][1]
        triples = []
        for d in range(1, first):
            there = lax.rem(place[axis] + d, first)
            triples.append((t.at[r, pl.ds(there * shard, shard)], r1.at[r, d - 1], peer(axis, d)))
        return send_all(triples, r1.at[r])

    def start_of(p, k):
        _, second, shard, window = part_sizes(PARTS[p])
        return lax.div((shard - window) * k, second - 1)

    def second_stage(r, p, copies):
        axis = PARTS[p][0]
        other = "z" if axis == "x" else "x"
        first, second, shard, window = part_sizes(PARTS[p])
        t, r1, s1, r2 = parts[p][:4]
        total = t[r, pl.ds(place[axis] * shard, shard)]
        copies.wait_recv()
        for d in range(1, first):
            total = total + r1[r, d - 1]
        s1[r] = total
        triples = []
        for d in range(1, second):
            there = lax.rem(place[other] + d, second)
            triples.append((s1.at[r, pl.ds(start_of(p, there), window)], r2.at[r, d - 1], peer(other, d)))
        return send_all(triples, r2.at[r])

    def third_stage(r, p, copies):
        other = "z" if PARTS[p][0] == "x" else "x"
        _, second, shard, window = part_sizes(PARTS[p])
        _, _, s1, r2, s2, a1, f1, _ = parts[p]
        total = s1[r, pl.ds(start_of(p, place[other]), window)]
        copies.wait_recv()
        for d in range(1, second):
            total = total + r2[r, d - 1]
        s2[r] = total
        return send_all([(s2.at[r], a1.at[r, d - 1], peer(other, d)) for d in range(1, second)], a1.at[r])

    def fourth_stage(r, p, copies):
        axis = PARTS[p][0]
        other = "z" if axis == "x" else "x"
        first, second, shard, window = part_sizes(PARTS[p])
        _, _, _, _, s2, a1, f1, g = parts[p]
        f1[r, pl.ds(start_of(p, place[other]), window)] = s2[r]
        copies.wait_recv()
        for d in range(1, second):
            there = lax.rem(place[other] + second - d, second)
            f1[r, pl.ds(start_of(p, there), window)] = a1[r, d - 1]
        here = pl.ds(place[axis] * shard, shard)
        out = send_all([(f1.at[r], g.at[r, here], peer(axis, d)) for d in range(1, first)], parts[p][1].at[r])
        g[r, here] = f1[r]
        return out

    class Sum:
        def __init__(self, r, b):
            self.r = 2 * r + b
            self.b = b

        def start(self, tail):
            source = sums_of(self.b, tail)
            self.copies = [start_stage(self.r, p, source) for p in range(len(PARTS))]

        def step(self, stage):
            self.copies = [stage(self.r, p, self.copies[p]) for p in range(len(PARTS))]

        def result(self):
            for group in self.copies:
                group.wait_recv()
            tiles = {}
            for p in range(len(PARTS)):
                for jj, j in enumerate(PARTS[p][1]):
                    tiles[j] = parts[p][7][self.r, jj * ROW_TILES:(jj + 1) * ROW_TILES].reshape(UNITS, 128)
            gate = jnp.concatenate([tiles[0], tiles[2][:, 0:64]], axis=1)
            up = jnp.concatenate([tiles[1], tiles[2][:, 64:128]], axis=1)
            down = jnp.concatenate([tiles[3], tiles[4][:, 0:64]], axis=1)
            return (gate, up, down), tiles[4][0:1, 64:65]

    def prepare_chunk(i, _):
        rows = pl.ds(pl.multiple_of(i * CHUNK, CHUNK), CHUNK)
        eta = rates[rows, :]
        for b in range(BLOCKS):
            gate, up, pulled = gate_s[b, rows, :], up_s[b, rows, :], pull_s[b, rows, :]
            sig, act, slope = silu_parts(gate)
            curve = sig * (1.0 - sig) * (2.0 + gate * (1.0 - 2.0 * sig))
            scaled = eta * pulled
            by_slope, by_act = eta * (up * slope), eta * act
            m1[b, rows, :], m2[b, rows, :] = scaled * up * curve, scaled * slope
            m3[b, rows, :], m4[b, rows, :] = by_slope, by_act
            e_ab_h[b, rows, GATE], e_ab_l[b, rows, GATE] = split(by_slope * pulled)
            e_ab_h[b, rows, UP], e_ab_l[b, rows, UP] = split(by_act * pulled)
            e_c_h[b, rows, :], e_c_l[b, rows, :] = split(by_act * up)
        return 0

    query_passed = {}

    def prepare():
        lax.fori_loop(0, ALL_ROWS // CHUNK, prepare_chunk, 0)

    def pass_queries():
        qg[0] = qg_send[y]
        for d in (1, 3, 2):
            query_passed[d] = pass_on(qg_copies, qg, d)

    def take_queries():
        qg_copies["own"].wait_recv()
        for d in (1, 3, 2):
            query_passed[d].wait_recv()
        for s in range(SLOTS):
            unpack_qg(s)

    tail = jnp.broadcast_to(total_part, (UNITS, 64))
    sums = [Sum(0, b) for b in range(BLOCKS)]
    for b in range(BLOCKS):
        with jax.named_scope("keys_last"):
            update_chunk(b, 2)
            sums[b].start(tail)
    prepare()
    for stage, work in ((second_stage, pass_queries), (third_stage, take_queries), (fourth_stage, None)):
        for b in range(BLOCKS):
            sums[b].step(stage)
        if work is not None:
            work()

    def new_weights(b):
        terms, total = sums[b].result()
        scale = COEFFICIENT / total
        for m in range(3):
            change = terms[m] * scale
            shifted = w_own[b, m] - change
            inverse = lax.rsqrt(jnp.sum(shifted * shifted, axis=1, keepdims=True) + epsilon)
            gm[b, m], moved[b, m], norms[b, m, 1] = change, shifted, inverse
            store_weights(nh_ab, nl_ab, nh_c, nl_c, b, m, shifted * (norms[b, m, 0] * inverse))
        clear(b)
        return total, scale

    def apply_block(b):
        def apply_chunk(i, _):
            rows = pl.ds(pl.multiple_of(i * WIDE, WIDE), WIDE)
            queries, grads = qb[rows, :], gb[rows, :]
            both = nt(queries, nh_ab[b]) + nt(queries, nl_ab[b])
            gate, up = both[:, GATE], both[:, UP]
            pulled = nt(grads, nh_c[b]) + nt(grads, nl_c[b])
            _, act, slope = silu_parts(gate)
            add_terms(b, rows, pulled * up * slope, pulled * act, act * up, queries, grads)
            return 0

        lax.fori_loop(0, ALL_ROWS // WIDE, apply_chunk, 0)

    new_sums = [Sum(1, b) for b in range(BLOCKS)]
    early = take_started()
    for b in range(BLOCKS):
        with jax.named_scope("apply"):
            totals, scale = new_weights(b)
            apply_block(b)
            new_sums[b].start(jnp.zeros((UNITS, 64), f32))

    def product(ah, al, bh, bl, rows):
        high = ah[rows, :]
        return nn(high, bh) + nn(high, bl) + nn(al[rows, :], bh)

    def query_grads(b):
        def query_chunk(i, _):
            rows = pl.ds(pl.multiple_of(i * CHUNK, CHUNK), CHUNK)
            part = product(s_ab_h.at[b], s_ab_l.at[b], nh_ab[b], nl_ab[b], rows)
            dq[i] = part[0:ROWS] if b == 0 else dq[i] + part[0:ROWS]
            dq[4 + i] = part[ROWS:CHUNK] if b == 0 else dq[4 + i] + part[ROWS:CHUNK]
            return 0

        lax.fori_loop(0, 4, query_chunk, 0)

    def return_rows(pair, partial, arrived, sums, landing):
        pair.wait_recv()
        out = []
        for d in (1, 3, 2, 0):
            if d == 0:
                landing[0] = partial[0] + arrived[0]
            else:
                sums[d] = partial[d] + arrived[d]
                out.append(send(sums.at[d], landing.at[d], peer("y", NY - d)))
        return out

    for b in range(BLOCKS):
        with jax.named_scope("query_grads"):
            query_grads(b)
        new_sums[b].step(second_stage)
    query_pair = send(dq.at[pl.ds(4, 4)], xq, peer("core", 1))
    new_sums[0].step(third_stage)
    query_back = return_rows(query_pair, dq, xq, oq, rq)
    drain(early)
    new_sums[1].step(third_stage)
    for b in range(BLOCKS):
        new_sums[b].step(fourth_stage)

    direct = {}

    def pull_weights(b):
        d_new, _ = new_sums[b].result()
        head_part = jnp.zeros((1, 1), f32)
        for m in range(3):
            init_norm, inverse = norms[b, m, 0], norms[b, m, 1]
            shifted = moved[b, m]
            dots = jnp.sum(d_new[m] * shifted, axis=1, keepdims=True)
            d_moved = d_new[m] * (init_norm * inverse) - shifted * (dots * init_norm * inverse * inverse * inverse)
            direct[b, m] = d_moved + w_own[b, m] * (dots * inverse / init_norm)
            by_row = jnp.sum(d_moved * gm[b, m], axis=1, keepdims=True)
            head_part = head_part - jnp.sum(by_row, axis=0, keepdims=True)
            store_weights(nh_ab, nl_ab, nh_c, nl_c, b, m, d_moved * scale)
        clear(b)
        return -head_part / totals

    def pull_block(b):
        def pull_chunk(i, _):
            rows = pl.ds(pl.multiple_of(i * WIDE, WIDE), WIDE)
            keys, values = kb[rows, :], vb[rows, :]
            both = nt(keys, nh_ab[b]) + nt(keys, nl_ab[b])
            one, two = both[:, GATE], both[:, UP]
            three = nt(values, nh_c[b]) + nt(values, nl_c[b])
            by_slope, by_act, by_two = m3[b, rows, :], m4[b, rows, :], m2[b, rows, :]
            c_gate = one * m1[b, rows, :] + two * by_two + three * by_slope
            c_up = one * by_two + three * by_act
            c_pull = one * by_slope + two * by_act
            add_terms(b, rows, c_gate, c_up, c_pull, keys, values)
            by_rate = c_pull * pull_s[b, rows, :] + three * (by_act * up_s[b, rows, :])
            by_rate_h, by_rate_l = split(by_rate * inv_rates[rows, :])
            ones = jnp.ones((8, PAD), bf16)
            part = nt(ones, by_rate_h) + nt(ones, by_rate_l)
            rate_rows[i] = part if b == 0 else rate_rows[i] + part
            return 0

        lax.fori_loop(0, ALL_ROWS // WIDE, pull_chunk, 0)

    early = take_started()
    weight_copies = []
    d_totals = jnp.zeros((1, 1), f32)
    for b in range(BLOCKS):
        with jax.named_scope("pull"):
            d_totals = d_totals + pull_weights(b)
            pull_block(b)
            tiles = sums_of(b, jnp.zeros((UNITS, 64), f32))
            for j in range(5):
                f_t[b, :, 128 * j:128 * (j + 1)] = tiles[j]
            triples = []
            for d in range(1, NX):
                first = pl.multiple_of(((x + d) % NX) * PIECE, PIECE)
                triples.append((f_t.at[b, pl.ds(first, PIECE)], f_r1.at[b, d - 1], peer("x", d)))
            weight_copies.append(send_all(triples, f_r1.at[b]))

    def key_chunk(i, _):
        rows = pl.ds(pl.multiple_of(i * CHUNK, CHUNK), CHUNK)
        key_part, value_part = 0.0, 0.0
        for b in range(BLOCKS):
            key_part += product(s_ab_h.at[b], s_ab_l.at[b], wh_ab[b], wl_ab[b], rows)
            key_part += product(e_ab_h.at[b], e_ab_l.at[b], nh_ab[b], nl_ab[b], rows)
            value_part += product(s_c_h.at[b], s_c_l.at[b], wh_c[b], wl_c[b], rows)
            value_part += product(e_c_h.at[b], e_c_l.at[b], nh_c[b], nl_c[b], rows)
        for slot, first in ((i, 0), (4 + i, ROWS)):
            dkv[slot, 0:ROWS, 0:HD] = key_part[first:first + ROWS]
            dkv[slot, 0:ROWS, HD:2 * HD] = value_part[first:first + ROWS]
        return 0

    with jax.named_scope("row_grads"):
        lax.fori_loop(0, 4, key_chunk, 0)
        for s in range(SLOTS):
            dkv[s, ROWS:ROWS + 8, :] = jnp.zeros((8, 2 * HD), f32)
            first = row_block(s).start
            lane = first % WIDE
            dkv[s, ROWS:ROWS + 8, 0:ROWS] = rate_rows[first // WIDE, :, lane:lane + ROWS] + d_totals
        pair = send(dkv.at[pl.ds(4, 4)], xkv, peer("core", 1))

    with jax.named_scope("x_sums"):
        for b in range(BLOCKS):
            total = f_t[b, pl.ds(pl.multiple_of(x * PIECE, PIECE), PIECE), :]
            weight_copies[b].wait_recv()
            for d in range(1, NX):
                total = total + f_r1[b, d - 1]
            for n in range(4):
                f_s1[4 * b + n, 0:GROUP, :] = total[GROUP * n:GROUP * (n + 1), :]
                f_s1[4 * b + n, GROUP:8, :] = jnp.zeros((8 - GROUP, 640), f32)
        triples = [(f_s1.at[(z + d) % NZ], f_r2.at[d - 1], peer("z", d)) for d in range(1, NZ)]
        weight_copies = send_all(triples, f_r2)
    with jax.named_scope("row_returns"):
        row_back = return_rows(pair, dkv, xkv, okv, rkv)
    with jax.named_scope("direct"):
        for b in range(BLOCKS):
            tiles = lanes_of(direct[b, 0], direct[b, 1], direct[b, 2], jnp.zeros((UNITS, 64), f32))
            for j in range(5):
                for n in range(16):
                    group = 8 * (n // 4) + 4 * b + n % 4
                    d_grp[group, 0:GROUP, 128 * j:128 * (j + 1)] = tiles[j][GROUP * n:GROUP * (n + 1), :]

    drain(early)
    z_scope = jax.named_scope("z_sums")
    z_scope.__enter__()
    total = f_s1[z]
    weight_copies.wait_recv()
    for d in range(1, NZ):
        total = total + f_r2[d - 1]
    total = (total + d_grp[8 * x + z]) * (1.0 / math.sqrt(TOTAL_ROWS))
    for m, (low, high) in enumerate(((0, 256), (128, 320), (384, 512))):
        f_msg[m, :, 0:128] = total[:, low:low + 128]
        f_msg[m, :, 128:HD] = total[:, high:high + 64]
    far_copies = []
    for m in range(3):
        slot = far_group[m] % 3
        owner = far_owner[m]
        copy = pltpu.make_async_remote_copy(
            src_ref=f_msg.at[m], dst_ref=fg_out.at[slot], send_sem=far_sems.at[0, m], recv_sem=far_sems.at[1, slot],
            device_id=(owner // 64, owner % 64), device_id_type=MESH,
        )

        @pl.when(owner != mine)
        def _():
            copy.start()

        @pl.when(owner == mine)
        def _():
            fg_out[slot] = f_msg[m]

        far_copies.append(copy)

    z_scope.__exit__(None, None, None)

    def rows_out(which, landing, lanes):
        for h in range(HEADS):
            d = (h + NY - y) % NY
            rows_ref[which, :, HD * h:HD * (h + 1)] = landing[d, 0:ROWS, lanes:lanes + HD].astype(bf16)

    with jax.named_scope("query_rows"):
        for copy in query_back:
            copy.wait_recv()
        rows_out(0, rq, 0)
    with jax.named_scope("key_rows"):
        for copy in row_back:
            copy.wait_recv()
        rows_out(1, rkv, 0)
        rows_out(2, rkv, HD)
        for h in range(HEADS):
            rg_out[h:h + 1, :] = rkv[(h + NY - y) % NY, ROWS:ROWS + 1, 0:ROWS]

    with jax.named_scope("columns"):
        for m in range(3):
            @pl.when(near_index[m] != mine)
            def _():
                pltpu.make_async_remote_copy(
                    src_ref=f_msg.at[m], dst_ref=fg_out.at[m], send_sem=far_sems.at[0, m],
                    recv_sem=far_sems.at[1, m], device_id=(view, patch), device_id_type=MESH,
                ).wait_recv()

            @pl.when(far_owner[m] != mine)
            def _():
                far_copies[m].wait_send()
        drain(started)


def finish(rows, rate_rows, groups, query_out, key_out, value_out, rate_out, fast_out, sems):
    copies = [
        pltpu.make_async_copy(rows.at[n], out, sems.at[n]) for n, out in enumerate((query_out, key_out, value_out))
    ]
    for copy in copies:
        copy.start()
    rate_out[...] = rate_rows[...]
    for m in range(3):
        fast_out[GROUP * m:GROUP * (m + 1), :] = groups[m, 0:GROUP, 0:HD]
    for copy in copies:
        copy.wait()


def scratch():
    tile = (8, 128)
    halves = (BLOCKS, ALL_ROWS)
    shapes = [
        *[pltpu.VMEM((ROWS, HEADS * HD), bf16)] * 4,
        pltpu.VMEM((HEADS, ROWS), f32),
        pltpu.VMEM((3, HD, FF), f32),
        pltpu.VMEM((BLOCKS, 3, UNITS, HD), f32),
        *[pltpu.VMEM((BLOCKS, 2 * PAD, HD), bf16)] * 4,
        *[pltpu.VMEM((BLOCKS, PAD, HD), bf16)] * 4,
        *[pltpu.VMEM((BLOCKS, 3, UNITS, HD), f32)] * 2,
        pltpu.VMEM((BLOCKS, 3, 2, UNITS, 1), f32),
        *[pltpu.VMEM((HEADS, ROWS + 8, 2 * HD), f32)] * 2,
        *[pltpu.VMEM((SLOTS, ROWS + 8, 2 * HD), f32)] * 2,
        *[pltpu.VMEM((ALL_ROWS, 1), f32)] * 2,
        *[pltpu.VMEM((ALL_ROWS, HD), bf16)] * 4,
        *[pltpu.VMEM(halves + (PAD,), f32)] * 7,
        *[pltpu.VMEM(halves + (2 * PAD,), bf16)] * 4,
        *[pltpu.VMEM(halves + (PAD,), bf16)] * 4,
        pltpu.VMEM((BLOCKS, 2 * PAD, HD), f32),
        pltpu.VMEM((BLOCKS, PAD, HD), f32),
        pltpu.VMEM((ALL_ROWS // WIDE, 8, WIDE), f32),
        pltpu.VMEM((SLOTS, ROWS, HD), f32),
        *[pltpu.VMEM((4, ROWS, HD), f32)] * 3,
        pltpu.VMEM((SLOTS, ROWS + 8, 2 * HD), f32),
        *[pltpu.VMEM((4, ROWS + 8, 2 * HD), f32)] * 3,
    ]
    rounds = 2 * BLOCKS
    for part in PARTS:
        first, second, shard, window = part_sizes(part)
        shapes += [
            pltpu.VMEM((rounds, first * shard) + tile, f32),
            pltpu.VMEM((rounds, first - 1, shard) + tile, f32),
            pltpu.VMEM((rounds, shard) + tile, f32),
            pltpu.VMEM((rounds, second - 1, window) + tile, f32),
            pltpu.VMEM((rounds, window) + tile, f32),
            pltpu.VMEM((rounds, second - 1, window) + tile, f32),
            pltpu.VMEM((rounds, shard) + tile, f32),
            pltpu.VMEM((rounds, first * shard) + tile, f32),
        ]
    shapes += [
        pltpu.VMEM((BLOCKS, UNITS, 640), f32),
        pltpu.VMEM((BLOCKS, NX - 1, PIECE, 640), f32),
        pltpu.VMEM((NZ, 8, 640), f32),
        pltpu.VMEM((NZ - 1, 8, 640), f32),
        pltpu.VMEM((HALF // GROUP, 8, 640), f32),
        pltpu.VMEM((3, 8, 256), f32),
        pltpu.SemaphoreType.DMA((N_SEMS,)),
        pltpu.SemaphoreType.DMA((N_SEMS,)),
        pltpu.SemaphoreType.DMA((2, 3)),
        pltpu.SemaphoreType.DMA((8,)),
    ]
    return shapes


def on_device(queries, key_rows, value_rows, step_rates, fast_init, out_grad):
    vmem = pl.BlockSpec(memory_space=pltpu.VMEM)
    anywhere = pl.BlockSpec(memory_space=pl.ANY)
    hbm = pl.BlockSpec(memory_space=pltpu.HBM)
    rates_shape = jax.ShapeDtypeStruct((HEADS, ROWS), f32)
    results = pl.pallas_call(
        kernel,
        out_shape=(
            jax.ShapeDtypeStruct((3, ROWS, HEADS * HD), bf16),
            rates_shape,
            jax.ShapeDtypeStruct((3, 8, 256), f32),
        ),
        in_specs=[hbm] * 6,
        out_specs=(vmem,) * 3,
        scratch_shapes=scratch(),
        compiler_params=pltpu.CompilerParams(
            collective_id=0, has_side_effects=True, vmem_limit_bytes=56 * 2**20
        ),
        name="layer_grad",
    )(queries, key_rows, value_rows, step_rates.T, out_grad, fast_init)
    rows = jax.ShapeDtypeStruct((ROWS, HEADS * HD), bf16)
    query_grad, key_grad, value_grad, rate_grad, fast_grad = pl.pallas_call(
        finish,
        out_shape=(rows, rows, rows, rates_shape, jax.ShapeDtypeStruct((3 * GROUP, HD), f32)),
        in_specs=[vmem] * 3,
        out_specs=(anywhere,) * 3 + (vmem,) * 2,
        scratch_shapes=[pltpu.SemaphoreType.DMA((3,))],
        compiler_params=pltpu.CompilerParams(vmem_limit_bytes=4 * 2**20),
        name="outputs",
    )(*results)
    return query_grad, key_grad, value_grad, rate_grad.T, fast_grad.T


def solution(mesh):
    both = ("view", "patch")
    return jax.shard_map(
        on_device,
        mesh=mesh,
        in_specs=(P(both, None), P(both, None), P(both, None), P(both, None), P(), P(both, None)),
        out_specs=(P(both, None), P(both, None), P(both, None), P(both, None), P(None, both)),
        check_vma=False,
    )
```

```python
import itertools
import math

import jax
import jax.numpy as jnp
from jax import lax
from jax.experimental import pallas as pl
from jax.experimental.pallas import tpu as pltpu
from jax.sharding import PartitionSpec as P

MESH = pl.DeviceIdType.MESH
f32, bf16 = jnp.float32, jnp.bfloat16

step_size = 0.2
epsilon = 1e-06

NX, NY, NZ = 4, 4, 8
HEADS, HD, FF = 4, 192, 384
HALF = FF // 2
ROWS = 128
SLOTS = 8
ALL_ROWS = SLOTS * ROWS
CHUNK = 256
WIDE = 512
TOTAL_ROWS = ROWS * NX * NY * NZ * 2
COEFFICIENT = step_size * math.sqrt(TOTAL_ROWS)
N_SEMS = 64
GROUP = 6


def device(x, y, z, core):
    return (lax.div(x, 2) * 2 + core, (y * 2 + lax.rem(x, 2)) * 8 + z)


BLOCKS = 2
UNITS = HALF // BLOCKS
PAD = 128
ROW_TILES = UNITS // 8
PIECE = UNITS // NX

PARTS = (("x", (0, 1, 2, 3, 4)),)


def part_sizes(part):
    axis, lane_tiles = part
    first, second = (NX, NZ) if axis == "x" else (NZ, NX)
    shard = ROW_TILES * len(lane_tiles) // first
    window = -(-shard // second)
    if (shard - window) // (second - 1) >= window and shard > second:
        window += 1
    return first, second, shard, window


def nt(a, b):
    return lax.dot_general(a, b, (((1,), (1,)), ((), ())), preferred_element_type=f32)


def nn(a, b):
    return lax.dot_general(a, b, (((1,), (0,)), ((), ())), preferred_element_type=f32)


def tn(a, b):
    return lax.dot_general(a, b, (((0,), (0,)), ((), ())), preferred_element_type=f32)


def split(value):
    high = value.astype(bf16)
    return high, (value - high.astype(f32)).astype(bf16)


def kernel(
    q_hbm, k_hbm, v_hbm, r_hbm, g_hbm, w_hbm,
    rows_hbm, rg_out, fg_out,
    q_ref, k_ref, v_ref, g_ref, r_ref,
    w_load, w_own, wh_ab, wl_ab, nh_ab, nl_ab, wh_c, wl_c, nh_c, nl_c, moved, gm, norms,
    kv_send, qg_send, kv, qg, rates, inv_rates, kb, vb, qb, gb,
    gate_s, up_s, pull_s, m1, m2, m3, m4,
    s_ab_h, s_ab_l, e_ab_h, e_ab_l, s_c_h, s_c_l, e_c_h, e_c_l,
    acc_ab, acc_c, rate_rows, dq, xq, oq, rq, dkv, xkv, okv, rkv,
    p0_t, p0_r1, p0_s1, p0_r2, p0_s2, p0_a1, p0_f1, p0_g,
    f_t, f_r1, f_s1, f_r2, d_grp, f_msg,
    rows_ref, send_sems, recv_sems, far_sems, load_sems,
):
    view, patch = lax.axis_index("view"), lax.axis_index("patch")
    x, core = (view // 2) * 2 + (patch // 8) % 2, view % 2
    y, z = patch // 16, patch % 8
    mine = view * 64 + patch
    half_block = 2 * y + core

    known = {}

    def peer(axis, offset):
        if (axis, offset) not in known:
            if axis == "x":
                target = device(lax.rem(x + offset, NX), y, z, core)
            elif axis == "y":
                target = device(x, lax.rem(y + offset, NY), z, core)
            elif axis == "z":
                target = device(x, y, lax.rem(z + offset, NZ), core)
            else:
                target = device(x, y, z, 1 - core)
            known[axis, offset] = target
        return known[axis, offset]

    place = {"x": x, "z": z}

    far_group = [32 * (8 * m + half_block) + 8 * x + z for m in range(3)]
    far_owner = [group // 3 for group in far_group]
    near_source = []
    for t in range(3):
        group = 3 * mine + t
        block, rest = group // 32, group % 32
        near_source.append((rest // 8, (block % 8) // 2, rest % 8, block % 2))
    near_index = []
    for sx, sy, sz, sc in near_source:
        sv, sp = device(sx, sy, sz, sc)
        near_index.append(sv * 64 + sp)

    barrier = pltpu.get_barrier_semaphore()
    peers = [("x", d) for d in range(1, NX)] + [("z", d) for d in range(1, NZ)]
    peers += [("y", d) for d in range(1, NY)] + [("core", 1)]
    for t in range(3):
        @pl.when(near_index[t] != mine)
        def _():
            pl.semaphore_signal(barrier, inc=1, device_id=device(*near_source[t]), device_id_type=MESH)
    peers = sorted(peers, key=lambda one: one[0], reverse=True)
    for axis, offset in peers:
        pl.semaphore_signal(barrier, inc=1, device_id=peer(axis, offset), device_id_type=MESH)

    ids = itertools.count()
    started = []

    def send(src, dst, target):
        which = next(ids)
        copy = pltpu.make_async_remote_copy(
            src_ref=src, dst_ref=dst, send_sem=send_sems.at[which], recv_sem=recv_sems.at[which],
            device_id=target, device_id_type=MESH,
        )
        copy.start()
        started.append(copy)
        return copy

    def send_all(triples, all_of_them):
        which = next(ids)
        for src, dst, target in triples:
            copy = pltpu.make_async_remote_copy(
                src_ref=src, dst_ref=dst, send_sem=send_sems.at[which], recv_sem=recv_sems.at[which],
                device_id=target, device_id_type=MESH,
            )
            copy.start()
        whole = pltpu.make_async_remote_copy(
            src_ref=all_of_them, dst_ref=all_of_them, send_sem=send_sems.at[which], recv_sem=recv_sems.at[which],
            device_id=target, device_id_type=MESH,
        )
        started.append(whole)
        return whole

    def take_started():
        taken = list(started)
        started.clear()
        return taken

    def drain(copies):
        for copy in copies:
            copy.wait_send()

    row_loads = []
    for n, (src, dst) in enumerate(((k_hbm, k_ref), (v_hbm, v_ref), (r_hbm, r_ref), (q_hbm, q_ref), (g_hbm, g_ref))):
        load = pltpu.make_async_copy(src, dst, load_sems.at[3 + n])
        load.start()
        row_loads.append(load)
    loads = []
    for m in range(3):
        first = pl.multiple_of(m * HEADS * FF + y * FF, 128)
        load = pltpu.make_async_copy(w_hbm.at[:, pl.ds(first, FF)], w_load.at[m], load_sems.at[m])
        load.start()
        loads.append(load)

    def pack(buffer, left, right):
        for h in range(HEADS):
            cols = slice(HD * h, HD * (h + 1))
            buffer[h, 0:ROWS, 0:HD] = left[:, cols].astype(f32)
            buffer[h, 0:ROWS, HD:2 * HD] = right[:, cols].astype(f32)

    for load in row_loads[:3]:
        load.wait()
    pack(kv_send, k_ref, v_ref)
    for h in range(HEADS):
        kv_send[h, ROWS:ROWS + 8, :] = jnp.zeros((8, 2 * HD), f32)
        kv_send[h, ROWS:ROWS + 8, 0:ROWS] = jnp.broadcast_to(r_ref[h:h + 1, :], (8, ROWS))

    far_count = sum((owner != mine).astype(jnp.int32) for owner in far_owner)
    pl.semaphore_wait(barrier, len(peers) + far_count)

    def scatter_heads(buffer, landing):
        out = {}
        for d in (1, 3, 2):
            out[d] = send(buffer.at[(y + d) % NY], landing.at[d], peer("y", d))
        out["own"] = send(buffer.at[y], landing.at[4], peer("core", 1))
        return out

    kv_copies = scatter_heads(kv_send, kv)
    for load in row_loads[3:]:
        load.wait()
    pack(qg_send, q_ref, g_ref)

    def store_weights(ab_h, ab_l, c_h, c_l, b, m, value):
        if m < 2:
            rows = (b, slice(PAD * m, PAD * m + UNITS))
            ab_h[rows], ab_l[rows] = split(value)
        else:
            rows = (b, slice(0, UNITS))
            c_h[rows], c_l[rows] = split(value)

    for b in range(BLOCKS):
        none = jnp.zeros((PAD - UNITS, HD), bf16)
        for ref in (wh_ab, wl_ab, nh_ab, nl_ab):
            ref[b, UNITS:PAD] = none
            ref[b, PAD + UNITS:2 * PAD] = none
        for ref in (wh_c, wl_c, nh_c, nl_c):
            ref[b, UNITS:PAD] = none
    for m in range(3):
        loads[m].wait()
        both = w_load[m]
        own = jnp.where(core == 0, both[:, 0:HALF], both[:, HALF:FF]).T
        for b in range(BLOCKS):
            pieces = [own[2 * PIECE * n + PIECE * b:2 * PIECE * n + PIECE * (b + 1), :] for n in range(NX)]
            block = jnp.concatenate(pieces, axis=0)
            w_own[b, m] = block
            norms[b, m, 0] = jnp.sqrt(jnp.sum(block * block, axis=1, keepdims=True) + epsilon)
            store_weights(wh_ab, wl_ab, wh_c, wl_c, b, m, block)

    def row_block(s):
        first = (s % 4) * CHUNK + (s // 4) * ROWS
        return slice(first, first + ROWS)

    def unpack_kv(s):
        kb[row_block(s), :] = kv[s, 0:ROWS, 0:HD].astype(bf16)
        vb[row_block(s), :] = kv[s, 0:ROWS, HD:2 * HD].astype(bf16)
        column = kv[s, ROWS:ROWS + 8, 0:ROWS].T[:, 0:1]
        rates[row_block(s), :] = column
        inv_rates[row_block(s), :] = 1.0 / column

    def unpack_qg(s):
        qb[row_block(s), :] = qg[s, 0:ROWS, 0:HD].astype(bf16)
        gb[row_block(s), :] = qg[s, 0:ROWS, HD:2 * HD].astype(bf16)

    def silu_parts(gate):
        sig = 1.0 / (1.0 + jnp.exp(-gate))
        act = gate * sig
        slope = sig + act * (1.0 - sig)
        return sig, act, slope

    def clear(b):
        acc_ab[b] = jnp.zeros((2 * PAD, HD), f32)
        acc_c[b] = jnp.zeros((PAD, HD), f32)

    for b in range(BLOCKS):
        clear(b)

    GATE, UP = slice(0, PAD), slice(PAD, 2 * PAD)

    def add_terms(b, rows, gate_term, up_term, pull_term, left, right):
        both = jnp.concatenate([gate_term, up_term], axis=1)
        both_h, both_l = split(both)
        pull_h, pull_l = split(pull_term)
        s_ab_h[b, rows, :], s_c_h[b, rows, :] = both_h, pull_h
        s_ab_l[b, rows, :], s_c_l[b, rows, :] = both_l, pull_l
        acc_ab[b] += tn(both_h, left) + tn(both_l, left)
        acc_c[b] += tn(pull_h, right) + tn(pull_l, right)

    def update_chunk(b, i):
        rows = slice(i * CHUNK, (i + 1) * CHUNK)
        keys, values, eta = kb[rows, :], vb[rows, :], rates[rows, :]
        both = nt(keys, wh_ab[b]) + nt(keys, wl_ab[b])
        gate, up = both[:, GATE], both[:, UP]
        pulled = nt(values, wh_c[b]) + nt(values, wl_c[b])
        gate_s[b, rows, :], up_s[b, rows, :], pull_s[b, rows, :] = gate, up, pulled
        _, act, slope = silu_parts(gate)
        scaled = -eta * pulled
        add_terms(b, rows, scaled * up * slope, scaled * act, -eta * act * up, keys, values)

    def take_pair(d):
        unpack_kv(d)
        unpack_kv(4 + d)

    def pass_on(copies, landing, d):
        copies[d].wait_recv()
        return send(landing.at[d], landing.at[4 + d], peer("core", 1))

    with jax.named_scope("keys_own"):
        kv[0] = kv_send[y]
        kv_copies["own"].wait_recv()
        take_pair(0)
        for b in range(BLOCKS):
            update_chunk(b, 0)
    passed = {}
    with jax.named_scope("keys_first"):
        passed[1] = pass_on(kv_copies, kv, 1)
        passed[3] = pass_on(kv_copies, kv, 3)
        passed[1].wait_recv()
        take_pair(1)
        for b in range(BLOCKS):
            update_chunk(b, 1)
    with jax.named_scope("keys_second"):
        passed[2] = pass_on(kv_copies, kv, 2)
        qg_copies = scatter_heads(qg_send, qg)
        passed[3].wait_recv()
        take_pair(3)
        for b in range(BLOCKS):
            update_chunk(b, 3)
    with jax.named_scope("keys_third"):
        passed[2].wait_recv()
        take_pair(2)

    rate_sum = sum(kv[s, ROWS:ROWS + 8, 0:ROWS] for s in range(SLOTS))
    total_part = jnp.sum(rate_sum[0:1, :], axis=1, keepdims=True)

    parts = ((p0_t, p0_r1, p0_s1, p0_r2, p0_s2, p0_a1, p0_f1, p0_g),)

    def lanes_of(first, second, third, tail):
        return (
            first[:, 0:128],
            second[:, 0:128],
            jnp.concatenate([first[:, 128:192], second[:, 128:192]], axis=1),
            third[:, 0:128],
            jnp.concatenate([third[:, 128:192], tail], axis=1),
        )

    def sums_of(b, tail):
        return lanes_of(
            acc_ab[b, 0:UNITS, :], acc_ab[b, PAD:PAD + UNITS, :], acc_c[b, 0:UNITS, :], tail
        )

    def start_stage(r, p, source):
        axis, lane_tiles = PARTS[p]
        first, second, shard, window = part_sizes(PARTS[p])
        t = parts[p][0]
        for jj, j in enumerate(lane_tiles):
            t[r, jj * ROW_TILES:(jj + 1) * ROW_TILES] = source[j].reshape(ROW_TILES, 8, 128)
        r1 = parts[p][1]
        triples = []
        for d in range(1, first):
            there = lax.rem(place[axis] + d, first)
            triples.append((t.at[r, pl.ds(there * shard, shard)], r1.at[r, d - 1], peer(axis, d)))
        return send_all(triples, r1.at[r])

    def start_of(p, k):
        _, second, shard, window = part_sizes(PARTS[p])
        return lax.div((shard - window) * k, second - 1)

    def second_stage(r, p, copies):
        axis = PARTS[p][0]
        other = "z" if axis == "x" else "x"
        first, second, shard, window = part_sizes(PARTS[p])
        t, r1, s1, r2 = parts[p][:4]
        total = t[r, pl.ds(place[axis] * shard, shard)]
        copies.wait_recv()
        for d in range(1, first):
            total = total + r1[r, d - 1]
        s1[r] = total
        triples = []
        for d in range(1, second):
            there = lax.rem(place[other] + d, second)
            triples.append((s1.at[r, pl.ds(start_of(p, there), window)], r2.at[r, d - 1], peer(other, d)))
        return send_all(triples, r2.at[r])

    def third_stage(r, p, copies):
        other = "z" if PARTS[p][0] == "x" else "x"
        _, second, shard, window = part_sizes(PARTS[p])
        _, _, s1, r2, s2, a1, f1, _ = parts[p]
        total = s1[r, pl.ds(start_of(p, place[other]), window)]
        copies.wait_recv()
        for d in range(1, second):
            total = total + r2[r, d - 1]
        s2[r] = total
        return send_all([(s2.at[r], a1.at[r, d - 1], peer(other, d)) for d in range(1, second)], a1.at[r])

    def fourth_stage(r, p, copies):
        axis = PARTS[p][0]
        other = "z" if axis == "x" else "x"
        first, second, shard, window = part_sizes(PARTS[p])
        _, _, _, _, s2, a1, f1, g = parts[p]
        f1[r, pl.ds(start_of(p, place[other]), window)] = s2[r]
        copies.wait_recv()
        for d in range(1, second):
            there = lax.rem(place[other] + second - d, second)
            f1[r, pl.ds(start_of(p, there), window)] = a1[r, d - 1]
        here = pl.ds(place[axis] * shard, shard)
        out = send_all([(f1.at[r], g.at[r, here], peer(axis, d)) for d in range(1, first)], parts[p][1].at[r])
        g[r, here] = f1[r]
        return out

    class Sum:
        def __init__(self, r, b):
            self.r = 2 * r + b
            self.b = b

        def start(self, tail):
            source = sums_of(self.b, tail)
            self.copies = [start_stage(self.r, p, source) for p in range(len(PARTS))]

        def step(self, stage):
            self.copies = [stage(self.r, p, self.copies[p]) for p in range(len(PARTS))]

        def result(self):
            for group in self.copies:
                group.wait_recv()
            tiles = {}
            for p in range(len(PARTS)):
                for jj, j in enumerate(PARTS[p][1]):
                    tiles[j] = parts[p][7][self.r, jj * ROW_TILES:(jj + 1) * ROW_TILES].reshape(UNITS, 128)
            gate = jnp.concatenate([tiles[0], tiles[2][:, 0:64]], axis=1)
            up = jnp.concatenate([tiles[1], tiles[2][:, 64:128]], axis=1)
            down = jnp.concatenate([tiles[3], tiles[4][:, 0:64]], axis=1)
            return (gate, up, down), tiles[4][0:1, 64:65]

    def prepare_chunk(i, _):
        rows = pl.ds(pl.multiple_of(i * CHUNK, CHUNK), CHUNK)
        eta = rates[rows, :]
        for b in range(BLOCKS):
            gate, up, pulled = gate_s[b, rows, :], up_s[b, rows, :], pull_s[b, rows, :]
            sig, act, slope = silu_parts(gate)
            curve = sig * (1.0 - sig) * (2.0 + gate * (1.0 - 2.0 * sig))
            scaled = eta * pulled
            by_slope, by_act = eta * (up * slope), eta * act
            m1[b, rows, :], m2[b, rows, :] = scaled * up * curve, scaled * slope
            m3[b, rows, :], m4[b, rows, :] = by_slope, by_act
            e_ab_h[b, rows, GATE], e_ab_l[b, rows, GATE] = split(by_slope * pulled)
            e_ab_h[b, rows, UP], e_ab_l[b, rows, UP] = split(by_act * pulled)
            e_c_h[b, rows, :], e_c_l[b, rows, :] = split(by_act * up)
        return 0

    query_passed = {}

    def prepare():
        lax.fori_loop(0, ALL_ROWS // CHUNK, prepare_chunk, 0)

    def pass_queries():
        qg[0] = qg_send[y]
        for d in (1, 3, 2):
            query_passed[d] = pass_on(qg_copies, qg, d)

    def take_queries():
        qg_copies["own"].wait_recv()
        for d in (1, 3, 2):
            query_passed[d].wait_recv()
        for s in range(SLOTS):
            unpack_qg(s)

    tail = jnp.broadcast_to(total_part, (UNITS, 64))
    sums = [Sum(0, b) for b in range(BLOCKS)]
    for b in range(BLOCKS):
        with jax.named_scope("keys_last"):
            update_chunk(b, 2)
            sums[b].start(tail)
    prepare()
    for stage, work in ((second_stage, pass_queries), (third_stage, take_queries), (fourth_stage, None)):
        for b in range(BLOCKS):
            sums[b].step(stage)
        if work is not None:
            work()

    def new_weights(b):
        terms, total = sums[b].result()
        scale = COEFFICIENT / total
        for m in range(3):
            change = terms[m] * scale
            shifted = w_own[b, m] - change
            inverse = lax.rsqrt(jnp.sum(shifted * shifted, axis=1, keepdims=True) + epsilon)
            gm[b, m], moved[b, m], norms[b, m, 1] = change, shifted, inverse
            store_weights(nh_ab, nl_ab, nh_c, nl_c, b, m, shifted * (norms[b, m, 0] * inverse))
        clear(b)
        return total, scale

    def apply_block(b):
        def apply_chunk(i, _):
            rows = pl.ds(pl.multiple_of(i * WIDE, WIDE), WIDE)
            queries, grads = qb[rows, :], gb[rows, :]
            both = nt(queries, nh_ab[b]) + nt(queries, nl_ab[b])
            gate, up = both[:, GATE], both[:, UP]
            pulled = nt(grads, nh_c[b]) + nt(grads, nl_c[b])
            _, act, slope = silu_parts(gate)
            add_terms(b, rows, pulled * up * slope, pulled * act, act * up, queries, grads)
            return 0

        lax.fori_loop(0, ALL_ROWS // WIDE, apply_chunk, 0)

    new_sums = [Sum(1, b) for b in range(BLOCKS)]
    early = take_started()
    for b in range(BLOCKS):
        with jax.named_scope("apply"):
            totals, scale = new_weights(b)
            apply_block(b)
            new_sums[b].start(jnp.zeros((UNITS, 64), f32))

    def product(ah, al, bh, bl, rows):
        high = ah[rows, :]
        return nn(high, bh) + nn(high, bl) + nn(al[rows, :], bh)

    def query_grads(b):
        def query_chunk(i, _):
            rows = pl.ds(pl.multiple_of(i * CHUNK, CHUNK), CHUNK)
            part = product(s_ab_h.at[b], s_ab_l.at[b], nh_ab[b], nl_ab[b], rows)
            dq[i] = part[0:ROWS] if b == 0 else dq[i] + part[0:ROWS]
            dq[4 + i] = part[ROWS:CHUNK] if b == 0 else dq[4 + i] + part[ROWS:CHUNK]
            return 0

        lax.fori_loop(0, 4, query_chunk, 0)

    def return_rows(pair, partial, arrived, sums, landing):
        pair.wait_recv()
        out = []
        for d in (1, 3, 2, 0):
            if d == 0:
                landing[0] = partial[0] + arrived[0]
            else:
                sums[d] = partial[d] + arrived[d]
                out.append(send(sums.at[d], landing.at[d], peer("y", NY - d)))
        return out

    for b in range(BLOCKS):
        with jax.named_scope("query_grads"):
            query_grads(b)
        new_sums[b].step(second_stage)
    query_pair = send(dq.at[pl.ds(4, 4)], xq, peer("core", 1))
    new_sums[0].step(third_stage)
    query_back = return_rows(query_pair, dq, xq, oq, rq)
    drain(early)
    new_sums[1].step(third_stage)
    for b in range(BLOCKS):
        new_sums[b].step(fourth_stage)

    direct = {}

    def pull_weights(b):
        d_new, _ = new_sums[b].result()
        head_part = jnp.zeros((1, 1), f32)
        for m in range(3):
            init_norm, inverse = norms[b, m, 0], norms[b, m, 1]
            shifted = moved[b, m]
            dots = jnp.sum(d_new[m] * shifted, axis=1, keepdims=True)
            d_moved = d_new[m] * (init_norm * inverse) - shifted * (dots * init_norm * inverse * inverse * inverse)
            direct[b, m] = d_moved + w_own[b, m] * (dots * inverse / init_norm)
            by_row = jnp.sum(d_moved * gm[b, m], axis=1, keepdims=True)
            head_part = head_part - jnp.sum(by_row, axis=0, keepdims=True)
            store_weights(nh_ab, nl_ab, nh_c, nl_c, b, m, d_moved * scale)
        clear(b)
        return -head_part / totals

    def pull_block(b):
        def pull_chunk(i, _):
            rows = pl.ds(pl.multiple_of(i * WIDE, WIDE), WIDE)
            keys, values = kb[rows, :], vb[rows, :]
            both = nt(keys, nh_ab[b]) + nt(keys, nl_ab[b])
            one, two = both[:, GATE], both[:, UP]
            three = nt(values, nh_c[b]) + nt(values, nl_c[b])
            by_slope, by_act, by_two = m3[b, rows, :], m4[b, rows, :], m2[b, rows, :]
            c_gate = one * m1[b, rows, :] + two * by_two + three * by_slope
            c_up = one * by_two + three * by_act
            c_pull = one * by_slope + two * by_act
            add_terms(b, rows, c_gate, c_up, c_pull, keys, values)
            by_rate = c_pull * pull_s[b, rows, :] + three * (by_act * up_s[b, rows, :])
            by_rate_h, by_rate_l = split(by_rate * inv_rates[rows, :])
            ones = jnp.ones((8, PAD), bf16)
            part = nt(ones, by_rate_h) + nt(ones, by_rate_l)
            rate_rows[i] = part if b == 0 else rate_rows[i] + part
            return 0

        lax.fori_loop(0, ALL_ROWS // WIDE, pull_chunk, 0)

    early = take_started()
    weight_copies = []
    d_totals = jnp.zeros((1, 1), f32)
    for b in range(BLOCKS):
        with jax.named_scope("pull"):
            d_totals = d_totals + pull_weights(b)
            pull_block(b)
            tiles = sums_of(b, jnp.zeros((UNITS, 64), f32))
            for j in range(5):
                f_t[b, :, 128 * j:128 * (j + 1)] = tiles[j]
            triples = []
            for d in range(1, NX):
                first = pl.multiple_of(((x + d) % NX) * PIECE, PIECE)
                triples.append((f_t.at[b, pl.ds(first, PIECE)], f_r1.at[b, d - 1], peer("x", d)))
            weight_copies.append(send_all(triples, f_r1.at[b]))

    def key_chunk(i, _):
        rows = pl.ds(pl.multiple_of(i * CHUNK, CHUNK), CHUNK)
        key_part, value_part = 0.0, 0.0
        for b in range(BLOCKS):
            key_part += product(s_ab_h.at[b], s_ab_l.at[b], wh_ab[b], wl_ab[b], rows)
            key_part += product(e_ab_h.at[b], e_ab_l.at[b], nh_ab[b], nl_ab[b], rows)
            value_part += product(s_c_h.at[b], s_c_l.at[b], wh_c[b], wl_c[b], rows)
            value_part += product(e_c_h.at[b], e_c_l.at[b], nh_c[b], nl_c[b], rows)
        for slot, first in ((i, 0), (4 + i, ROWS)):
            dkv[slot, 0:ROWS, 0:HD] = key_part[first:first + ROWS]
            dkv[slot, 0:ROWS, HD:2 * HD] = value_part[first:first + ROWS]
        return 0

    with jax.named_scope("row_grads"):
        lax.fori_loop(0, 4, key_chunk, 0)
        for s in range(SLOTS):
            dkv[s, ROWS:ROWS + 8, :] = jnp.zeros((8, 2 * HD), f32)
            first = row_block(s).start
            lane = first % WIDE
            dkv[s, ROWS:ROWS + 8, 0:ROWS] = rate_rows[first // WIDE, :, lane:lane + ROWS] + d_totals
        pair = send(dkv.at[pl.ds(4, 4)], xkv, peer("core", 1))

    with jax.named_scope("x_sums"):
        for b in range(BLOCKS):
            total = f_t[b, pl.ds(pl.multiple_of(x * PIECE, PIECE), PIECE), :]
            weight_copies[b].wait_recv()
            for d in range(1, NX):
                total = total + f_r1[b, d - 1]
            for n in range(4):
                f_s1[4 * b + n, 0:GROUP, :] = total[GROUP * n:GROUP * (n + 1), :]
                f_s1[4 * b + n, GROUP:8, :] = jnp.zeros((8 - GROUP, 640), f32)
        triples = [(f_s1.at[(z + d) % NZ], f_r2.at[d - 1], peer("z", d)) for d in range(1, NZ)]
        weight_copies = send_all(triples, f_r2)
    with jax.named_scope("row_returns"):
        row_back = return_rows(pair, dkv, xkv, okv, rkv)
    with jax.named_scope("direct"):
        for b in range(BLOCKS):
            tiles = lanes_of(direct[b, 0], direct[b, 1], direct[b, 2], jnp.zeros((UNITS, 64), f32))
            for j in range(5):
                for n in range(16):
                    group = 8 * (n // 4) + 4 * b + n % 4
                    d_grp[group, 0:GROUP, 128 * j:128 * (j + 1)] = tiles[j][GROUP * n:GROUP * (n + 1), :]

    drain(early)
    z_scope = jax.named_scope("z_sums")
    z_scope.__enter__()
    total = f_s1[z]
    weight_copies.wait_recv()
    for d in range(1, NZ):
        total = total + f_r2[d - 1]
    total = (total + d_grp[8 * x + z]) * (1.0 / math.sqrt(TOTAL_ROWS))
    for m, (low, high) in enumerate(((0, 256), (128, 320), (384, 512))):
        f_msg[m, :, 0:128] = total[:, low:low + 128]
        f_msg[m, :, 128:HD] = total[:, high:high + 64]
    far_copies = []
    for m in range(3):
        slot = far_group[m] % 3
        owner = far_owner[m]
        copy = pltpu.make_async_remote_copy(
            src_ref=f_msg.at[m], dst_ref=fg_out.at[slot], send_sem=far_sems.at[0, m], recv_sem=far_sems.at[1, slot],
            device_id=(owner // 64, owner % 64), device_id_type=MESH,
        )

        @pl.when(owner != mine)
        def _():
            copy.start()

        @pl.when(owner == mine)
        def _():
            fg_out[slot] = f_msg[m]

        far_copies.append(copy)

    z_scope.__exit__(None, None, None)

    def rows_out(which, landing, lanes):
        for h in range(HEADS):
            d = (h + NY - y) % NY
            rows_ref[which, :, HD * h:HD * (h + 1)] = landing[d, 0:ROWS, lanes:lanes + HD].astype(bf16)
        store = pltpu.make_async_copy(rows_ref.at[which], rows_hbm.at[which], load_sems.at[8 + which])
        store.start()
        stores.append(store)

    stores = []

    with jax.named_scope("query_rows"):
        for copy in query_back:
            copy.wait_recv()
        rows_out(0, rq, 0)
    with jax.named_scope("key_rows"):
        for copy in row_back:
            copy.wait_recv()
        rows_out(1, rkv, 0)
        rows_out(2, rkv, HD)
        for h in range(HEADS):
            rg_out[h:h + 1, :] = rkv[(h + NY - y) % NY, ROWS:ROWS + 1, 0:ROWS]

    with jax.named_scope("columns"):
        for m in range(3):
            @pl.when(near_index[m] != mine)
            def _():
                pltpu.make_async_remote_copy(
                    src_ref=f_msg.at[m], dst_ref=fg_out.at[m], send_sem=far_sems.at[0, m],
                    recv_sem=far_sems.at[1, m], device_id=(view, patch), device_id_type=MESH,
                ).wait_recv()

            @pl.when(far_owner[m] != mine)
            def _():
                far_copies[m].wait_send()
        drain(started)
        for store in stores:
            store.wait()


def finish(rows, rate_rows, groups, query_out, key_out, value_out, rate_out, fast_out, sems):
    copies = [
        pltpu.make_async_copy(rows.at[n], out, sems.at[n]) for n, out in enumerate((query_out, key_out, value_out))
    ]
    for copy in copies:
        copy.start()
    rate_out[...] = rate_rows[...]
    for m in range(3):
        fast_out[GROUP * m:GROUP * (m + 1), :] = groups[m, 0:GROUP, 0:HD]
    for copy in copies:
        copy.wait()


def scratch():
    tile = (8, 128)
    halves = (BLOCKS, ALL_ROWS)
    shapes = [
        *[pltpu.VMEM((ROWS, HEADS * HD), bf16)] * 4,
        pltpu.VMEM((HEADS, ROWS), f32),
        pltpu.VMEM((3, HD, FF), f32),
        pltpu.VMEM((BLOCKS, 3, UNITS, HD), f32),
        *[pltpu.VMEM((BLOCKS, 2 * PAD, HD), bf16)] * 4,
        *[pltpu.VMEM((BLOCKS, PAD, HD), bf16)] * 4,
        *[pltpu.VMEM((BLOCKS, 3, UNITS, HD), f32)] * 2,
        pltpu.VMEM((BLOCKS, 3, 2, UNITS, 1), f32),
        *[pltpu.VMEM((HEADS, ROWS + 8, 2 * HD), f32)] * 2,
        *[pltpu.VMEM((SLOTS, ROWS + 8, 2 * HD), f32)] * 2,
        *[pltpu.VMEM((ALL_ROWS, 1), f32)] * 2,
        *[pltpu.VMEM((ALL_ROWS, HD), bf16)] * 4,
        *[pltpu.VMEM(halves + (PAD,), f32)] * 7,
        *[pltpu.VMEM(halves + (2 * PAD,), bf16)] * 4,
        *[pltpu.VMEM(halves + (PAD,), bf16)] * 4,
        pltpu.VMEM((BLOCKS, 2 * PAD, HD), f32),
        pltpu.VMEM((BLOCKS, PAD, HD), f32),
        pltpu.VMEM((ALL_ROWS // WIDE, 8, WIDE), f32),
        pltpu.VMEM((SLOTS, ROWS, HD), f32),
        *[pltpu.VMEM((4, ROWS, HD), f32)] * 3,
        pltpu.VMEM((SLOTS, ROWS + 8, 2 * HD), f32),
        *[pltpu.VMEM((4, ROWS + 8, 2 * HD), f32)] * 3,
    ]
    rounds = 2 * BLOCKS
    for part in PARTS:
        first, second, shard, window = part_sizes(part)
        shapes += [
            pltpu.VMEM((rounds, first * shard) + tile, f32),
            pltpu.VMEM((rounds, first - 1, shard) + tile, f32),
            pltpu.VMEM((rounds, shard) + tile, f32),
            pltpu.VMEM((rounds, second - 1, window) + tile, f32),
            pltpu.VMEM((rounds, window) + tile, f32),
            pltpu.VMEM((rounds, second - 1, window) + tile, f32),
            pltpu.VMEM((rounds, shard) + tile, f32),
            pltpu.VMEM((rounds, first * shard) + tile, f32),
        ]
    shapes += [
        pltpu.VMEM((BLOCKS, UNITS, 640), f32),
        pltpu.VMEM((BLOCKS, NX - 1, PIECE, 640), f32),
        pltpu.VMEM((NZ, 8, 640), f32),
        pltpu.VMEM((NZ - 1, 8, 640), f32),
        pltpu.VMEM((HALF // GROUP, 8, 640), f32),
        pltpu.VMEM((3, 8, 256), f32),
        pltpu.VMEM((3, ROWS, HEADS * HD), bf16),
        pltpu.SemaphoreType.DMA((N_SEMS,)),
        pltpu.SemaphoreType.DMA((N_SEMS,)),
        pltpu.SemaphoreType.DMA((2, 3)),
        pltpu.SemaphoreType.DMA((11,)),
    ]
    return shapes


def on_device(queries, key_rows, value_rows, step_rates, fast_init, out_grad):
    vmem = pl.BlockSpec(memory_space=pltpu.VMEM)
    anywhere = pl.BlockSpec(memory_space=pl.ANY)
    hbm = pl.BlockSpec(memory_space=pltpu.HBM)
    rates_shape = jax.ShapeDtypeStruct((HEADS, ROWS), f32)
    results = pl.pallas_call(
        kernel,
        out_shape=(
            jax.ShapeDtypeStruct((3, ROWS, HEADS * HD), bf16),
            rates_shape,
            jax.ShapeDtypeStruct((3, 8, 256), f32),
        ),
        in_specs=[hbm] * 6,
        out_specs=(anywhere, vmem, vmem),
        scratch_shapes=scratch(),
        compiler_params=pltpu.CompilerParams(
            collective_id=0, has_side_effects=True, vmem_limit_bytes=56 * 2**20
        ),
        name="layer_grad",
    )(queries, key_rows, value_rows, step_rates.T, out_grad, fast_init)
    rows = jax.ShapeDtypeStruct((ROWS, HEADS * HD), bf16)
    query_grad, key_grad, value_grad, rate_grad, fast_grad = pl.pallas_call(
        finish,
        out_shape=(rows, rows, rows, rates_shape, jax.ShapeDtypeStruct((3 * GROUP, HD), f32)),
        in_specs=[anywhere, vmem, vmem],
        out_specs=(anywhere,) * 3 + (vmem,) * 2,
        scratch_shapes=[pltpu.SemaphoreType.DMA((3,))],
        name="outputs",
    )(*results)
    return query_grad, key_grad, value_grad, rate_grad.T, fast_grad.T


def solution(mesh):
    both = ("view", "patch")
    return jax.shard_map(
        on_device,
        mesh=mesh,
        in_specs=(P(both, None), P(both, None), P(both, None), P(both, None), P(), P(both, None)),
        out_specs=(P(both, None), P(both, None), P(both, None), P(both, None), P(None, both)),
        check_vma=False,
    )
```

```python
import itertools
import math

import jax
import jax.numpy as jnp
from jax import lax
from jax.experimental import pallas as pl
from jax.experimental.pallas import tpu as pltpu
from jax.sharding import PartitionSpec as P

MESH = pl.DeviceIdType.MESH
f32, bf16 = jnp.float32, jnp.bfloat16

step_size = 0.2
epsilon = 1e-06

NX, NY, NZ = 4, 4, 8
HEADS, HD, FF = 4, 192, 384
HALF = FF // 2
ROWS = 128
SLOTS = 8
ALL_ROWS = SLOTS * ROWS
CHUNK = 256
WIDE = 512
TOTAL_ROWS = ROWS * NX * NY * NZ * 2
COEFFICIENT = step_size * math.sqrt(TOTAL_ROWS)
N_SEMS = 64
GROUP = 6


def device(x, y, z, core):
    return (lax.div(x, 2) * 2 + core, (y * 2 + lax.rem(x, 2)) * 8 + z)


BLOCKS = 2
UNITS = HALF // BLOCKS
PAD = 128
ROW_TILES = UNITS // 8
PIECE = UNITS // NX

PARTS = (("x", (0, 1, 2, 3, 4)),)


def part_sizes(part):
    axis, lane_tiles = part
    first, second = (NX, NZ) if axis == "x" else (NZ, NX)
    shard = ROW_TILES * len(lane_tiles) // first
    window = -(-shard // second)
    if (shard - window) // (second - 1) >= window and shard > second:
        window += 1
    return first, second, shard, window


def nt(a, b):
    return lax.dot_general(a, b, (((1,), (1,)), ((), ())), preferred_element_type=f32)


def nn(a, b):
    return lax.dot_general(a, b, (((1,), (0,)), ((), ())), preferred_element_type=f32)


def tn(a, b):
    return lax.dot_general(a, b, (((0,), (0,)), ((), ())), preferred_element_type=f32)


def split(value):
    high = value.astype(bf16)
    return high, (value - high.astype(f32)).astype(bf16)


def kernel(
    q_hbm, k_hbm, v_hbm, r_hbm, g_hbm, w_hbm,
    rows_hbm, rg_out, fg_out,
    q_ref, k_ref, v_ref, g_ref, r_ref,
    w_load, w_own, wh_ab, wl_ab, nh_ab, nl_ab, wh_c, wl_c, nh_c, nl_c, moved, gm, norms,
    kv_send, qg_send, kv, qg, rates, inv_rates, kb, vb, qb, gb,
    gate_s, up_s, pull_s, m1, m2, m3, m4,
    s_ab_h, s_ab_l, e_ab_h, e_ab_l, s_c_h, s_c_l, e_c_h, e_c_l,
    acc_ab, acc_c, rate_rows, dq, xq, oq, rq, dkv, xkv, okv, rkv,
    p0_t, p0_r1, p0_s1, p0_r2, p0_s2, p0_a1, p0_f1, p0_g,
    f_t, f_r1, f_s1, f_r2, d_grp, f_msg,
    rows_ref, send_sems, recv_sems, far_sems, load_sems,
):
    view, patch = lax.axis_index("view"), lax.axis_index("patch")
    x, core = (view // 2) * 2 + (patch // 8) % 2, view % 2
    y, z = patch // 16, patch % 8
    mine = view * 64 + patch
    half_block = 2 * y + core

    known = {}

    def peer(axis, offset):
        if (axis, offset) not in known:
            if axis == "x":
                target = device(lax.rem(x + offset, NX), y, z, core)
            elif axis == "y":
                target = device(x, lax.rem(y + offset, NY), z, core)
            elif axis == "z":
                target = device(x, y, lax.rem(z + offset, NZ), core)
            else:
                target = device(x, y, z, 1 - core)
            known[axis, offset] = target
        return known[axis, offset]

    place = {"x": x, "z": z}

    far_group = [32 * (8 * m + half_block) + 8 * x + z for m in range(3)]
    far_owner = [group // 3 for group in far_group]
    near_source = []
    for t in range(3):
        group = 3 * mine + t
        block, rest = group // 32, group % 32
        near_source.append((rest // 8, (block % 8) // 2, rest % 8, block % 2))
    near_index = []
    for sx, sy, sz, sc in near_source:
        sv, sp = device(sx, sy, sz, sc)
        near_index.append(sv * 64 + sp)

    barrier = pltpu.get_barrier_semaphore()
    peers = [("x", d) for d in range(1, NX)] + [("z", d) for d in range(1, NZ)]
    peers += [("y", d) for d in range(1, NY)] + [("core", 1)]
    for t in range(3):
        @pl.when(near_index[t] != mine)
        def _():
            pl.semaphore_signal(barrier, inc=1, device_id=device(*near_source[t]), device_id_type=MESH)
    peers = sorted(peers, key=lambda one: one[0], reverse=True)
    for axis, offset in peers:
        pl.semaphore_signal(barrier, inc=1, device_id=peer(axis, offset), device_id_type=MESH)

    ids = itertools.count()
    started = []

    def send(src, dst, target):
        which = next(ids)
        copy = pltpu.make_async_remote_copy(
            src_ref=src, dst_ref=dst, send_sem=send_sems.at[which], recv_sem=recv_sems.at[which],
            device_id=target, device_id_type=MESH,
        )
        copy.start()
        started.append(copy)
        return copy

    def send_all(triples, all_of_them):
        which = next(ids)
        for src, dst, target in triples:
            copy = pltpu.make_async_remote_copy(
                src_ref=src, dst_ref=dst, send_sem=send_sems.at[which], recv_sem=recv_sems.at[which],
                device_id=target, device_id_type=MESH,
            )
            copy.start()
        whole = pltpu.make_async_remote_copy(
            src_ref=all_of_them, dst_ref=all_of_them, send_sem=send_sems.at[which], recv_sem=recv_sems.at[which],
            device_id=target, device_id_type=MESH,
        )
        started.append(whole)
        return whole

    def take_started():
        taken = list(started)
        started.clear()
        return taken

    def drain(copies):
        for copy in copies:
            copy.wait_send()

    row_loads = []
    for n, (src, dst) in enumerate(((k_hbm, k_ref), (v_hbm, v_ref), (r_hbm, r_ref), (q_hbm, q_ref), (g_hbm, g_ref))):
        load = pltpu.make_async_copy(src, dst, load_sems.at[3 + n])
        load.start()
        row_loads.append(load)
    loads = []
    for m in range(3):
        first = pl.multiple_of(m * HEADS * FF + y * FF, 128)
        load = pltpu.make_async_copy(w_hbm.at[:, pl.ds(first, FF)], w_load.at[m], load_sems.at[m])
        load.start()
        loads.append(load)

    def pack(buffer, left, right):
        for h in range(HEADS):
            cols = slice(HD * h, HD * (h + 1))
            buffer[h, 0:ROWS, 0:HD] = left[:, cols].astype(f32)
            buffer[h, 0:ROWS, HD:2 * HD] = right[:, cols].astype(f32)

    for load in row_loads[:3]:
        load.wait()
    pack(kv_send, k_ref, v_ref)
    for h in range(HEADS):
        kv_send[h, ROWS:ROWS + 8, :] = jnp.zeros((8, 2 * HD), f32)
        kv_send[h, ROWS:ROWS + 8, 0:ROWS] = jnp.broadcast_to(r_ref[h:h + 1, :], (8, ROWS))

    far_count = sum((owner != mine).astype(jnp.int32) for owner in far_owner)
    pl.semaphore_wait(barrier, len(peers) + far_count)

    def scatter_heads(buffer, landing):
        out = {}
        for d in (1, 3, 2):
            out[d] = send(buffer.at[(y + d) % NY], landing.at[d], peer("y", d))
        out["own"] = send(buffer.at[y], landing.at[4], peer("core", 1))
        return out

    kv_copies = scatter_heads(kv_send, kv)
    for load in row_loads[3:]:
        load.wait()
    pack(qg_send, q_ref, g_ref)

    def store_weights(ab_h, ab_l, c_h, c_l, b, m, value):
        if m < 2:
            rows = (b, slice(PAD * m, PAD * m + UNITS))
            ab_h[rows], ab_l[rows] = split(value)
        else:
            rows = (b, slice(0, UNITS))
            c_h[rows], c_l[rows] = split(value)

    for b in range(BLOCKS):
        none = jnp.zeros((PAD - UNITS, HD), bf16)
        for ref in (wh_ab, wl_ab, nh_ab, nl_ab):
            ref[b, UNITS:PAD] = none
            ref[b, PAD + UNITS:2 * PAD] = none
        for ref in (wh_c, wl_c, nh_c, nl_c):
            ref[b, UNITS:PAD] = none
    for m in range(3):
        loads[m].wait()
        both = w_load[m]
        own = jnp.where(core == 0, both[:, 0:HALF], both[:, HALF:FF]).T
        for b in range(BLOCKS):
            pieces = [own[2 * PIECE * n + PIECE * b:2 * PIECE * n + PIECE * (b + 1), :] for n in range(NX)]
            block = jnp.concatenate(pieces, axis=0)
            w_own[b, m] = block
            norms[b, m, 0] = jnp.sqrt(jnp.sum(block * block, axis=1, keepdims=True) + epsilon)
            store_weights(wh_ab, wl_ab, wh_c, wl_c, b, m, block)

    def row_block(s):
        first = (s % 4) * CHUNK + (s // 4) * ROWS
        return slice(first, first + ROWS)

    def unpack_kv(s):
        kb[row_block(s), :] = kv[s, 0:ROWS, 0:HD].astype(bf16)
        vb[row_block(s), :] = kv[s, 0:ROWS, HD:2 * HD].astype(bf16)
        column = kv[s, ROWS:ROWS + 8, 0:ROWS].T[:, 0:1]
        rates[row_block(s), :] = column
        inv_rates[row_block(s), :] = 1.0 / column

    def unpack_qg(s):
        qb[row_block(s), :] = qg[s, 0:ROWS, 0:HD].astype(bf16)
        gb[row_block(s), :] = qg[s, 0:ROWS, HD:2 * HD].astype(bf16)

    def silu_parts(gate):
        sig = 1.0 / (1.0 + jnp.exp(-gate))
        act = gate * sig
        slope = sig + act * (1.0 - sig)
        return sig, act, slope

    def clear(b):
        acc_ab[b] = jnp.zeros((2 * PAD, HD), f32)
        acc_c[b] = jnp.zeros((PAD, HD), f32)

    for b in range(BLOCKS):
        clear(b)

    GATE, UP = slice(0, PAD), slice(PAD, 2 * PAD)

    def add_terms(b, rows, gate_term, up_term, pull_term, left, right):
        both = jnp.concatenate([gate_term, up_term], axis=1)
        both_h, both_l = split(both)
        pull_h, pull_l = split(pull_term)
        s_ab_h[b, rows, :], s_c_h[b, rows, :] = both_h, pull_h
        s_ab_l[b, rows, :], s_c_l[b, rows, :] = both_l, pull_l
        acc_ab[b] += tn(both_h, left) + tn(both_l, left)
        acc_c[b] += tn(pull_h, right) + tn(pull_l, right)

    def update_chunk(b, i):
        rows = slice(i * CHUNK, (i + 1) * CHUNK)
        keys, values, eta = kb[rows, :], vb[rows, :], rates[rows, :]
        both = nt(keys, wh_ab[b]) + nt(keys, wl_ab[b])
        gate, up = both[:, GATE], both[:, UP]
        pulled = nt(values, wh_c[b]) + nt(values, wl_c[b])
        gate_s[b, rows, :], up_s[b, rows, :], pull_s[b, rows, :] = gate, up, pulled
        _, act, slope = silu_parts(gate)
        scaled = -eta * pulled
        add_terms(b, rows, scaled * up * slope, scaled * act, -eta * act * up, keys, values)

    def take_pair(d):
        unpack_kv(d)
        unpack_kv(4 + d)

    def pass_on(copies, landing, d):
        copies[d].wait_recv()
        return send(landing.at[d], landing.at[4 + d], peer("core", 1))

    with jax.named_scope("keys_own"):
        kv[0] = kv_send[y]
        kv_copies["own"].wait_recv()
        take_pair(0)
        for b in range(BLOCKS):
            update_chunk(b, 0)
    passed = {}
    with jax.named_scope("keys_first"):
        passed[1] = pass_on(kv_copies, kv, 1)
        passed[3] = pass_on(kv_copies, kv, 3)
        passed[1].wait_recv()
        take_pair(1)
        for b in range(BLOCKS):
            update_chunk(b, 1)
    with jax.named_scope("keys_second"):
        passed[2] = pass_on(kv_copies, kv, 2)
        qg_copies = scatter_heads(qg_send, qg)
        passed[3].wait_recv()
        take_pair(3)
        for b in range(BLOCKS):
            update_chunk(b, 3)
    with jax.named_scope("keys_third"):
        passed[2].wait_recv()
        take_pair(2)

    rate_sum = sum(kv[s, ROWS:ROWS + 8, 0:ROWS] for s in range(SLOTS))
    total_part = jnp.sum(rate_sum[0:1, :], axis=1, keepdims=True)

    parts = ((p0_t, p0_r1, p0_s1, p0_r2, p0_s2, p0_a1, p0_f1, p0_g),)

    def lanes_of(first, second, third, tail):
        return (
            first[:, 0:128],
            second[:, 0:128],
            jnp.concatenate([first[:, 128:192], second[:, 128:192]], axis=1),
            third[:, 0:128],
            jnp.concatenate([third[:, 128:192], tail], axis=1),
        )

    def sums_of(b, tail):
        return lanes_of(
            acc_ab[b, 0:UNITS, :], acc_ab[b, PAD:PAD + UNITS, :], acc_c[b, 0:UNITS, :], tail
        )

    def start_stage(r, p, source):
        axis, lane_tiles = PARTS[p]
        first, second, shard, window = part_sizes(PARTS[p])
        t = parts[p][0]
        for jj, j in enumerate(lane_tiles):
            t[r, jj * ROW_TILES:(jj + 1) * ROW_TILES] = source[j].reshape(ROW_TILES, 8, 128)
        r1 = parts[p][1]
        triples = []
        for d in range(1, first):
            there = lax.rem(place[axis] + d, first)
            triples.append((t.at[r, pl.ds(there * shard, shard)], r1.at[r, d - 1], peer(axis, d)))
        return send_all(triples, r1.at[r])

    def start_of(p, k):
        _, second, shard, window = part_sizes(PARTS[p])
        return lax.div((shard - window) * k, second - 1)

    def second_stage(r, p, copies):
        axis = PARTS[p][0]
        other = "z" if axis == "x" else "x"
        first, second, shard, window = part_sizes(PARTS[p])
        t, r1, s1, r2 = parts[p][:4]
        total = t[r, pl.ds(place[axis] * shard, shard)]
        copies.wait_recv()
        for d in range(1, first):
            total = total + r1[r, d - 1]
        s1[r] = total
        triples = []
        for d in range(1, second):
            there = lax.rem(place[other] + d, second)
            triples.append((s1.at[r, pl.ds(start_of(p, there), window)], r2.at[r, d - 1], peer(other, d)))
        return send_all(triples, r2.at[r])

    def third_stage(r, p, copies):
        other = "z" if PARTS[p][0] == "x" else "x"
        _, second, shard, window = part_sizes(PARTS[p])
        _, _, s1, r2, s2, a1, f1, _ = parts[p]
        total = s1[r, pl.ds(start_of(p, place[other]), window)]
        copies.wait_recv()
        for d in range(1, second):
            total = total + r2[r, d - 1]
        s2[r] = total
        return send_all([(s2.at[r], a1.at[r, d - 1], peer(other, d)) for d in range(1, second)], a1.at[r])

    def fourth_stage(r, p, copies):
        axis = PARTS[p][0]
        other = "z" if axis == "x" else "x"
        first, second, shard, window = part_sizes(PARTS[p])
        _, _, _, _, s2, a1, f1, g = parts[p]
        f1[r, pl.ds(start_of(p, place[other]), window)] = s2[r]
        copies.wait_recv()
        for d in range(1, second):
            there = lax.rem(place[other] + second - d, second)
            f1[r, pl.ds(start_of(p, there), window)] = a1[r, d - 1]
        here = pl.ds(place[axis] * shard, shard)
        out = send_all([(f1.at[r], g.at[r, here], peer(axis, d)) for d in range(1, first)], parts[p][1].at[r])
        g[r, here] = f1[r]
        return out

    class Sum:
        def __init__(self, r, b):
            self.r = 2 * r + b
            self.b = b

        def start(self, tail):
            source = sums_of(self.b, tail)
            self.copies = [start_stage(self.r, p, source) for p in range(len(PARTS))]

        def step(self, stage):
            self.copies = [stage(self.r, p, self.copies[p]) for p in range(len(PARTS))]

        def result(self):
            for group in self.copies:
                group.wait_recv()
            tiles = {}
            for p in range(len(PARTS)):
                for jj, j in enumerate(PARTS[p][1]):
                    tiles[j] = parts[p][7][self.r, jj * ROW_TILES:(jj + 1) * ROW_TILES].reshape(UNITS, 128)
            gate = jnp.concatenate([tiles[0], tiles[2][:, 0:64]], axis=1)
            up = jnp.concatenate([tiles[1], tiles[2][:, 64:128]], axis=1)
            down = jnp.concatenate([tiles[3], tiles[4][:, 0:64]], axis=1)
            return (gate, up, down), tiles[4][0:1, 64:65]

    def prepare_chunk(i, _):
        rows = pl.ds(pl.multiple_of(i * CHUNK, CHUNK), CHUNK)
        eta = rates[rows, :]
        for b in range(BLOCKS):
            gate, up, pulled = gate_s[b, rows, :], up_s[b, rows, :], pull_s[b, rows, :]
            sig, act, slope = silu_parts(gate)
            curve = sig * (1.0 - sig) * (2.0 + gate * (1.0 - 2.0 * sig))
            scaled = eta * pulled
            by_slope, by_act = eta * (up * slope), eta * act
            m1[b, rows, :], m2[b, rows, :] = scaled * up * curve, scaled * slope
            m3[b, rows, :], m4[b, rows, :] = by_slope, by_act
            e_ab_h[b, rows, GATE], e_ab_l[b, rows, GATE] = split(by_slope * pulled)
            e_ab_h[b, rows, UP], e_ab_l[b, rows, UP] = split(by_act * pulled)
            e_c_h[b, rows, :], e_c_l[b, rows, :] = split(by_act * up)
        return 0

    query_passed = {}

    def prepare():
        lax.fori_loop(0, ALL_ROWS // CHUNK, prepare_chunk, 0)

    def pass_queries():
        qg[0] = qg_send[y]
        for d in (1, 3, 2):
            query_passed[d] = pass_on(qg_copies, qg, d)

    def take_queries():
        qg_copies["own"].wait_recv()
        for d in (1, 3, 2):
            query_passed[d].wait_recv()
        for s in range(SLOTS):
            unpack_qg(s)

    tail = jnp.broadcast_to(total_part, (UNITS, 64))
    sums = [Sum(0, b) for b in range(BLOCKS)]
    for b in range(BLOCKS):
        with jax.named_scope("keys_last"):
            update_chunk(b, 2)
            sums[b].start(tail)
    prepare()
    for stage, work in ((second_stage, pass_queries), (third_stage, take_queries), (fourth_stage, None)):
        for b in range(BLOCKS):
            sums[b].step(stage)
        if work is not None:
            work()

    def new_weights(b):
        terms, total = sums[b].result()
        scale = COEFFICIENT / total
        for m in range(3):
            change = terms[m] * scale
            shifted = w_own[b, m] - change
            inverse = lax.rsqrt(jnp.sum(shifted * shifted, axis=1, keepdims=True) + epsilon)
            gm[b, m], moved[b, m], norms[b, m, 1] = change, shifted, inverse
            store_weights(nh_ab, nl_ab, nh_c, nl_c, b, m, shifted * (norms[b, m, 0] * inverse))
        clear(b)
        return total, scale

    def apply_block(b):
        def apply_chunk(i, _):
            rows = pl.ds(pl.multiple_of(i * WIDE, WIDE), WIDE)
            queries, grads = qb[rows, :], gb[rows, :]
            both = nt(queries, nh_ab[b]) + nt(queries, nl_ab[b])
            gate, up = both[:, GATE], both[:, UP]
            pulled = nt(grads, nh_c[b]) + nt(grads, nl_c[b])
            _, act, slope = silu_parts(gate)
            add_terms(b, rows, pulled * up * slope, pulled * act, act * up, queries, grads)
            return 0

        lax.fori_loop(0, ALL_ROWS // WIDE, apply_chunk, 0)

    new_sums = [Sum(1, b) for b in range(BLOCKS)]
    early = take_started()
    for b in range(BLOCKS):
        with jax.named_scope("apply"):
            totals, scale = new_weights(b)
            apply_block(b)
            new_sums[b].start(jnp.zeros((UNITS, 64), f32))

    def product(ah, al, bh, bl, rows):
        high = ah[rows, :]
        return nn(high, bh) + nn(high, bl) + nn(al[rows, :], bh)

    def query_grads(b):
        def query_chunk(i, _):
            rows = pl.ds(pl.multiple_of(i * CHUNK, CHUNK), CHUNK)
            part = product(s_ab_h.at[b], s_ab_l.at[b], nh_ab[b], nl_ab[b], rows)
            dq[i] = part[0:ROWS] if b == 0 else dq[i] + part[0:ROWS]
            dq[4 + i] = part[ROWS:CHUNK] if b == 0 else dq[4 + i] + part[ROWS:CHUNK]
            return 0

        lax.fori_loop(0, 4, query_chunk, 0)

    def return_rows(pair, partial, arrived, sums, landing):
        pair.wait_recv()
        out = []
        for d in (1, 3, 2, 0):
            if d == 0:
                landing[0] = partial[0] + arrived[0]
            else:
                sums[d] = partial[d] + arrived[d]
                out.append(send(sums.at[d], landing.at[d], peer("y", NY - d)))
        return out

    for b in range(BLOCKS):
        with jax.named_scope("query_grads"):
            query_grads(b)
        new_sums[b].step(second_stage)
    query_pair = send(dq.at[pl.ds(4, 4)], xq, peer("core", 1))
    new_sums[0].step(third_stage)
    query_back = return_rows(query_pair, dq, xq, oq, rq)
    drain(early)
    new_sums[1].step(third_stage)
    for b in range(BLOCKS):
        new_sums[b].step(fourth_stage)

    direct = {}

    def pull_weights(b):
        d_new, _ = new_sums[b].result()
        head_part = jnp.zeros((1, 1), f32)
        for m in range(3):
            init_norm, inverse = norms[b, m, 0], norms[b, m, 1]
            shifted = moved[b, m]
            dots = jnp.sum(d_new[m] * shifted, axis=1, keepdims=True)
            d_moved = d_new[m] * (init_norm * inverse) - shifted * (dots * init_norm * inverse * inverse * inverse)
            direct[b, m] = d_moved + w_own[b, m] * (dots * inverse / init_norm)
            by_row = jnp.sum(d_moved * gm[b, m], axis=1, keepdims=True)
            head_part = head_part - jnp.sum(by_row, axis=0, keepdims=True)
            store_weights(nh_ab, nl_ab, nh_c, nl_c, b, m, d_moved * scale)
        clear(b)
        return -head_part / totals

    def pull_block(b):
        def pull_chunk(i, _):
            rows = pl.ds(pl.multiple_of(i * WIDE, WIDE), WIDE)
            keys, values = kb[rows, :], vb[rows, :]
            both = nt(keys, nh_ab[b]) + nt(keys, nl_ab[b])
            one, two = both[:, GATE], both[:, UP]
            three = nt(values, nh_c[b]) + nt(values, nl_c[b])
            by_slope, by_act, by_two = m3[b, rows, :], m4[b, rows, :], m2[b, rows, :]
            c_gate = one * m1[b, rows, :] + two * by_two + three * by_slope
            c_up = one * by_two + three * by_act
            c_pull = one * by_slope + two * by_act
            add_terms(b, rows, c_gate, c_up, c_pull, keys, values)
            by_rate = c_pull * pull_s[b, rows, :] + three * (by_act * up_s[b, rows, :])
            by_rate_h, by_rate_l = split(by_rate * inv_rates[rows, :])
            ones = jnp.ones((8, PAD), bf16)
            part = nt(ones, by_rate_h) + nt(ones, by_rate_l)
            rate_rows[i] = part if b == 0 else rate_rows[i] + part
            return 0

        lax.fori_loop(0, ALL_ROWS // WIDE, pull_chunk, 0)

    early = take_started()
    weight_copies = []
    d_totals = jnp.zeros((1, 1), f32)
    for b in range(BLOCKS):
        with jax.named_scope("pull"):
            d_totals = d_totals + pull_weights(b)
            pull_block(b)
            tiles = sums_of(b, jnp.zeros((UNITS, 64), f32))
            for j in range(5):
                f_t[b, :, 128 * j:128 * (j + 1)] = tiles[j]
            triples = []
            for d in range(1, NX):
                first = pl.multiple_of(((x + d) % NX) * PIECE, PIECE)
                triples.append((f_t.at[b, pl.ds(first, PIECE)], f_r1.at[b, d - 1], peer("x", d)))
            weight_copies.append(send_all(triples, f_r1.at[b]))

    def key_chunk(i, _):
        rows = pl.ds(pl.multiple_of(i * CHUNK, CHUNK), CHUNK)
        key_part, value_part = 0.0, 0.0
        for b in range(BLOCKS):
            key_part += product(s_ab_h.at[b], s_ab_l.at[b], wh_ab[b], wl_ab[b], rows)
            key_part += product(e_ab_h.at[b], e_ab_l.at[b], nh_ab[b], nl_ab[b], rows)
            value_part += product(s_c_h.at[b], s_c_l.at[b], wh_c[b], wl_c[b], rows)
            value_part += product(e_c_h.at[b], e_c_l.at[b], nh_c[b], nl_c[b], rows)
        for slot, first in ((i, 0), (4 + i, ROWS)):
            dkv[slot, 0:ROWS, 0:HD] = key_part[first:first + ROWS]
            dkv[slot, 0:ROWS, HD:2 * HD] = value_part[first:first + ROWS]
        return 0

    with jax.named_scope("row_grads"):
        lax.fori_loop(0, 4, key_chunk, 0)
        for s in range(SLOTS):
            dkv[s, ROWS:ROWS + 8, :] = jnp.zeros((8, 2 * HD), f32)
            first = row_block(s).start
            lane = first % WIDE
            dkv[s, ROWS:ROWS + 8, 0:ROWS] = rate_rows[first // WIDE, :, lane:lane + ROWS] + d_totals
        pair = send(dkv.at[pl.ds(4, 4)], xkv, peer("core", 1))

    with jax.named_scope("x_sums"):
        for b in range(BLOCKS):
            total = f_t[b, pl.ds(pl.multiple_of(x * PIECE, PIECE), PIECE), :]
            weight_copies[b].wait_recv()
            for d in range(1, NX):
                total = total + f_r1[b, d - 1]
            for n in range(4):
                f_s1[4 * b + n, 0:GROUP, :] = total[GROUP * n:GROUP * (n + 1), :]
                f_s1[4 * b + n, GROUP:8, :] = jnp.zeros((8 - GROUP, 640), f32)
        triples = [(f_s1.at[(z + d) % NZ], f_r2.at[d - 1], peer("z", d)) for d in range(1, NZ)]
        weight_copies = send_all(triples, f_r2)
    with jax.named_scope("row_returns"):
        row_back = return_rows(pair, dkv, xkv, okv, rkv)
    with jax.named_scope("direct"):
        for b in range(BLOCKS):
            tiles = lanes_of(direct[b, 0], direct[b, 1], direct[b, 2], jnp.zeros((UNITS, 64), f32))
            for j in range(5):
                for n in range(16):
                    group = 8 * (n // 4) + 4 * b + n % 4
                    d_grp[group, 0:GROUP, 128 * j:128 * (j + 1)] = tiles[j][GROUP * n:GROUP * (n + 1), :]

    drain(early)
    z_scope = jax.named_scope("z_sums")
    z_scope.__enter__()
    total = f_s1[z]
    weight_copies.wait_recv()
    for d in range(1, NZ):
        total = total + f_r2[d - 1]
    total = (total + d_grp[8 * x + z]) * (1.0 / math.sqrt(TOTAL_ROWS))
    for m, (low, high) in enumerate(((0, 256), (128, 320), (384, 512))):
        f_msg[m, :, 0:128] = total[:, low:low + 128]
        f_msg[m, :, 128:HD] = total[:, high:high + 64]
    far_copies = []
    for m in range(3):
        slot = far_group[m] % 3
        owner = far_owner[m]
        copy = pltpu.make_async_remote_copy(
            src_ref=f_msg.at[m], dst_ref=fg_out.at[slot], send_sem=far_sems.at[0, m], recv_sem=far_sems.at[1, slot],
            device_id=(owner // 64, owner % 64), device_id_type=MESH,
        )

        @pl.when(owner != mine)
        def _():
            copy.start()

        @pl.when(owner == mine)
        def _():
            fg_out[slot] = f_msg[m]

        far_copies.append(copy)

    z_scope.__exit__(None, None, None)

    def rows_out(which, landing, lanes):
        for h in range(HEADS):
            d = (h + NY - y) % NY
            rows_ref[which, :, HD * h:HD * (h + 1)] = landing[d, 0:ROWS, lanes:lanes + HD].astype(bf16)
        store = pltpu.make_async_copy(rows_ref.at[which], rows_hbm.at[which], load_sems.at[8 + which])
        store.start()
        stores.append(store)

    stores = []

    with jax.named_scope("query_rows"):
        for copy in query_back:
            copy.wait_recv()
        rows_out(0, rq, 0)
    with jax.named_scope("key_rows"):
        for copy in row_back:
            copy.wait_recv()
        rows_out(1, rkv, 0)
        rows_out(2, rkv, HD)
        for h in range(HEADS):
            rg_out[h:h + 1, :] = rkv[(h + NY - y) % NY, ROWS:ROWS + 1, 0:ROWS]

    with jax.named_scope("columns"):
        for m in range(3):
            @pl.when(near_index[m] != mine)
            def _():
                pltpu.make_async_remote_copy(
                    src_ref=f_msg.at[m], dst_ref=fg_out.at[m], send_sem=far_sems.at[0, m],
                    recv_sem=far_sems.at[1, m], device_id=(view, patch), device_id_type=MESH,
                ).wait_recv()

            @pl.when(far_owner[m] != mine)
            def _():
                far_copies[m].wait_send()
        drain(started)
        for store in stores:
            store.wait()


def finish(rows, rate_rows, groups, query_out, key_out, value_out, rate_out, fast_out, sems):
    copies = [
        pltpu.make_async_copy(rows.at[n], out, sems.at[n]) for n, out in enumerate((query_out, key_out, value_out))
    ]
    for copy in copies:
        copy.start()
    rate_out[...] = rate_rows[...]
    for m in range(3):
        fast_out[GROUP * m:GROUP * (m + 1), :] = groups[m, 0:GROUP, 0:HD]
    for copy in copies:
        copy.wait()


def scratch():
    tile = (8, 128)
    halves = (BLOCKS, ALL_ROWS)
    shapes = [
        *[pltpu.VMEM((ROWS, HEADS * HD), bf16)] * 4,
        pltpu.VMEM((HEADS, ROWS), f32),
        pltpu.VMEM((3, HD, FF), f32),
        pltpu.VMEM((BLOCKS, 3, UNITS, HD), f32),
        *[pltpu.VMEM((BLOCKS, 2 * PAD, HD), bf16)] * 4,
        *[pltpu.VMEM((BLOCKS, PAD, HD), bf16)] * 4,
        *[pltpu.VMEM((BLOCKS, 3, UNITS, HD), f32)] * 2,
        pltpu.VMEM((BLOCKS, 3, 2, UNITS, 1), f32),
        *[pltpu.VMEM((HEADS, ROWS + 8, 2 * HD), f32)] * 2,
        *[pltpu.VMEM((SLOTS, ROWS + 8, 2 * HD), f32)] * 2,
        *[pltpu.VMEM((ALL_ROWS, 1), f32)] * 2,
        *[pltpu.VMEM((ALL_ROWS, HD), bf16)] * 4,
        *[pltpu.VMEM(halves + (PAD,), f32)] * 7,
        *[pltpu.VMEM(halves + (2 * PAD,), bf16)] * 4,
        *[pltpu.VMEM(halves + (PAD,), bf16)] * 4,
        pltpu.VMEM((BLOCKS, 2 * PAD, HD), f32),
        pltpu.VMEM((BLOCKS, PAD, HD), f32),
        pltpu.VMEM((ALL_ROWS // WIDE, 8, WIDE), f32),
        pltpu.VMEM((SLOTS, ROWS, HD), f32),
        *[pltpu.VMEM((4, ROWS, HD), f32)] * 3,
        pltpu.VMEM((SLOTS, ROWS + 8, 2 * HD), f32),
        *[pltpu.VMEM((4, ROWS + 8, 2 * HD), f32)] * 3,
    ]
    rounds = 2 * BLOCKS
    for part in PARTS:
        first, second, shard, window = part_sizes(part)
        shapes += [
            pltpu.VMEM((rounds, first * shard) + tile, f32),
            pltpu.VMEM((rounds, first - 1, shard) + tile, f32),
            pltpu.VMEM((rounds, shard) + tile, f32),
            pltpu.VMEM((rounds, second - 1, window) + tile, f32),
            pltpu.VMEM((rounds, window) + tile, f32),
            pltpu.VMEM((rounds, second - 1, window) + tile, f32),
            pltpu.VMEM((rounds, shard) + tile, f32),
            pltpu.VMEM((rounds, first * shard) + tile, f32),
        ]
    shapes += [
        pltpu.VMEM((BLOCKS, UNITS, 640), f32),
        pltpu.VMEM((BLOCKS, NX - 1, PIECE, 640), f32),
        pltpu.VMEM((NZ, 8, 640), f32),
        pltpu.VMEM((NZ - 1, 8, 640), f32),
        pltpu.VMEM((HALF // GROUP, 8, 640), f32),
        pltpu.VMEM((3, 8, 256), f32),
        pltpu.VMEM((3, ROWS, HEADS * HD), bf16),
        pltpu.SemaphoreType.DMA((N_SEMS,)),
        pltpu.SemaphoreType.DMA((N_SEMS,)),
        pltpu.SemaphoreType.DMA((2, 3)),
        pltpu.SemaphoreType.DMA((11,)),
    ]
    return shapes


def on_device(queries, key_rows, value_rows, step_rates, fast_init, out_grad):
    vmem = pl.BlockSpec(memory_space=pltpu.VMEM)
    anywhere = pl.BlockSpec(memory_space=pl.ANY)
    hbm = pl.BlockSpec(memory_space=pltpu.HBM)
    rates_shape = jax.ShapeDtypeStruct((HEADS, ROWS), f32)
    results = pl.pallas_call(
        kernel,
        out_shape=(
            jax.ShapeDtypeStruct((3, ROWS, HEADS * HD), bf16),
            rates_shape,
            jax.ShapeDtypeStruct((3, 8, 256), f32),
        ),
        in_specs=[hbm] * 6,
        out_specs=(anywhere, vmem, vmem),
        scratch_shapes=scratch(),
        compiler_params=pltpu.CompilerParams(
            collective_id=0, has_side_effects=True, vmem_limit_bytes=56 * 2**20
        ),
        name="layer_grad",
    )(queries, key_rows, value_rows, step_rates.T, out_grad, fast_init)
    rows = jax.ShapeDtypeStruct((ROWS, HEADS * HD), bf16)
    query_grad, key_grad, value_grad, rate_grad, fast_grad = pl.pallas_call(
        finish,
        out_shape=(rows, rows, rows, rates_shape, jax.ShapeDtypeStruct((3 * GROUP, HD), f32)),
        in_specs=[vmem] * 3,
        out_specs=(anywhere,) * 3 + (vmem,) * 2,
        scratch_shapes=[pltpu.SemaphoreType.DMA((3,))],
        name="outputs",
    )(*results)
    return query_grad, key_grad, value_grad, rate_grad.T, fast_grad.T


def solution(mesh):
    both = ("view", "patch")
    return jax.shard_map(
        on_device,
        mesh=mesh,
        in_specs=(P(both, None), P(both, None), P(both, None), P(both, None), P(), P(both, None)),
        out_specs=(P(both, None), P(both, None), P(both, None), P(both, None), P(None, both)),
        check_vma=False,
    )
```
